32 devices in a mesh: dp: 4 (over y, core), tensor: 8 (over z, x).
Axes of the slice: x: 2, y: 2, z: 4, core: 2. Of those that a mesh axis runs over, the one named last changes fastest.
Arguments:
- embedded: bfloat16 [2, 8192, 1024], P(None, ('dp', 'tensor')), may hold values from -6 to 6
- token_table: bfloat16 [30, 1024], replicated, may hold values from -6 to 6
- masked_pos: int32 [2, 8, 204], P(None, 'dp'), may hold values from 0 to 1024, as said below
- replace_ids: int32 [2, 8, 204], P(None, 'dp'), may hold values from 0 to 29
- w_query: bfloat16 [1024, 1024], P(None, 'tensor'), may hold values from -0.1875 to 0.1875
- b_query: bfloat16 [1024], P('tensor'), may hold values from -3 to 3
- w_key: bfloat16 [1024, 1024], P(None, 'tensor'), may hold values from -0.25 to 0.25
- w_value: bfloat16 [1024, 1024], P(None, 'tensor'), may hold values from -0.1875 to 0.1875
- b_value: bfloat16 [1024], P('tensor'), may hold values from -3 to 3
- w_out: bfloat16 [1024, 1024], P('tensor'), may hold values from -2 to 2
- b_out: bfloat16 [1024], replicated, may hold values from -3 to 3
- ln1_gain: bfloat16 [1024], replicated, may hold values from 0.5 to 1.5
- ln1_bias: bfloat16 [1024], replicated, may hold values from -2 to 2
- w_up: bfloat16 [1024, 4096], P(None, 'tensor'), may hold values from -0.1875 to 0.1875
- b_up: bfloat16 [4096], P('tensor'), may hold values from -3 to 3
- w_down: bfloat16 [4096, 1024], P('tensor'), may hold values from -0.09375 to 0.09375
- b_down: bfloat16 [1024], replicated, may hold values from -3 to 3
- ln2_gain: bfloat16 [1024], replicated, may hold values from 0.5 to 1.5
- ln2_bias: bfloat16 [1024], replicated, may hold values from -2 to 2
- grad_masked: bfloat16 [2, 8, 204, 1024], P(None, 'dp'), may hold values from -6 to 6
Outputs:
- layer_out: bfloat16 [2, 8192, 1024], P(None, ('dp', 'tensor'))
- grad_embedded: float32 [2, 8192, 1024], P(None, ('dp', 'tensor'))
- grad_token_table: float32 [30, 1024], replicated
- grad_w_query: float32 [1024, 1024], P(None, 'tensor')
- grad_b_query: float32 [1024], P('tensor')
- grad_w_key: float32 [1024, 1024], P(None, 'tensor')
- grad_w_value: float32 [1024, 1024], P(None, 'tensor')
- grad_b_value: float32 [1024], P('tensor')
- grad_w_out: float32 [1024, 1024], P('tensor')
- grad_b_out: float32 [1024], replicated
- grad_ln1_gain: float32 [1024], replicated
- grad_ln1_bias: float32 [1024], replicated
- grad_w_up: float32 [1024, 4096], P(None, 'tensor')
- grad_b_up: float32 [4096], P('tensor')
- grad_w_down: float32 [4096, 1024], P('tensor')
- grad_b_down: float32 [1024], replicated
- grad_ln2_gain: float32 [1024], replicated
- grad_ln2_bias: float32 [1024], replicated
The draws below stay inside these ranges and needn't reach their ends.
Inputs may be any that keep to these rules, and one draw needn't show every extreme that they name: `masked_pos`: in each row of a micro-batch, the used slots come first and hold distinct positions below 1024; the other slots hold 1024. Between half of 204 and 204 slots of a row are used, and some row uses all 204.
All inputs are finite; a program needn't handle non-finite values.
Results may differ from the reference program's by a relative error of at most 0.018.
The reference program's roundings to bfloat16 on the way count: a program that leaves them out, or rounds other values in their place, can miss the bound.
Values may be sent and summed in bfloat16 or wider, within the bound.
No kernel may reach another device: no remote copies, remote signals or barrier semaphores. Data moves between devices by JAX's collectives and lax.ppermute only.
A program may use at most 320 MiB of HBM per device.

```python
import jax
import jax.numpy as jnp
from jax import lax

D = 1024
HEADS = 16
HD = 64
FF = 4096
VOCAB = 30
LEN = 1024
MICRO = 2
MMAX = 204
SEQ_MB = 2
SEQS = 8
TOK_MB = 8192
N_DP = 4


def draw_masked_pos(key, part):
    key = jax.random.fold_in(key, 11)
    perm_key, count_key, full_key = jax.random.split(key, 3)
    row_total = MICRO * SEQS
    chosen = jax.vmap(lambda k: jax.random.permutation(k, LEN)[:MMAX])(jax.random.split(perm_key, row_total))
    slot_used = jax.random.randint(count_key, (row_total,), (MMAX + 1) // 2, MMAX + 1)
    full_row = jax.random.randint(full_key, (), 0, row_total)
    slot_used = jnp.where(jnp.arange(row_total) == full_row, MMAX, slot_used)
    slot_index = jnp.arange(MMAX)[None, :]
    filled = jnp.where(slot_index < slot_used[:, None], chosen, LEN)
    return filled.reshape(MICRO, SEQS, MMAX).astype(jnp.int32)


def with_ends(drawn, rng, low, high):
    dims = drawn.shape
    place = [jax.random.randint(jax.random.fold_in(rng, axis), (), 0, dims[axis]) for axis in range(len(dims))]
    drawn = drawn.at[tuple(place)].set(low)
    longest = dims.index(max(dims))
    place[longest] = (place[longest] + 1) % dims[longest]
    return drawn.at[tuple(place)].set(high)


def shard_levels(rng, extent, cuts, least, largest):
    loudness, own = 1.0, jax.random.fold_in(rng, 6)
    for axis_at, parts in cuts:
        draws = jnp.exp(jax.random.uniform(jax.random.fold_in(own, axis_at), (parts,), jnp.float32, least / len(cuts), largest / len(cuts)))
        loudness = loudness * jnp.repeat(draws, extent[axis_at] // parts).reshape([-1 if axis == axis_at else 1 for axis in range(len(extent))])
    return loudness


def scatter_about(key, dims, spread, reach, cuts=(), held_as=jnp.bfloat16):
    drawn = spread * jax.random.normal(key, dims, jnp.float32)
    if cuts:
        drawn = drawn * shard_levels(key, dims, cuts, -0.22, 0.18)
    return jnp.clip(drawn, -reach, reach).astype(held_as)


def setup_inputs(seed: int = 0) -> dict:
    key_of = jax.random.split(jax.random.key(seed), 21)
    return {
        "embedded": scatter_about(key_of[0], (MICRO, TOK_MB, D), 1.0, 6.0, ((1, 32),)),
        "token_table": scatter_about(key_of[1], (VOCAB, D), 1.0, 6.0),
        "masked_pos": draw_masked_pos(jax.random.fold_in(key_of[20], 71), 0),
        "replace_ids": with_ends(jax.random.randint(key_of[3], (MICRO, SEQS, MMAX), 0, VOCAB), jax.random.fold_in(key_of[3], 1), 0, VOCAB - 1).astype(jnp.int32),
        "w_query": scatter_about(key_of[4], (D, D), D ** -0.5, 0.1875, ((1, 8),)),
        "b_query": scatter_about(key_of[5], (D,), 0.5, 3.0, ((0, 8),)),
        "w_key": scatter_about(key_of[6], (D, D), (D // 2) ** -0.5, 0.25, ((1, 8),)),
        "w_value": scatter_about(key_of[7], (D, D), D ** -0.5, 0.1875, ((1, 8),)),
        "b_value": scatter_about(key_of[8], (D,), 0.5, 3.0, ((0, 8),)),
        "w_out": scatter_about(key_of[9], (D, D), (max(1, D // 128)) ** -0.5, 2.0, ((0, 8),)),
        "b_out": scatter_about(key_of[10], (D,), 0.5, 3.0),
        "ln1_gain": jnp.clip(1.0 + 0.1 * jax.random.normal(key_of[11], (D,), jnp.float32), 0.5, 1.5).astype(jnp.bfloat16),
        "ln1_bias": scatter_about(key_of[12], (D,), 0.3, 2.0),
        "w_up": scatter_about(key_of[13], (D, FF), D ** -0.5, 0.1875, ((1, 8),)),
        "b_up": scatter_about(key_of[14], (FF,), 0.5, 3.0, ((0, 8),)),
        "w_down": scatter_about(key_of[15], (FF, D), FF ** -0.5, 0.09375, ((0, 8),)),
        "b_down": scatter_about(key_of[16], (D,), 0.5, 3.0),
        "ln2_gain": jnp.clip(1.0 + 0.1 * jax.random.normal(key_of[17], (D,), jnp.float32), 0.5, 1.5).astype(jnp.bfloat16),
        "ln2_bias": scatter_about(key_of[18], (D,), 0.3, 2.0),
        "grad_masked": scatter_about(key_of[19], (MICRO, SEQS, MMAX, D), 1.0, 6.0, ((1, 4),)),
    }


PRECISE = lax.Precision.HIGHEST
EPSILON = 1e-12

@jax.custom_vjp
def low(v):
    return lax.optimization_barrier(v.astype(jnp.bfloat16)).astype(jnp.float32)

@jax.custom_vjp
def low_back(v):
    return v

def low_keep(v):
    return (low(v), None)

def low_pass(kept, grad):
    return (grad,)

def back_keep(v):
    return (v, None)

def back_low(kept, grad):
    return (low(grad),)
low.defvjp(low_keep, low_pass)
low_back.defvjp(back_keep, back_low)

def matmul(left_mat, right_mat):
    return jnp.dot(left_mat, right_mat, precision=PRECISE)

def layer_norm(values, gain_vec, bias_vec):
    row_mean = lax.optimization_barrier(jnp.mean(values, axis=-1, keepdims=True))
    centred = values - row_mean
    row_var = lax.optimization_barrier(jnp.mean(centred * centred, axis=-1, keepdims=True))
    return centred * lax.rsqrt(row_var + EPSILON) * gain_vec + bias_vec

def group_forward(words_group, positions, token_ids, table_rows, params):
    w_query, b_query, w_key, w_value, b_value, w_out, b_out, ln1_gain, ln1_bias, w_up, b_up, w_down, b_down, ln2_gain, ln2_bias = params
    inserted = table_rows[token_ids]
    placed = jax.vmap(lambda s, p, e: s.at[p].set(e, mode='drop'))(words_group, positions, inserted)
    seq_here = placed.shape[0]
    flat_rows = placed.reshape(seq_here * LEN, D)
    sent_rows = low(flat_rows)
    query_heads = low(low_back(matmul(sent_rows, w_query) + b_query)).reshape(seq_here, LEN, HEADS, HD)
    key_heads = low(low_back(matmul(sent_rows, w_key))).reshape(seq_here, LEN, HEADS, HD)
    value_heads = low(low_back(matmul(sent_rows, w_value) + b_value)).reshape(seq_here, LEN, HEADS, HD)
    scores = low_back(jnp.einsum('sqhd,skhd->shqk', query_heads, key_heads, precision=PRECISE) * HD ** (-0.5))
    row_top = lax.optimization_barrier(jnp.max(scores, axis=-1, keepdims=True))
    exp_scores = jnp.exp(scores - row_top)
    attn_probs = exp_scores / lax.optimization_barrier(jnp.sum(exp_scores, axis=-1, keepdims=True))
    mixed_heads = jnp.einsum('shqk,skhd->sqhd', low(attn_probs), value_heads, precision=PRECISE)
    heads_out = low(low_back(mixed_heads)).reshape(seq_here * LEN, D)
    attended = low_back(matmul(heads_out, w_out)) + b_out
    first_norm = layer_norm(flat_rows + attended, ln1_gain, ln1_bias)
    upper_proj = low_back(matmul(low(first_norm), w_up) + b_up)
    hidden = low(jax.nn.gelu(upper_proj, approximate=False))
    ffn_out = low_back(matmul(hidden, w_down)) + b_down
    return layer_norm(first_norm + ffn_out, ln2_gain, ln2_bias).reshape(seq_here, LEN, D)

def reference(embedded, token_table, masked_pos, replace_ids, w_query, b_query, w_key, w_value, b_value, w_out, b_out, ln1_gain, ln1_bias, w_up, b_up, w_down, b_down, ln2_gain, ln2_bias, grad_masked):
    group_count = MICRO * N_DP
    word_groups = embedded.astype(jnp.float32).reshape(group_count, SEQ_MB, LEN, D)
    pos_groups = masked_pos.reshape(group_count, SEQ_MB, MMAX)
    id_groups = replace_ids.reshape(group_count, SEQ_MB, MMAX)
    table_f = token_table.astype(jnp.float32)
    params = tuple((p.astype(jnp.float32) for p in (w_query, b_query, w_key, w_value, b_value, w_out, b_out, ln1_gain, ln1_bias, w_up, b_up, w_down, b_down, ln2_gain, ln2_bias)))

    def forward(word_f, table_rows, weights_all):

        def one_group(group):
            return jax.checkpoint(group_forward)(group[0], group[1], group[2], table_rows, weights_all)
        return lax.map(one_group, (word_f, pos_groups, id_groups))
    outputs, pullback = jax.vjp(forward, word_groups, table_f, params)
    flat_pos = masked_pos.reshape(MICRO * SEQS, MMAX)
    flat_grad = grad_masked.astype(jnp.float32).reshape(MICRO * SEQS, MMAX, D)
    dense = jax.vmap(lambda p, g: jnp.zeros((LEN, D), jnp.float32).at[p].add(g, mode='drop'))(flat_pos, flat_grad)
    dense = dense.reshape(group_count, SEQ_MB, LEN, D)
    grad_words, grad_table, grad_params = pullback(dense)
    layer_out = outputs.reshape(MICRO, TOK_MB, D).astype(jnp.bfloat16)
    grad_embedded = grad_words.reshape(MICRO, TOK_MB, D)
    return (layer_out, grad_embedded, grad_table, grad_params[0], grad_params[1], grad_params[2], grad_params[3], grad_params[4], grad_params[5], grad_params[6], grad_params[7], grad_params[8], grad_params[9], grad_params[10], grad_params[11], grad_params[12], grad_params[13], grad_params[14])
```

```python
import jax
import jax.numpy as jnp
from jax import lax
from jax.experimental import pallas as pl
from jax.experimental.pallas import tpu as pltpu
from jax.sharding import PartitionSpec as P

HD = 64
LEN = 1024
EPSILON = 1e-12
SCALE = HD ** (-0.5)
ROWS_DIMS = (((0,), (0,)), ((), ()))
LAST_DIMS = (((1,), (1,)), ((), ()))
BF = jnp.bfloat16
F32 = jnp.float32
PAD = 16
Q_ROWS = 256
VMEM_BYTES = 48 * 1024 * 1024


def product(left_mat, right_mat):
    return jnp.dot(left_mat, right_mat, preferred_element_type=F32)


def over_rows(left_mat, right_mat):
    return lax.dot_general(left_mat, right_mat, ROWS_DIMS, preferred_element_type=F32)


def against(left_mat, right_mat):
    return lax.dot_general(left_mat, right_mat, LAST_DIMS, preferred_element_type=F32)


def swap(values, axis, bit):
    count = lax.axis_size(axis)
    return lax.ppermute(values, axis, [(i, i ^ bit) for i in range(count)])


def attn_forward_kernel(q_ref, k_ref, v_ref, o_ref):
    for head in range(2):
        lanes = pl.ds(head * HD, HD)
        scores = against(q_ref[:, lanes], k_ref[:, lanes])
        top = jnp.max(scores, axis=-1, keepdims=True)
        weights = jnp.exp((scores - top) * SCALE)
        total = jnp.sum(weights, axis=-1, keepdims=True)
        mixed = product(weights.astype(BF), v_ref[:, lanes])
        o_ref[:, lanes] = (mixed / total).astype(BF)


def attn_forward(joint, width):
    rows = joint.shape[0]
    pairs = width // 128
    return pl.pallas_call(
        attn_forward_kernel,
        out_shape=jax.ShapeDtypeStruct((rows, width), BF),
        grid=(pairs, rows // Q_ROWS),
        in_specs=[
            pl.BlockSpec((Q_ROWS, 128), lambda g, i: (i, g)),
            pl.BlockSpec((rows, 128), lambda g, i: (0, pairs + g)),
            pl.BlockSpec((rows, 128), lambda g, i: (0, 2 * pairs + g)),
        ],
        out_specs=pl.BlockSpec((Q_ROWS, 128), lambda g, i: (i, g)),
        compiler_params=pltpu.CompilerParams(vmem_limit_bytes=VMEM_BYTES),
        cost_estimate=pl.CostEstimate(
            flops=16 * rows * rows * width,
            bytes_accessed=8 * rows * width,
            transcendentals=rows * rows * width // HD,
        ),
        name="attn_forward",
    )(joint, joint, joint)


def attn_backward_kernel(
    q_ref, k_ref, v_ref, g_ref, dq_ref, dk_ref, dv_ref, kt_ref, dk_acc, dv_acc
):
    step = pl.program_id(1)

    @pl.when(step == 0)
    def _():
        kt_ref[...] = k_ref[...].T
        dk_acc[...] = jnp.zeros_like(dk_acc)
        dv_acc[...] = jnp.zeros_like(dv_acc)

    dq_parts = []
    for head in range(2):
        lanes = pl.ds(head * HD, HD)
        queries = q_ref[:, lanes]
        grads = g_ref[:, lanes]
        scores = against(k_ref[:, lanes], queries)
        top = jnp.max(scores, axis=0, keepdims=True)
        weights = jnp.exp((scores - top) * SCALE)
        probs = weights * (1.0 / jnp.sum(weights, axis=0, keepdims=True))
        d_probs = against(v_ref[:, lanes], grads)
        row_dot = jnp.sum(probs * d_probs, axis=0, keepdims=True)
        d_scores = (probs * (d_probs - row_dot)).astype(BF)
        dv_acc[:, lanes] += product(probs.astype(BF), grads)
        dk_acc[:, lanes] += product(d_scores, queries)
        dq_parts.append(product(kt_ref[lanes, :], d_scores))
    dq_ref[...] = (jnp.concatenate(dq_parts, axis=0).T * SCALE).astype(BF)

    @pl.when(step == pl.num_programs(1) - 1)
    def _():
        dk_ref[...] = (dk_acc[...] * SCALE).astype(BF)
        dv_ref[...] = dv_acc[...].astype(BF)


def attn_backward(joint, d_heads, width):
    rows = joint.shape[0]
    pairs = width // 128
    shape = jax.ShapeDtypeStruct((rows, width), BF)
    block = pl.BlockSpec((Q_ROWS, 128), lambda g, i: (i, g))
    whole = pl.BlockSpec((rows, 128), lambda g, i: (0, g))
    return pl.pallas_call(
        attn_backward_kernel,
        out_shape=(shape, shape, shape),
        grid=(pairs, rows // Q_ROWS),
        in_specs=[
            block,
            pl.BlockSpec((rows, 128), lambda g, i: (0, pairs + g)),
            pl.BlockSpec((rows, 128), lambda g, i: (0, 2 * pairs + g)),
            block,
        ],
        out_specs=(block, whole, whole),
        scratch_shapes=[
            pltpu.VMEM((128, rows), BF),
            pltpu.VMEM((rows, 128), F32),
            pltpu.VMEM((rows, 128), F32),
        ],
        compiler_params=pltpu.CompilerParams(vmem_limit_bytes=VMEM_BYTES),
        cost_estimate=pl.CostEstimate(
            flops=40 * rows * rows * width,
            bytes_accessed=14 * rows * width,
            transcendentals=rows * rows * width // HD,
        ),
        name="attn_backward",
    )(joint, joint, joint, d_heads)


def norm_forward(values):
    row_mean = jnp.mean(values, axis=-1, keepdims=True)
    centred = values - row_mean
    row_var = jnp.mean(centred * centred, axis=-1, keepdims=True)
    scale = lax.rsqrt(row_var + EPSILON)
    return centred * scale, scale


def norm_backward(normed, scale, gain_vec, grads):
    d_normed = grads * gain_vec
    mean_d = jnp.mean(d_normed, axis=-1, keepdims=True)
    mean_dn = jnp.mean(d_normed * normed, axis=-1, keepdims=True)
    return (d_normed - mean_d - normed * mean_dn) * scale


def shards(
    embedded,
    token_table,
    masked_pos,
    replace_ids,
    w_query,
    b_query,
    w_key,
    w_value,
    b_value,
    w_out,
    b_out,
    ln1_gain,
    ln1_bias,
    w_up,
    b_up,
    w_down,
    b_down,
    ln2_gain,
    ln2_bias,
    grad_masked,
):
    rank = lax.axis_index("tensor")
    count = lax.axis_size("tensor")
    dp_count = lax.axis_size("dp")
    core = lax.axis_index("dp") % 2
    micro_count, row_count, width = embedded.shape
    local_width = w_query.shape[1]
    ff_local = w_up.shape[1]
    vocab_count = token_table.shape[0]
    parts = LEN // row_count
    groups = count // parts
    part = rank % parts
    group = rank // parts
    part_width = width // parts
    own_first = core == 0

    def by_core(mine, other, axis=0):
        return jnp.where(
            own_first,
            jnp.concatenate([mine, other], axis=axis),
            jnp.concatenate([other, mine], axis=axis),
        )

    order = list(range(0, count, 2)) + list(range(count - 1, 0, -2))
    ring_fw = [(order[i], order[(i + 1) % count]) for i in range(count)]
    ring_bw = [(b, a) for a, b in ring_fw]
    far = count // 2
    ring_pos = jnp.where(rank % 2 == 0, rank // 2, count - 1 - rank // 2)

    def forward(values):
        return lax.ppermute(values, "tensor", ring_fw)

    def backward(values):
        return lax.ppermute(values, "tensor", ring_bw)

    slot_pos = lax.dynamic_index_in_dim(masked_pos, group, 1, keepdims=False)
    slot_ids = lax.dynamic_index_in_dim(replace_ids, group, 1, keepdims=False)
    slot_grads = lax.dynamic_index_in_dim(grad_masked, group, 1, keepdims=False)
    vocab_iota = jnp.arange(vocab_count, dtype=jnp.int32)

    def replacement(positions, step):
        matches = positions[:, None] == slot_pos[step][None, :]
        replaced = jnp.any(matches, axis=1)
        row_ids = jnp.sum(jnp.where(matches, slot_ids[step][None, :], 0), axis=1)
        hot = (row_ids[:, None] == vocab_iota[None, :]) & replaced[:, None]
        return matches, replaced, hot

    row_iota = jnp.arange(row_count, dtype=jnp.int32)
    placed_list, replaced_list, hot_list, cot_list, seq_hot_list = [], [], [], [], []
    for step in range(micro_count):
        matches, replaced, hot = replacement(part * row_count + row_iota, step)
        inserted = product(hot.astype(BF), token_table)
        placed_list.append(
            jnp.where(replaced[:, None], inserted, embedded[step].astype(F32)).astype(BF)
        )
        replaced_list.append(replaced)
        hot_list.append(hot.astype(F32))
        cot_list.append(product(matches.astype(BF), slot_grads[step]))
        seq_pos = jnp.concatenate([(part ^ j) * row_count + row_iota for j in range(parts)])
        seq_hot_list.append(replacement(seq_pos, step)[2].astype(BF))

    half_rows = width // 2
    joint_half = jnp.concatenate(
        [
            lax.dynamic_slice_in_dim(jnp.concatenate([w_query, w_key, w_value], axis=1), core * half_rows, half_rows, 0),
            jnp.pad(
                jnp.concatenate([b_query, jnp.zeros_like(b_query), b_value])[None, :],
                ((0, PAD - 1), (0, 0)),
            ),
        ],
        axis=0,
    )
    spread = [
        [(groups * p + i, p + parts * ((i + k) % groups)) for p in range(parts) for i in range(groups)]
        for k in range(groups)
    ]
    full_w, full_b = [], []
    for k in range(groups):
        mine = lax.ppermute(joint_half, "tensor", spread[k])
        other = swap(mine[:half_rows], "dp", 1)
        full_w.append(by_core(mine[:half_rows], other))
        full_b.append(mine[half_rows])
    stack_w, stack_b = jnp.stack(full_w), jnp.stack(full_b)
    shard_w = [lax.dynamic_index_in_dim(stack_w, (group - i) % groups, 0, keepdims=False) for i in range(groups)]
    shard_b = [lax.dynamic_index_in_dim(stack_b, (group - i) % groups, 0, keepdims=False) for i in range(groups)]
    w_seq = jnp.concatenate(
        [w[:, a * local_width : (a + 1) * local_width] for a in range(3) for w in shard_w], axis=1
    )
    b_seq = jnp.concatenate(
        [b[a * local_width : (a + 1) * local_width] for a in range(3) for b in shard_b]
    ).astype(F32)

    half_count = row_count // 2
    x_seqs, joints, heads_list = [], [], []
    for step in range(micro_count):
        sent = placed_list[step]
        from_one = swap(sent, "tensor", 1)
        from_two = swap(sent, "tensor", 2)
        from_three_a = swap(from_one[:half_count], "tensor", 2)
        from_three_b = swap(from_two[half_count:], "tensor", 1)
        x_seq = jnp.concatenate([sent, from_one, from_two, from_three_a, from_three_b], axis=0)
        x_seqs.append(x_seq)
        joints.append((product(x_seq, w_seq) + b_seq).astype(BF))

    w_out_all = lax.all_gather(w_out, "tensor", axis=0, tiled=True)

    ff_half = ff_local // 2
    up_t = w_up.T
    piece = jnp.concatenate(
        [
            lax.dynamic_slice_in_dim(up_t, core * ff_half, ff_half, 0),
            jnp.pad(
                lax.dynamic_slice_in_dim(b_up, core * ff_half, ff_half, 0)[None, :],
                ((0, PAD - 1), (0, width - ff_half)),
            ),
            lax.dynamic_slice_in_dim(w_down, core * ff_half, ff_half, 0),
        ],
        axis=0,
    )
    cut = ff_half + PAD
    piece = lax.optimization_barrier((piece, x_seqs, w_seq))[0]
    got = {0: piece}
    fw = bw = piece
    for s in range(1, far):
        fw, bw = forward(fw), backward(bw)
        got[-s], got[s] = fw, bw
    got[far] = jnp.concatenate([forward(fw[:cut]), backward(bw[cut:])], axis=0)
    offsets = [0] + [sign * s for s in range(1, far) for sign in (-1, 1)] + [far]
    slots = {}
    blocks = []
    for o in offsets:
        slots[o] = len(blocks)
        blocks.append(got[o])
        blocks.append(swap(got[o], "dp", 1))
    up_all = jnp.concatenate([b[:ff_half] for b in blocks], axis=0)
    down_all = jnp.concatenate([b[cut:] for b in blocks], axis=0)
    b_up_all = jnp.concatenate([b[ff_half, :ff_half] for b in blocks]).astype(F32)

    for step in range(micro_count):
        heads = attn_forward(joints[step], part_width)
        pieces = [heads[:row_count]] + [
            swap(heads[j * row_count : (j + 1) * row_count], "tensor", j) for j in range(1, parts)
        ]
        stacked = jnp.stack(pieces)
        heads_list.append(
            jnp.concatenate(
                [lax.dynamic_index_in_dim(stacked, part ^ j, 0, keepdims=False) for j in range(parts)],
                axis=1,
            )
        )

    placed = jnp.concatenate(placed_list, axis=0).astype(F32)
    replaced = jnp.concatenate(replaced_list, axis=0)
    cot = jnp.concatenate(cot_list, axis=0)
    heads_out = jnp.concatenate(heads_list, axis=0)
    gain_one, gain_two = ln1_gain.astype(F32), ln2_gain.astype(F32)
    norm_one, scale_one = norm_forward(placed + product(heads_out, w_out_all) + b_out.astype(F32))
    first = norm_one * gain_one + ln1_bias.astype(F32)
    first_low = first.astype(BF)
    upper = against(first_low, up_all) + b_up_all
    hidden_low = jax.nn.gelu(upper, approximate=False).astype(BF)
    fed = product(hidden_low, down_all) + b_down.astype(F32)
    norm_two, scale_two = norm_forward(first + fed)
    layer_out = (norm_two * gain_two + ln2_bias.astype(F32)).astype(BF)

    d_pre_two = norm_backward(norm_two, scale_two, gain_two, cot)
    d_fed = d_pre_two.astype(BF)
    d_hidden = against(d_fed, down_all)
    phi = jnp.exp(-0.5 * upper * upper) * (0.5 / jnp.pi) ** 0.5
    big_phi = 0.5 * (1.0 + lax.erf(upper * 0.5**0.5))
    d_upper = (d_hidden * (big_phi + upper * phi)).astype(BF)
    d_first = d_pre_two + product(d_upper, up_all)
    d_pre_one = norm_backward(norm_one, scale_one, gain_one, d_first)
    d_attended = d_pre_one.astype(BF)
    d_heads = against(d_attended, w_out_all).astype(BF)

    d_joints = []
    for step in range(micro_count):
        own = d_heads[step * row_count : (step + 1) * row_count]
        cols = [
            lax.dynamic_slice_in_dim(own, (part ^ j) * part_width, part_width, 1) for j in range(parts)
        ]
        seq_grads = jnp.concatenate(
            [cols[0]] + [swap(cols[j], "tensor", j) for j in range(1, parts)], axis=0
        )
        d_joints.append(jnp.concatenate(attn_backward(joints[step], seq_grads, part_width), axis=1))

    def ff_block(index):
        cols = slice(index * ff_half, (index + 1) * ff_half)
        return jnp.concatenate(
            [over_rows(d_upper[:, cols], first_low), over_rows(hidden_low[:, cols], d_fed)], axis=0
        )

    def ff_share(offset):
        other = swap(ff_block(slots[offset] + 1).astype(BF), "dp", 1)
        return ff_block(slots[offset]) + other.astype(F32)

    share = ff_share(far)
    fw = forward(share[:ff_half].astype(BF))
    bw = backward(share[ff_half:].astype(BF))
    for s in range(far - 1, 0, -1):
        fw_add, bw_add = fw.astype(F32), bw.astype(F32)
        if s == far - 1:
            fw_add = jnp.pad(fw_add, ((0, ff_half), (0, 0)))
            bw_add = jnp.pad(bw_add, ((ff_half, 0), (0, 0)))
        fw = forward((ff_share(s) + fw_add).astype(BF))
        bw = backward((ff_share(-s) + bw_add).astype(BF))
    ff_sum = (ff_share(0) + fw.astype(F32) + bw.astype(F32)).astype(BF)

    def over_dp(values):
        bit = 2
        while bit < dp_count:
            values = (values.astype(F32) + swap(values, "dp", bit).astype(F32)).astype(BF)
            bit *= 2
        return values

    ff_sum = over_dp(ff_sum)
    ff_other = swap(ff_sum, "dp", 1)
    grad_w_up = by_core(ff_sum[:ff_half], ff_other[:ff_half]).astype(F32).T
    grad_w_down = by_core(ff_sum[ff_half:], ff_other[ff_half:]).astype(F32)

    grad_w_out = lax.psum(
        lax.psum_scatter(
            over_rows(heads_out, d_attended).astype(BF), "tensor", scatter_dimension=0, tiled=True
        ),
        "dp",
    ).astype(F32)

    d_w_seq = sum(over_rows(x_seqs[m], d_joints[m]) for m in range(micro_count))
    other_half = lax.dynamic_slice_in_dim(d_w_seq, (1 - core) * half_rows, half_rows, 0).astype(BF)
    my_half = lax.dynamic_slice_in_dim(d_w_seq, core * half_rows, half_rows, 0)
    my_half = (my_half + swap(other_half, "dp", 1).astype(F32)).astype(BF)
    by_shard = jnp.stack(
        [
            jnp.concatenate(
                [
                    my_half[:, a * part_width + i * local_width : a * part_width + (i + 1) * local_width]
                    for a in range(3)
                ],
                axis=1,
            )
            for i in range(groups)
        ]
    )
    joint_sum = sum(
        lax.ppermute(
            lax.dynamic_index_in_dim(by_shard, (group - k) % groups, 0, keepdims=False),
            "tensor",
            [(b, a) for a, b in spread[k]],
        ).astype(F32)
        for k in range(groups)
    )
    joint_sum = over_dp(joint_sum.astype(BF))
    grad_joint = by_core(joint_sum, swap(joint_sum, "dp", 1)).astype(F32)

    grad_list = []
    for step in range(micro_count):
        share = against(d_joints[step], w_seq)
        rows = [share[j * row_count : (j + 1) * row_count] for j in range(parts)]
        to_two = swap(rows[3][:half_count].astype(BF), "tensor", 2).astype(F32)
        to_one = swap(rows[3][half_count:].astype(BF), "tensor", 1).astype(F32)
        via_one = rows[1] + jnp.pad(to_two, ((0, half_count), (0, 0)))
        via_two = rows[2] + jnp.pad(to_one, ((half_count, 0), (0, 0)))
        total = (
            rows[0]
            + swap(via_one.astype(BF), "tensor", 1).astype(F32)
            + swap(via_two.astype(BF), "tensor", 2).astype(F32)
        )
        mine = slice(step * row_count, (step + 1) * row_count)
        grad_list.append(jnp.where(replaced[mine, None], 0.0, d_pre_one[mine] + total))

    def over_all(values):
        for axis, size in (("dp", dp_count), ("tensor", count)):
            bit = 1
            while bit < size:
                values = values + swap(values, axis, bit)
                bit *= 2
        return values

    rel_b_up = jnp.sum(d_upper.astype(F32), axis=0).reshape(count, 2, ff_half)
    rel_b_up = jnp.where(own_first, rel_b_up, rel_b_up[:, ::-1]).reshape(count, ff_local)
    slot_of = [0] * count
    for o in offsets:
        slot_of[o % count] = slots[o] // 2
    place = jnp.array([order.index(s) for s in range(count)], jnp.int32)
    wanted = jnp.array(slot_of, jnp.int32)[(place - ring_pos) % count]
    all_b_up = rel_b_up[wanted].reshape(-1, width)
    early = jnp.concatenate(
        [
            all_b_up,
            jnp.sum(d_pre_one, axis=0)[None],
            jnp.sum(d_first * norm_one, axis=0)[None],
            jnp.sum(d_first, axis=0)[None],
            jnp.sum(d_pre_two, axis=0)[None],
            jnp.sum(cot * norm_two, axis=0)[None],
            jnp.sum(cot, axis=0)[None],
        ],
        axis=0,
    )
    early = over_all(early)
    b_rows = all_b_up.shape[0]
    grad_b_up = lax.dynamic_slice_in_dim(early[:b_rows].reshape(-1), rank * ff_local, ff_local, 0)
    grad_b_out, grad_gone, grad_bone, grad_b_down, grad_gtwo, grad_btwo = (
        early[b_rows + i] for i in range(6)
    )
    table = jnp.zeros((vocab_count, width), F32)
    for step in range(micro_count):
        table = table + lax.dot_general(
            hot_list[step],
            d_pre_one[step * row_count : (step + 1) * row_count],
            ROWS_DIMS,
            precision=lax.Precision.HIGHEST,
            preferred_element_type=F32,
        )
    hot_sum = sum(over_rows(seq_hot_list[m], d_joints[m]) for m in range(micro_count))
    table = table + lax.dot_general(
        hot_sum,
        w_seq.astype(F32),
        LAST_DIMS,
        precision=lax.Precision.HIGHEST,
        preferred_element_type=F32,
    )
    d_b_seq = sum(jnp.sum(d_joints[m].astype(F32), axis=0) for m in range(micro_count))
    empty = jnp.zeros((width,), F32)
    d_b_query = lax.dynamic_update_slice_in_dim(empty, d_b_seq[:part_width], part * part_width, 0)
    d_b_value = lax.dynamic_update_slice_in_dim(empty, d_b_seq[2 * part_width :], part * part_width, 0)
    late = over_all(jnp.concatenate([table, d_b_query[None], d_b_value[None]], axis=0))
    grad_table = late[:vocab_count]
    grad_b_query = lax.dynamic_slice_in_dim(late[vocab_count], rank * local_width, local_width, 0)
    grad_b_value = lax.dynamic_slice_in_dim(late[vocab_count + 1], rank * local_width, local_width, 0)

    return (
        layer_out.reshape(micro_count, row_count, width),
        jnp.stack(grad_list),
        grad_table,
        grad_joint[:, :local_width],
        grad_b_query,
        grad_joint[:, local_width : 2 * local_width],
        grad_joint[:, 2 * local_width :],
        grad_b_value,
        grad_w_out,
        grad_b_out,
        grad_gone,
        grad_bone,
        grad_w_up,
        grad_b_up,
        grad_w_down,
        grad_b_down,
        grad_gtwo,
        grad_btwo,
    )


def solution(mesh):
    return jax.shard_map(
        shards,
        mesh=mesh,
        in_specs=(
            P(None, ("dp", "tensor"), None),
            P(),
            P(None, "dp", None),
            P(None, "dp", None),
            P(None, "tensor"),
            P("tensor"),
            P(None, "tensor"),
            P(None, "tensor"),
            P("tensor"),
            P("tensor", None),
            P(),
            P(),
            P(),
            P(None, "tensor"),
            P("tensor"),
            P("tensor", None),
            P(),
            P(),
            P(),
            P(None, "dp", None, None),
        ),
        out_specs=(
            P(None, ("dp", "tensor"), None),
            P(None, ("dp", "tensor"), None),
            P(),
            P(None, "tensor"),
            P("tensor"),
            P(None, "tensor"),
            P(None, "tensor"),
            P("tensor"),
            P("tensor", None),
            P(),
            P(),
            P(),
            P(None, "tensor"),
            P("tensor"),
            P("tensor", None),
            P(),
            P(),
            P(),
        ),
        check_vma=False,
    )
```

```python
import functools

import jax
import jax.numpy as jnp
from jax import lax
from jax.experimental import pallas as pl
from jax.experimental.pallas import tpu as pltpu
from jax.sharding import PartitionSpec as P

HD = 64
LEN = 1024
EPSILON = 1e-12
SCALE = HD ** (-0.5)
ROWS_DIMS = (((0,), (0,)), ((), ()))
LAST_DIMS = (((1,), (1,)), ((), ()))
BF = jnp.bfloat16
F32 = jnp.float32
PAD = 16
PAIR = 2 * HD
VMEM_BYTES = 48 * 1024 * 1024


def product(left_mat, right_mat):
    return jnp.dot(left_mat, right_mat, preferred_element_type=F32)


def over_rows(left_mat, right_mat):
    return lax.dot_general(left_mat, right_mat, ROWS_DIMS, preferred_element_type=F32)


def against(left_mat, right_mat):
    return lax.dot_general(left_mat, right_mat, LAST_DIMS, preferred_element_type=F32)


def swap(values, axis, bit):
    count = lax.axis_size(axis)
    return lax.ppermute(values, axis, [(i, i ^ bit) for i in range(count)])


def fence(*trees):
    return lax.optimization_barrier(trees)


def whole_block(*shape):
    return pl.BlockSpec(shape, lambda *_: (0,) * len(shape))


def params():
    return pltpu.CompilerParams(vmem_limit_bytes=VMEM_BYTES)


def cost(flops, nbytes, transcendentals=0):
    return pl.CostEstimate(flops=flops, bytes_accessed=nbytes, transcendentals=transcendentals)


def assemble_kernel(groups, local, half, at_ref, *refs):
    mines, others = refs[:groups], refs[groups : 2 * groups]
    w_ref, b_ref = refs[2 * groups :]
    for i in range(groups):
        for k in range(groups):

            @pl.when(at_ref[1 + i] == k)
            def _(i=i, k=k):
                for a in range(3):
                    source = pl.ds(a * local, local)
                    lane = (3 * (i * local // PAIR) + a) * PAIR + i * local % PAIR
                    target = pl.ds(lane, local)
                    top = pl.multiple_of(at_ref[0] * half, half)
                    low = pl.multiple_of((1 - at_ref[0]) * half, half)
                    w_ref[pl.ds(top, half), target] = mines[k][pl.ds(0, half), source]
                    w_ref[pl.ds(low, half), target] = others[k][:, source]
                    b_ref[:, target] = mines[k][pl.ds(half, PAD), source][0:1].astype(F32)


def assemble(at, mines, others, local):
    groups = len(mines)
    half, width3 = others[0].shape
    return pl.pallas_call(
        functools.partial(assemble_kernel, groups, local, half),
        out_shape=(
            jax.ShapeDtypeStruct((2 * half, groups * width3), BF),
            jax.ShapeDtypeStruct((1, groups * width3), F32),
        ),
        grid_spec=pltpu.PrefetchScalarGridSpec(
            num_scalar_prefetch=1,
            grid=(1,),
            in_specs=[whole_block(*m.shape) for m in (*mines, *others)],
            out_specs=(whole_block(2 * half, groups * width3), whole_block(1, groups * width3)),
        ),
        compiler_params=params(),
        cost_estimate=cost(0, 8 * half * groups * width3),
        name="assemble",
    )(at, *mines, *others)


def project_kernel(parts, at_ref, *refs):
    pieces = refs[: parts + 1]
    w_ref, b_ref, joint_ref, mine_ref, other_ref, x_ref = refs[parts + 1 :]
    step = pl.program_id(0)
    for j in range(parts - 1):

        @pl.when(step == j)
        def _(j=j):
            x_ref[...] = pieces[j][...]

    @pl.when(step == parts - 1)
    def _():
        rows = pieces[-1].shape[0]
        x_ref[pl.ds(0, rows), :] = pieces[-2][...]
        x_ref[pl.ds(rows, rows), :] = pieces[-1][...]

    joint_ref[...] = (product(x_ref[...], w_ref[...]) + b_ref[...]).astype(BF)
    half = mine_ref.shape[1]
    mine_ref[...] = x_ref[:, pl.ds(pl.multiple_of(at_ref[0] * half, half), half)]
    other_ref[...] = x_ref[:, pl.ds(pl.multiple_of((1 - at_ref[0]) * half, half), half)]


def project(at, pieces, w_seq, b_seq):
    parts = len(pieces) - 1
    rows, width = pieces[0].shape
    joint_width = w_seq.shape[1]
    half = jax.ShapeDtypeStruct((parts * rows, width // 2), BF)
    half_block = pl.BlockSpec((rows, width // 2), lambda i, s: (i, 0))
    return pl.pallas_call(
        functools.partial(project_kernel, parts),
        out_shape=(jax.ShapeDtypeStruct((parts * rows, joint_width), BF), half, half),
        grid_spec=pltpu.PrefetchScalarGridSpec(
            num_scalar_prefetch=1,
            grid=(parts,),
            in_specs=[whole_block(*p.shape) for p in pieces]
            + [whole_block(*w_seq.shape), whole_block(*b_seq.shape)],
            out_specs=(pl.BlockSpec((rows, joint_width), lambda i, s: (i, 0)), half_block, half_block),
            scratch_shapes=[pltpu.VMEM((rows, width), BF)],
        ),
        compiler_params=params(),
        cost_estimate=cost(2 * parts * rows * width * joint_width, 12 * parts * rows * width),
        name="project",
    )(at, *pieces, w_seq, b_seq)


def attn_forward_kernel(q_ref, k_ref, v_ref, *outs):
    mixed = []
    for head in range(2):
        lanes = pl.ds(head * HD, HD)
        scores = against(q_ref[:, lanes], k_ref[:, lanes])
        top = jnp.max(scores, axis=-1, keepdims=True)
        weights = jnp.exp((scores - top) * SCALE)
        total = jnp.sum(weights, axis=-1, keepdims=True)
        mixed.append(product(weights.astype(BF), v_ref[:, lanes]) / total)
    value = jnp.concatenate(mixed, axis=1).astype(BF)
    for j, out in enumerate(outs):

        @pl.when(pl.program_id(1) == j)
        def _(out=out):
            out[...] = value


def attn_forward(joint, parts):
    rows = joint.shape[0] // parts
    pairs = joint.shape[1] // (3 * PAIR)
    shape = jax.ShapeDtypeStruct((rows, pairs * PAIR), BF)
    return pl.pallas_call(
        attn_forward_kernel,
        out_shape=(shape,) * parts,
        grid=(pairs, parts),
        in_specs=[
            pl.BlockSpec((rows, PAIR), lambda g, i: (i, 3 * g)),
            pl.BlockSpec((parts * rows, PAIR), lambda g, i: (0, 3 * g + 1)),
            pl.BlockSpec((parts * rows, PAIR), lambda g, i: (0, 3 * g + 2)),
        ],
        out_specs=(pl.BlockSpec((rows, PAIR), lambda g, i: (0, g)),) * parts,
        compiler_params=params(),
        cost_estimate=cost(
            16 * joint.shape[0] ** 2 * pairs * PAIR, 3 * joint.size, 2 * pairs * joint.shape[0] ** 2
        ),
        name="attn_forward",
    )(joint, joint, joint)


def attn_backward_kernel(parts, q_ref, k_ref, v_ref, *refs):
    pieces = refs[:parts]
    d_ref, g_ref, kt_ref, dk_acc, dv_acc = refs[-5:]
    step = pl.program_id(0)
    rows = q_ref.shape[0]
    for j, piece in enumerate(pieces):

        @pl.when(step == j)
        def _(piece=piece):
            g_ref[...] = piece[...]

    @pl.when(step == 0)
    def _():
        kt_ref[...] = k_ref[...].T
        dk_acc[...] = jnp.zeros_like(dk_acc)
        dv_acc[...] = jnp.zeros_like(dv_acc)

    dq_parts = []
    for head in range(2):
        lanes = pl.ds(head * HD, HD)
        queries = q_ref[:, lanes]
        grads = g_ref[:, lanes]
        scores = against(k_ref[:, lanes], queries)
        top = jnp.max(scores, axis=0, keepdims=True)
        weights = jnp.exp((scores - top) * SCALE)
        probs = weights * (1.0 / jnp.sum(weights, axis=0, keepdims=True))
        d_probs = against(v_ref[:, lanes], grads)
        row_dot = jnp.sum(probs * d_probs, axis=0, keepdims=True)
        d_scores = (probs * (d_probs - row_dot)).astype(BF)
        dv_acc[:, lanes] += product(probs.astype(BF), grads)
        dk_acc[:, lanes] += product(d_scores, queries)
        dq_parts.append(product(kt_ref[lanes, :], d_scores))
    d_ref[pl.ds(step * rows, rows), pl.ds(0, PAIR)] = (
        jnp.concatenate(dq_parts, axis=0).T * SCALE
    ).astype(BF)

    @pl.when(step == parts - 1)
    def _():
        d_ref[:, pl.ds(PAIR, PAIR)] = (dk_acc[...] * SCALE).astype(BF)
        d_ref[:, pl.ds(2 * PAIR, PAIR)] = dv_acc[...].astype(BF)


def attn_backward(joint, pieces, step, pair, kept):
    parts = len(pieces)
    rows = joint.shape[0] // parts
    return pl.pallas_call(
        functools.partial(attn_backward_kernel, parts),
        out_shape=jax.ShapeDtypeStruct(joint.shape, BF),
        grid=(parts,),
        in_specs=[
            pl.BlockSpec((rows, PAIR), lambda i: (i, 3 * pair)),
            pl.BlockSpec((parts * rows, PAIR), lambda i: (0, 3 * pair + 1)),
            pl.BlockSpec((parts * rows, PAIR), lambda i: (0, 3 * pair + 2)),
        ]
        + [pl.BlockSpec((rows, PAIR), lambda i: (step, pair))] * parts
        + [pl.BlockSpec(memory_space=pl.ANY)] * len(kept),
        out_specs=pl.BlockSpec((parts * rows, 3 * PAIR), lambda i: (0, pair)),
        scratch_shapes=[
            pltpu.VMEM((rows, PAIR), BF),
            pltpu.VMEM((PAIR, parts * rows), BF),
            pltpu.VMEM((parts * rows, PAIR), F32),
            pltpu.VMEM((parts * rows, PAIR), F32),
        ],
        input_output_aliases={3 + parts + i: i for i in range(len(kept))},
        compiler_params=params(),
        cost_estimate=cost(20 * joint.shape[0] ** 2 * PAIR, 14 * joint.shape[0] * PAIR, 2 * joint.shape[0] ** 2),
        name="attn_backward",
    )(joint, joint, joint, *pieces, *kept)


def normed(values):
    row_mean = jnp.mean(values, axis=-1, keepdims=True)
    centred = values - row_mean
    row_var = jnp.mean(centred * centred, axis=-1, keepdims=True)
    scale = lax.rsqrt(row_var + EPSILON)
    return centred * scale, scale


def norm_backward(norm, scale, gain_vec, grads):
    d_norm = grads * gain_vec
    mean_d = jnp.mean(d_norm, axis=-1, keepdims=True)
    mean_dn = jnp.mean(d_norm * norm, axis=-1, keepdims=True)
    return (d_norm - mean_d - norm * mean_dn) * scale


def column_sums(sums_ref, *values):
    @pl.when(pl.program_id(0) == 0)
    def _():
        sums_ref[...] = jnp.zeros_like(sums_ref)

    for index, value in enumerate(values):
        sums_ref[pl.ds(index, 1), :] += jnp.sum(value, axis=0, keepdims=True)


def attend_kernel(micros, parts, at_ref, *refs):
    pieces, placed = refs[: micros * parts], refs[micros * parts : micros * (parts + 1)]
    mine_ref, other_ref, vec_ref, heads_ref, norm_ref, scale_ref, first_ref, low_ref, w_ref = refs[
        micros * (parts + 1) :
    ]

    @pl.when(pl.program_id(0) == 0)
    def _():
        shards_, rows = mine_ref.shape[:2]
        for shard in range(shards_):
            for half, core in ((mine_ref, at_ref[parts]), (other_ref, 1 - at_ref[parts])):
                row = pl.multiple_of((2 * shard + core) * rows, rows)
                w_ref[pl.ds(row, rows), :] = half[shard]

    for m in range(micros):

        @pl.when(pl.program_id(0) == m)
        def _(m=m):
            total = placed[m][...].astype(F32) + vec_ref[0:1, :]
            for j in range(parts):
                piece = pieces[m * parts + j][...]
                cols = piece.shape[1]
                at = pl.multiple_of(at_ref[j] * cols, cols)
                total = total + product(piece, w_ref[pl.ds(at, cols), :])
                heads_ref[:, pl.ds(at, cols)] = piece
            norm, scale = normed(total)
            first = norm * vec_ref[1:2, :] + vec_ref[2:3, :]
            norm_ref[...] = norm
            scale_ref[...] = jnp.broadcast_to(scale, scale_ref.shape)
            first_ref[...] = first + vec_ref[3:4, :]
            low_ref[...] = first.astype(BF)


def attend(at, pieces, placed, w_mine, w_other, vectors):
    micros, parts = len(pieces), len(pieces[0])
    rows, width = placed[0].shape
    flat = [p for group in pieces for p in group]

    def out(cols, dtype):
        return jax.ShapeDtypeStruct((micros * rows, cols), dtype)

    return pl.pallas_call(
        functools.partial(attend_kernel, micros, parts),
        out_shape=(
            out(width, BF),
            out(width, F32),
            out(128, F32),
            out(width, F32),
            out(width, BF),
            jax.ShapeDtypeStruct((width, width), BF),
        ),
        grid_spec=pltpu.PrefetchScalarGridSpec(
            num_scalar_prefetch=1,
            grid=(micros,),
            in_specs=[whole_block(*a.shape) for a in (*flat, *placed, w_mine, w_other, vectors)],
            out_specs=tuple(
                pl.BlockSpec((rows, cols), lambda i, s: (i, 0)) for cols in (width, width, 128, width, width)
            )
            + (whole_block(width, width),),
        ),
        compiler_params=params(),
        cost_estimate=cost(2 * micros * rows * width * width, 20 * micros * rows * width),
        name="attend",
    )(at, *flat, *placed, w_mine, w_other, vectors)


def second_norm_kernel(pre_ref, cot_ref, vec_ref, out_ref, d_ref, low_ref, sums_ref):
    norm, scale = normed(pre_ref[...])
    cot = cot_ref[...]
    out_ref[...] = (norm * vec_ref[0:1, :] + vec_ref[1:2, :]).astype(BF)
    d_pre = norm_backward(norm, scale, vec_ref[0:1, :], cot)
    d_ref[...] = d_pre
    low_ref[...] = d_pre.astype(BF)
    column_sums(sums_ref, d_pre, cot * norm, cot)


def second_norm(pre, cot, vectors):
    rows, width = pre.shape
    block = pl.BlockSpec((128, width), lambda i: (i, 0))
    return pl.pallas_call(
        second_norm_kernel,
        out_shape=(
            jax.ShapeDtypeStruct((rows, width), BF),
            jax.ShapeDtypeStruct((rows, width), F32),
            jax.ShapeDtypeStruct((rows, width), BF),
            jax.ShapeDtypeStruct((8, width), F32),
        ),
        grid=(rows // 128,),
        in_specs=[block, block, whole_block(*vectors.shape)],
        out_specs=(block, block, block, whole_block(8, width)),
        compiler_params=params(),
        cost_estimate=cost(30 * rows * width, 16 * rows * width),
        name="second_norm",
    )(pre, cot, vectors)


def attend_back_kernel(parts, at_ref, d_first_ref, norm_ref, scale_ref, vec_ref, w_ref, *refs):
    d_ref, low_ref, sums_ref = refs[:3]
    outs, low_all = refs[3:-1], refs[-1]
    d_first, norm = d_first_ref[...], norm_ref[...]
    d_pre = norm_backward(norm, scale_ref[:, 0:1], vec_ref[1:2, :], d_first)
    low = d_pre.astype(BF)
    d_ref[...] = d_pre
    low_ref[...] = low
    column_sums(sums_ref, d_pre, d_first * norm, d_first)
    rows = low.shape[0]
    step = pl.program_id(0)
    low_all[pl.ds(pl.multiple_of(step * rows, rows), rows), :] = low

    @pl.when(step == pl.num_programs(0) - 1)
    def _():
        for j in range(parts):
            cols = outs[j].shape[1]
            at = pl.multiple_of(at_ref[j] * cols, cols)
            outs[j][...] = against(low_all[...], w_ref[pl.ds(at, cols), :]).astype(BF)


def attend_back(at, d_first, norm, scale, vectors, w_out, parts):
    rows, width = d_first.shape
    split = 4
    block = pl.BlockSpec((rows // split, width), lambda i, s: (i, 0))
    piece = (rows, width // parts)
    return pl.pallas_call(
        functools.partial(attend_back_kernel, parts),
        out_shape=(
            jax.ShapeDtypeStruct((rows, width), F32),
            jax.ShapeDtypeStruct((rows, width), BF),
            jax.ShapeDtypeStruct((8, width), F32),
        )
        + (jax.ShapeDtypeStruct(piece, BF),) * parts,
        grid_spec=pltpu.PrefetchScalarGridSpec(
            num_scalar_prefetch=1,
            grid=(split,),
            in_specs=[
                block,
                block,
                pl.BlockSpec((rows // split, 128), lambda i, s: (i, 0)),
                whole_block(*vectors.shape),
                whole_block(*w_out.shape),
            ],
            out_specs=(block, block, whole_block(8, width)) + (whole_block(*piece),) * parts,
            scratch_shapes=[pltpu.VMEM((rows, width), BF)],
        ),
        compiler_params=params(),
        cost_estimate=cost(2 * rows * width * width, 20 * rows * width),
        name="attend_back",
    )(at, d_first, norm, scale, vectors, w_out)


def next_blocks(blocks, buf, sem):
    step = pl.program_id(0)

    def start(index, slot):
        for h in range(2):
            pltpu.make_async_copy(blocks[2 * index + h], buf.at[slot, h], sem.at[slot, h]).start()

    @pl.when(step == 0)
    def _():
        start(0, 0)

    for index in range(1, len(blocks) // 2):

        @pl.when(step + 1 == index)
        def _(index=index):
            start(index, index % 2)

    slot = step % 2
    for h in range(2):
        pltpu.make_async_copy(blocks[0], buf.at[slot, h], sem.at[slot, h]).wait()
    return [buf.at[slot, h] for h in range(2)]


def upper_tail(size, falling):
    t = 1.0 / (1.0 + (0.3275911 * 0.5**0.5) * size)
    series = 0.5 * 1.061405429 * t - 0.5 * 1.453152027
    series = series * t + 0.5 * 1.421413741
    series = series * t - 0.5 * 0.284496736
    series = series * t + 0.5 * 0.254829592
    return series * t * falling


def ff_forward_kernel(ff_half, count, first_ref, init_ref, *refs):
    sum_ref, hidden_ref, slope_ref, buf, sem = refs[-5:]
    cut = ff_half + PAD

    @pl.when(pl.program_id(0) == 0)
    def _():
        sum_ref[...] = init_ref[...]

    total = 0.0
    for h, block in enumerate(next_blocks(refs[:count], buf, sem)):
        bias = block[pl.ds(ff_half, PAD), pl.ds(0, ff_half)][0:1].astype(F32)
        upper = against(first_ref[...], block[pl.ds(0, ff_half), :]) + bias
        falling = jnp.exp(-0.5 * upper * upper)
        tail = upper_tail(jnp.abs(upper), falling)
        big_phi = jnp.where(upper > 0.0, 1.0 - tail, tail)
        hidden = (upper * big_phi).astype(BF)
        lanes = pl.ds(h * ff_half, ff_half)
        hidden_ref[:, lanes] = hidden
        slope_ref[:, lanes] = big_phi + upper * (falling * 0.3989422804014327)
        total = total + product(hidden, block[pl.ds(cut, ff_half), :])
    sum_ref[...] += total


def ff_forward(first_low, init, blocks, kept, base, ff_half, total):
    rows, width = first_low.shape
    count = len(blocks)
    column = pl.BlockSpec((rows, 2 * ff_half), lambda i: (0, base // 2 + i))
    anywhere = pl.BlockSpec(memory_space=pl.ANY)
    kept = list(kept)
    return pl.pallas_call(
        functools.partial(ff_forward_kernel, ff_half, count),
        out_shape=(
            jax.ShapeDtypeStruct((rows, width), F32),
            jax.ShapeDtypeStruct((rows, total), BF),
            jax.ShapeDtypeStruct((rows, total), F32),
        ),
        grid=(count // 2,),
        in_specs=[whole_block(rows, width)] * 2 + [anywhere] * (count + len(kept)),
        out_specs=(whole_block(rows, width), column, column),
        scratch_shapes=[
            pltpu.VMEM((2, 2) + blocks[0].shape, BF),
            pltpu.SemaphoreType.DMA((2, 2)),
        ],
        input_output_aliases={2 + count + i: 1 + i for i in range(len(kept))},
        compiler_params=params(),
        cost_estimate=cost(
            8 * rows * width * ff_half * count,
            10 * rows * width + count * ff_half * (4 * width + 6 * rows),
            2 * rows * ff_half * count,
        ),
        name="ff_forward",
    )(first_low, init, *blocks, *kept)


def ff_backward_kernel(ff_half, count, d_fed_ref, init_ref, slope_ref, *refs):
    d_upper_ref, d_first_ref, column_ref, buf, sem = refs[count:]
    cut = ff_half + PAD

    @pl.when(pl.program_id(0) == 0)
    def _():
        d_first_ref[...] = init_ref[...]

    total = 0.0
    for h, block in enumerate(next_blocks(refs[:count], buf, sem)):
        lanes = pl.ds(h * ff_half, ff_half)
        d_hidden = against(d_fed_ref[...], block[pl.ds(cut, ff_half), :])
        d_upper = (d_hidden * slope_ref[:, lanes]).astype(BF)
        d_upper_ref[:, lanes] = d_upper
        column_ref[0, :, lanes] = jnp.sum(d_upper.astype(F32), axis=0, keepdims=True)
        total = total + product(d_upper, block[pl.ds(0, ff_half), :])
    d_first_ref[...] += total


def ff_backward(d_fed, init, slope, blocks, ff_half):
    rows, width = d_fed.shape
    count = len(blocks)
    column = pl.BlockSpec((rows, 2 * ff_half), lambda i: (0, i))
    return pl.pallas_call(
        functools.partial(ff_backward_kernel, ff_half, count),
        out_shape=(
            jax.ShapeDtypeStruct((rows, count * ff_half), BF),
            jax.ShapeDtypeStruct((rows, width), F32),
            jax.ShapeDtypeStruct((count // 2, 1, 2 * ff_half), F32),
        ),
        grid=(count // 2,),
        in_specs=[whole_block(rows, width)] * 2 + [column] + [pl.BlockSpec(memory_space=pl.ANY)] * count,
        out_specs=(column, whole_block(rows, width), pl.BlockSpec((1, 1, 2 * ff_half), lambda i: (i, 0, 0))),
        scratch_shapes=[
            pltpu.VMEM((2, 2) + blocks[0].shape, BF),
            pltpu.SemaphoreType.DMA((2, 2)),
        ],
        compiler_params=params(),
        cost_estimate=cost(
            4 * rows * width * ff_half * count,
            10 * rows * width + count * ff_half * (4 * width + 6 * rows),
        ),
        name="ff_backward",
    )(d_fed, init, slope, *blocks)


def ff_grad_kernel(ff_half, spans, splits, joined, index_ref, first_ref, fed_ref, *refs):
    count = len(spans)
    total = splits[-1]
    ups, hiddens, outs = (refs[i * count : (i + 1) * count] for i in range(3))
    adds = list(refs[3 * count : 3 * count + sum(map(len, spans))])
    results = refs[3 * count + len(adds) :]
    pieces = len(splits) - 1
    for index in range(count):
        mine = [adds.pop(0) for _ in spans[index]]
        values = (
            (0, ff_half, lambda: over_rows(ups[index][...], first_ref[...])),
            (ff_half, 2 * ff_half, lambda: over_rows(hiddens[index][...], fed_ref[...])),
            (2 * ff_half, total, lambda: outs[index][...].astype(F32)),
        )
        for low, high, value in values:
            share = value()
            for (start, stop), add in zip(spans[index], mine):
                if start <= low and high <= stop:
                    share = share + add[pl.ds(low - start, high - low), :].astype(F32)
            for piece in range(pieces):
                if splits[piece] <= low and high <= splits[piece + 1]:
                    target = results[0 if joined else index * pieces + piece]
                    row = low - splits[piece] + joined * index * total
                    target[pl.ds(row, high - low), :] = share.astype(BF)


def ff_grad(d_upper, hidden, first_low, d_fed, d_out, items, out_index, ff_half, out_half, cuts=(), joined=False):
    rows, width = first_low.shape
    cols = width // 2
    count = len(items)
    total = 2 * ff_half + out_half
    splits = (0, *cuts, total)
    lanes = pl.BlockSpec((rows, cols), lambda i, s: (0, i))
    adds = [add for _, arrived in items for add in arrived]
    spans = tuple(tuple((start, start + height) for start, height, _, _ in arrived) for _, arrived in items)

    def column(block):
        return pl.BlockSpec((rows, ff_half), lambda i, s: (0, block))

    def out_rows(j):
        return pl.BlockSpec((out_half, cols), lambda i, s: (s[j], i))

    def lane_block(height, at=0):
        return pl.BlockSpec((height, cols), lambda i, s: (at, i))

    columns = [column(block) for block, _ in items]
    heights = [count * total] if joined else [b - a for a, b in zip(splits, splits[1:])] * count
    return pl.pallas_call(
        functools.partial(ff_grad_kernel, ff_half, spans, splits, int(joined)),
        out_shape=tuple(jax.ShapeDtypeStruct((height, width), BF) for height in heights),
        grid_spec=pltpu.PrefetchScalarGridSpec(
            num_scalar_prefetch=1,
            grid=(2,),
            in_specs=[lanes, lanes]
            + columns
            + columns
            + [out_rows(j) for j in range(count)]
            + [lane_block(height, at) for _, height, _, at in adds],
            out_specs=tuple(lane_block(height) for height in heights),
        ),
        compiler_params=params(),
        cost_estimate=cost(
            4 * rows * width * ff_half * count,
            4 * rows * width + count * 4 * rows * ff_half + (count + len(adds)) * 2 * total * width,
        ),
        name="ff_grad",
    )(
        out_index, first_low, d_fed, *[d_upper] * count, *[hidden] * count, *[d_out] * count,
        *[array for _, _, array, _ in adds],
    )


def shards(
    embedded,
    token_table,
    masked_pos,
    replace_ids,
    w_query,
    b_query,
    w_key,
    w_value,
    b_value,
    w_out,
    b_out,
    ln1_gain,
    ln1_bias,
    w_up,
    b_up,
    w_down,
    b_down,
    ln2_gain,
    ln2_bias,
    grad_masked,
):
    rank = lax.axis_index("tensor")
    count = lax.axis_size("tensor")
    dp_count = lax.axis_size("dp")
    core = lax.axis_index("dp") % 2
    micro_count, row_count, width = embedded.shape
    local_width = w_query.shape[1]
    ff_local = w_up.shape[1]
    vocab_count = token_table.shape[0]
    parts = LEN // row_count
    groups = count // parts
    part = rank % parts
    group = rank // parts
    part_width = width // parts
    pairs = part_width // PAIR
    half_count = row_count // 2
    half_rows = width // 2
    ff_half = ff_local // 2
    out_half = local_width // 2
    cut = ff_half + PAD
    own_first = core == 0
    micros = range(micro_count)

    def by_core(mine, other, axis=0):
        return jnp.where(
            own_first,
            jnp.concatenate([mine, other], axis=axis),
            jnp.concatenate([other, mine], axis=axis),
        )

    order = list(range(0, count, 2)) + list(range(count - 1, 0, -2))
    ring_fw = [(order[i], order[(i + 1) % count]) for i in range(count)]
    ring_bw = [(b, a) for a, b in ring_fw]
    far = count // 2
    ring_pos = jnp.where(rank % 2 == 0, rank // 2, count - 1 - rank // 2)
    offsets = [0] + [sign * s for s in range(1, far) for sign in (-1, 1)] + [far]
    slots = {o: index for index, o in enumerate(offsets)}

    def forward(values):
        return lax.ppermute(values, "tensor", ring_fw)

    def backward(values):
        return lax.ppermute(values, "tensor", ring_bw)

    part_order = jnp.stack([part ^ j for j in range(parts)]).astype(jnp.int32)

    slot_pos = lax.dynamic_index_in_dim(masked_pos, group, 1, keepdims=False)
    slot_ids = lax.dynamic_index_in_dim(replace_ids, group, 1, keepdims=False)
    slot_grads = lax.dynamic_index_in_dim(grad_masked, group, 1, keepdims=False)
    vocab_iota = jnp.arange(vocab_count, dtype=jnp.int32)

    def replacement(positions, step):
        matches = positions[:, None] == slot_pos[step][None, :]
        replaced = jnp.any(matches, axis=1)
        row_ids = jnp.sum(jnp.where(matches, slot_ids[step][None, :], 0), axis=1)
        hot = (row_ids[:, None] == vocab_iota[None, :]) & replaced[:, None]
        return matches, replaced, hot

    row_iota = jnp.arange(row_count, dtype=jnp.int32)
    placed, replaced_list, hots, cots, seq_hots = [], [], [], [], []
    for step in micros:
        matches, replaced, hot = replacement(part * row_count + row_iota, step)
        inserted = product(hot.astype(BF), token_table)
        placed.append(jnp.where(replaced[:, None], inserted, embedded[step].astype(F32)).astype(BF))
        replaced_list.append(replaced)
        hots.append(hot.astype(F32))
        cots.append(product(matches.astype(BF), slot_grads[step]))
        seq_pos = jnp.concatenate([(part ^ j) * row_count + row_iota for j in range(parts)])
        seq_hots.append(replacement(seq_pos, step)[2].astype(BF))

    joint_half = jnp.concatenate(
        [
            lax.dynamic_slice_in_dim(
                jnp.concatenate([w_query, w_key, w_value], axis=1), core * half_rows, half_rows, 0
            ),
            jnp.pad(
                jnp.concatenate([b_query, jnp.zeros_like(b_query), b_value])[None, :],
                ((0, PAD - 1), (0, 0)),
            ),
        ],
        axis=0,
    )
    spread = [
        [(groups * p + i, p + parts * ((i + k) % groups)) for p in range(parts) for i in range(groups)]
        for k in range(groups)
    ]
    piece = jnp.concatenate(
        [
            lax.dynamic_slice_in_dim(w_up.T, core * ff_half, ff_half, 0),
            jnp.pad(
                lax.dynamic_slice_in_dim(b_up, core * ff_half, ff_half, 0)[None, :],
                ((0, PAD - 1), (0, width - ff_half)),
            ),
            lax.dynamic_slice_in_dim(w_down, core * ff_half, ff_half, 0),
        ],
        axis=0,
    )

    w_mine = [lax.ppermute(joint_half, "tensor", spread[k]) for k in range(groups)]
    ones = [swap(placed[0], "tensor", 1)]
    twos = [swap(placed[0], "tensor", 2)]
    ones, twos, w_mine, placed, piece, cots, w_out = fence(ones, twos, w_mine, placed, piece, cots, w_out)
    w_out_half = lax.all_gather(
        lax.dynamic_slice_in_dim(w_out, core * out_half, out_half, 0), "tensor", axis=0
    )
    w_other = [swap(w[:half_rows], "dp", 1) for w in w_mine]
    w_seq, b_seq = assemble(
        jnp.stack([core] + [(group - i) % groups for i in range(groups)]).astype(jnp.int32),
        w_mine,
        w_other,
        local_width,
    )

    joints, x_mine, x_other, heads = [], [], [], []
    near = [piece[:cut], piece[cut:]]
    arrived = []
    at_core = core[None].astype(jnp.int32)
    for step in micros:
        threes = (swap(ones[step][:half_count], "tensor", 2), swap(twos[step][half_count:], "tensor", 1))
        rows = [placed[step], ones[step], twos[step], *threes]
        if step + 1 < micro_count:
            ones.append(swap(placed[step + 1], "tensor", 1))
            twos.append(swap(placed[step + 1], "tensor", 2))
        moved = (forward(near[step]), backward(near[step]))
        joint, mine, other = project(at_core, rows, w_seq, b_seq)
        pieces = attn_forward(joint, parts)
        joints.append(joint)
        x_mine.append(mine)
        x_other.append(other)
        ones, twos, moved, pieces, near = fence(ones, twos, moved, pieces, near)
        arrived.append(moved)
        heads.append([pieces[0]] + [swap(pieces[j], "tensor", j) for j in range(1, parts)])
    fw, bw = (jnp.concatenate([arrived[0][d], arrived[1][d]], axis=0) for d in range(2))
    heads, fw, bw, w_out_half = fence(heads, fw, bw, w_out_half)
    w_out_other = swap(w_out_half, "dp", 1)
    blocks = [piece, swap(piece, "dp", 1), fw, swap(fw, "dp", 1), bw, swap(bw, "dp", 1)]

    vectors_one = jnp.stack([b_out, ln1_gain, ln1_bias, b_down] + [b_out] * 4).astype(F32)
    heads_out, norm_one, scale_one, pre_two, first_low, w_out_all = attend(
        jnp.concatenate([part_order, at_core]), heads, placed, w_out_half, w_out_other, vectors_one
    )

    kept = ()

    def work_on(s):
        at = 0 if s == 0 else 4 * s - 2
        return ff_forward(
            first_low, pre_two, blocks[at : at + (2 if s in (0, far) else 4)], kept, at, ff_half,
            2 * count * ff_half,
        )

    for s in range(2, far + 1):
        if s < far:
            moved = [forward(fw), backward(bw)]
        else:
            moved = [jnp.concatenate([forward(fw[:cut]), backward(bw[cut:])], axis=0)]
        for t in (0, 1) if s == 2 else (s - 1,):
            pre_two, *kept = work_on(t)
        if s < far:
            moved, pre_two, kept = fence(moved, pre_two, kept)
            fw, bw = moved
        for block in moved:
            blocks += [block, swap(block, "dp", 1)]
    pre_two, *kept = work_on(far)
    hidden_low, slope = kept

    vectors_two = jnp.stack([ln2_gain, ln2_bias] + [ln2_bias] * 6).astype(F32)
    layer_out, d_pre_two, d_fed, sums_two = second_norm(pre_two, jnp.concatenate(cots, axis=0), vectors_two)
    d_upper, d_first, rel_b_up = ff_backward(d_fed, d_pre_two, slope, blocks, ff_half)
    d_pre_one, d_attended, sums_one, *d_heads = attend_back(
        part_order, d_first, norm_one, scale_one, vectors_one, w_out_all, parts
    )
    d_out = over_rows(heads_out, d_attended).astype(BF)
    seq_grads = [d_heads[0]] + [swap(d_heads[j], "tensor", j) for j in range(1, parts)]

    order_array = jnp.array(order, jnp.int32)

    total = 2 * ff_half + out_half

    def ff_blocks(items, other, cuts=()):
        index = [2 * order_array[(ring_pos + o) % count] + (1 - core if other else core) for o, _ in items]
        result = ff_grad(
            d_upper, hidden_low, first_low, d_fed, d_out,
            [(2 * slots[o] + other, arrived) for o, arrived in items],
            jnp.stack(index).astype(jnp.int32), ff_half, out_half, cuts, bool(other),
        )
        return result[0] if other else result

    d_joints = [() for _ in micros]
    work = [(m, g) for m in micros for g in range(pairs)]

    def row_share(step, j, low=0, high=row_count):
        rows = d_joints[step][0][j * row_count + low : j * row_count + high]
        return against(rows, w_seq)

    def diagonal(step):
        share = row_share(step, 3).astype(BF)
        return (swap(share[:half_count], "tensor", 2), swap(share[half_count:], "tensor", 1))

    def sides(step, arrived):
        to_two, to_one = (a.astype(F32) for a in arrived)
        via_one = row_share(step, 1) + jnp.pad(to_two, ((0, half_count), (0, 0)))
        via_two = row_share(step, 2) + jnp.pad(to_one, ((half_count, 0), (0, 0)))
        return (swap(via_one.astype(BF), "tensor", 1), swap(via_two.astype(BF), "tensor", 2))

    def input_grad(step, arrived):
        mine = slice(step * row_count, (step + 1) * row_count)
        total = d_pre_one[mine] + row_share(step, 0) + arrived[0].astype(F32) + arrived[1].astype(F32)
        return jnp.where(replaced_list[step][:, None], 0.0, total)

    others = swap(ff_blocks([(far, [])], 1), "dp", 1)
    next_others = ff_blocks([(far - 1, []), (1 - far, [])], 1)
    parcel = ff_blocks([(far, [(0, total, others, 0)])], 0, (ff_half,))
    seq_grads, parcel, next_others = fence(seq_grads, parcel, next_others)
    partial = [() for _ in micros]
    for index, s in enumerate(range(far, 0, -1)):
        joints, d_joints, d_upper, parcel = fence(joints, d_joints, d_upper, parcel)
        moved = [forward(parcel[0]), backward(parcel[1])]
        others = swap(next_others, "dp", 1)
        for m in micros:
            if index == pairs * (m + 1):
                partial[m] = diagonal(m)
            elif index == pairs * (m + 1) + 1:
                partial[m] = sides(m, partial[m])
        next_others = ()
        if s > 1:
            next_others = ff_blocks([(s - 2, []), (2 - s, [])] if s > 2 else [(0, [])], 1)
        if work:
            m, g = work.pop(0)
            d_joints[m] = (attn_backward(joints[m], seq_grads, m, g, d_joints[m]),)
        moved, others, next_others, d_joints, partial = fence(moved, others, next_others, d_joints, partial)
        if s > 1:
            heights = (ff_half, total - ff_half) if s == far else (total, total)
            starts = (0, ff_half) if s == far else (0, 0)
            parcel = ff_blocks(
                [
                    (s - 1, [(0, total, others, 0), (starts[0], heights[0], moved[0], 0)]),
                    (1 - s, [(0, total, others, 1), (starts[1], heights[1], moved[1], 0)]),
                ],
                0,
            )
    ff_sum = ff_blocks([(0, [(0, total, others, 0), (0, total, moved[0], 0), (0, total, moved[1], 0)])], 0)[0]

    def over_dp(values):
        bit = 2
        while bit < dp_count:
            values = (values.astype(F32) + swap(values, "dp", bit).astype(F32)).astype(BF)
            bit *= 2
        return values

    def over_bits(values, axis, low, high):
        while low < high:
            if 2 * low < high:
                near, side, both = (swap(values, axis, bit) for bit in (low, 2 * low, 3 * low))
                values = (values + near) + (side + both)
            else:
                values = values + swap(values, axis, low)
            low *= 4
        return values

    rel_b_up = rel_b_up.reshape(count, 2, ff_half)
    rel_b_up = jnp.where(own_first, rel_b_up, rel_b_up[:, ::-1]).reshape(count, ff_local)
    slot_of = [0] * count
    for o, slot in slots.items():
        slot_of[o % count] = slot
    place = jnp.array([order.index(s) for s in range(count)], jnp.int32)
    wanted = jnp.array(slot_of, jnp.int32)[(place - ring_pos) % count]
    all_b_up = rel_b_up[wanted].reshape(-1, width)
    b_rows = all_b_up.shape[0]
    table = jnp.zeros((vocab_count, width), F32)
    for step in micros:
        table = table + lax.dot_general(
            hots[step],
            d_pre_one[step * row_count : (step + 1) * row_count],
            ROWS_DIMS,
            precision=lax.Precision.HIGHEST,
            preferred_element_type=F32,
        )
    hot_sum = sum(over_rows(seq_hots[m], d_joints[m][0]) for m in micros)
    table = table + lax.dot_general(
        hot_sum,
        w_seq.astype(F32),
        LAST_DIMS,
        precision=lax.Precision.HIGHEST,
        preferred_element_type=F32,
    )
    d_b_seq = sum(jnp.sum(d_joints[m][0].astype(F32), axis=0) for m in micros)
    empty = jnp.zeros((width,), F32)
    d_b_query, d_b_value = (
        lax.dynamic_update_slice_in_dim(
            empty,
            jnp.concatenate([d_b_seq[(3 * g + a) * PAIR : (3 * g + a + 1) * PAIR] for g in range(pairs)]),
            part * part_width,
            0,
        )
        for a in (0, 2)
    )
    small = jnp.concatenate(
        [table, d_b_query[None], d_b_value[None], sums_one[:3], sums_two[:3], all_b_up], axis=0
    )

    last = micro_count - 1
    other_half = sum(over_rows(x_other[m], d_joints[m][0]) for m in micros).astype(BF)
    other_half = swap(other_half, "dp", 1)
    if far < 2 + pairs * micro_count:
        partial[last] = diagonal(last)
    small = over_bits(small, "dp", 1, dp_count)
    my_half = sum(over_rows(x_mine[m], d_joints[m][0]) for m in micros)
    my_half = (my_half + other_half.astype(F32)).astype(BF)
    my_half, ff_sum, partial, small = fence(my_half, ff_sum, partial, small)

    if local_width != PAIR:
        columns = [
            jnp.concatenate(
                [my_half[:, (3 * g + a) * PAIR : (3 * g + a + 1) * PAIR] for g in range(pairs)], axis=1
            )
            for a in range(3)
        ]
        my_half = jnp.concatenate(
            [c[:, i * local_width : (i + 1) * local_width] for i in range(groups) for c in columns], axis=1
        )
    joint_sum = sum(
        lax.ppermute(
            lax.dynamic_slice_in_dim(
                my_half, (group - k) % groups * 3 * local_width, 3 * local_width, 1
            ),
            "tensor",
            [(b, a) for a, b in spread[k]],
        ).astype(F32)
        for k in range(groups)
    ).astype(BF)
    if far < 2 + pairs * micro_count:
        partial[last] = sides(last, partial[last])
    ff_sum = over_dp(ff_sum)
    small = over_bits(small, "tensor", 1, min(4, count))
    joint_sum, ff_sum, partial, small = fence(joint_sum, ff_sum, partial, small)

    ff_other = swap(ff_sum, "dp", 1)
    joint_sum = over_dp(joint_sum)
    small = over_bits(small, "tensor", 4, count)
    joint_sum, small, ff_other = fence(joint_sum, small, ff_other)
    grad_joint = by_core(joint_sum, swap(joint_sum, "dp", 1)).astype(F32)
    grad_w_up = by_core(ff_sum[:ff_half], ff_other[:ff_half]).astype(F32).T
    grad_w_down = by_core(ff_sum[ff_half : 2 * ff_half], ff_other[ff_half : 2 * ff_half]).astype(F32)
    grad_w_out = by_core(ff_sum[2 * ff_half :], ff_other[2 * ff_half :]).astype(F32)
    grad_list = [input_grad(m, partial[m]) for m in micros]
    grad_b_query, grad_b_value = (
        lax.dynamic_slice_in_dim(small[vocab_count + i], rank * local_width, local_width, 0) for i in range(2)
    )
    grad_b_out, grad_gone, grad_bone, grad_b_down, grad_gtwo, grad_btwo = (
        small[vocab_count + 2 + i] for i in range(6)
    )
    grad_b_up = lax.dynamic_slice_in_dim(small[vocab_count + 8 :].reshape(-1), rank * ff_local, ff_local, 0)

    return (
        layer_out.reshape(micro_count, row_count, width),
        jnp.stack(grad_list),
        small[:vocab_count],
        grad_joint[:, :local_width],
        grad_b_query,
        grad_joint[:, local_width : 2 * local_width],
        grad_joint[:, 2 * local_width :],
        grad_b_value,
        grad_w_out,
        grad_b_out,
        grad_gone,
        grad_bone,
        grad_w_up,
        grad_b_up,
        grad_w_down,
        grad_b_down,
        grad_gtwo,
        grad_btwo,
    )


def solution(mesh):
    return jax.shard_map(
        shards,
        mesh=mesh,
        in_specs=(
            P(None, ("dp", "tensor"), None),
            P(),
            P(None, "dp", None),
            P(None, "dp", None),
            P(None, "tensor"),
            P("tensor"),
            P(None, "tensor"),
            P(None, "tensor"),
            P("tensor"),
            P("tensor", None),
            P(),
            P(),
            P(),
            P(None, "tensor"),
            P("tensor"),
            P("tensor", None),
            P(),
            P(),
            P(),
            P(None, "dp", None, None),
        ),
        out_specs=(
            P(None, ("dp", "tensor"), None),
            P(None, ("dp", "tensor"), None),
            P(),
            P(None, "tensor"),
            P("tensor"),
            P(None, "tensor"),
            P(None, "tensor"),
            P("tensor"),
            P("tensor", None),
            P(),
            P(),
            P(),
            P(None, "tensor"),
            P("tensor"),
            P("tensor", None),
            P(),
            P(),
            P(),
        ),
        check_vma=False,
    )
```

```python
import functools

import jax
import jax.numpy as jnp
from jax import lax
from jax.experimental import pallas as pl
from jax.experimental.pallas import tpu as pltpu
from jax.sharding import PartitionSpec as P

HD = 64
LEN = 1024
EPSILON = 1e-12
SCALE = HD ** (-0.5)
ROWS_DIMS = (((0,), (0,)), ((), ()))
LAST_DIMS = (((1,), (1,)), ((), ()))
BF = jnp.bfloat16
F32 = jnp.float32
PAD = 16
PAIR = 2 * HD
LOG2E = 1.4426950408889634


def product(left_mat, right_mat):
    return jnp.dot(left_mat, right_mat, preferred_element_type=F32)


def over_rows(left_mat, right_mat):
    return lax.dot_general(left_mat, right_mat, ROWS_DIMS, preferred_element_type=F32)


def against(left_mat, right_mat):
    return lax.dot_general(left_mat, right_mat, LAST_DIMS, preferred_element_type=F32)


def swap(values, axis, bit):
    count = lax.axis_size(axis)
    return lax.ppermute(values, axis, [(i, i ^ bit) for i in range(count)])


def fence(*trees):
    return lax.optimization_barrier(trees)


def whole_block(*shape):
    return pl.BlockSpec(shape, lambda *_: (0,) * len(shape))


def params(megabytes=24):
    return pltpu.CompilerParams(vmem_limit_bytes=megabytes * 1024 * 1024)


def cost(flops, nbytes, transcendentals=0):
    return pl.CostEstimate(flops=flops, bytes_accessed=nbytes, transcendentals=transcendentals)


def assemble_kernel(groups, local, half, at_ref, *refs):
    mines, others = refs[:groups], refs[groups : 2 * groups]
    w_ref, b_ref = refs[2 * groups :]
    for i in range(groups):
        for k in range(groups):

            @pl.when(at_ref[1 + i] == k)
            def _(i=i, k=k):
                for a in range(3):
                    source = pl.ds(a * local, local)
                    lane = (3 * (i * local // PAIR) + a) * PAIR + i * local % PAIR
                    target = pl.ds(lane, local)
                    top = pl.multiple_of(at_ref[0] * half, half)
                    low = pl.multiple_of((1 - at_ref[0]) * half, half)
                    w_ref[pl.ds(top, half), target] = mines[k][pl.ds(0, half), source]
                    w_ref[pl.ds(low, half), target] = others[k][pl.ds(0, half), source]
                    b_ref[:, target] = mines[k][pl.ds(half, PAD), source][0:1].astype(F32)


def assemble(at, mines, others, local):
    groups = len(mines)
    half, width3 = others[0].shape[0] - PAD, others[0].shape[1]
    return pl.pallas_call(
        functools.partial(assemble_kernel, groups, local, half),
        out_shape=(
            jax.ShapeDtypeStruct((2 * half, groups * width3), BF),
            jax.ShapeDtypeStruct((1, groups * width3), F32),
        ),
        grid_spec=pltpu.PrefetchScalarGridSpec(
            num_scalar_prefetch=1,
            grid=(1,),
            in_specs=[whole_block(*m.shape) for m in (*mines, *others)],
            out_specs=(whole_block(2 * half, groups * width3), whole_block(1, groups * width3)),
        ),
        compiler_params=params(),
        cost_estimate=cost(0, 8 * half * groups * width3),
        name="assemble",
    )(at, *mines, *others)


def project_kernel(parts, at_ref, *refs):
    pieces = refs[: parts + 1]
    w_ref, b_ref, joint_ref, mine_ref, other_ref, x_ref = refs[parts + 1 :]
    step = pl.program_id(0)
    for j in range(parts - 1):

        @pl.when(step == j)
        def _(j=j):
            x_ref[...] = pieces[j][...]

    @pl.when(step == parts - 1)
    def _():
        rows = pieces[-1].shape[0]
        x_ref[pl.ds(0, rows), :] = pieces[-2][...]
        x_ref[pl.ds(rows, rows), :] = pieces[-1][...]

    joint_ref[...] = (product(x_ref[...], w_ref[...]) + b_ref[...]).astype(BF)
    half = mine_ref.shape[1]
    mine_ref[...] = x_ref[:, pl.ds(pl.multiple_of(at_ref[0] * half, half), half)]
    other_ref[...] = x_ref[:, pl.ds(pl.multiple_of((1 - at_ref[0]) * half, half), half)]


def project(at, pieces, w_seq, b_seq):
    parts = len(pieces) - 1
    rows, width = pieces[0].shape
    joint_width = w_seq.shape[1]
    half = jax.ShapeDtypeStruct((parts * rows, width // 2), BF)
    half_block = pl.BlockSpec((rows, width // 2), lambda i, s: (i, 0))
    return pl.pallas_call(
        functools.partial(project_kernel, parts),
        out_shape=(jax.ShapeDtypeStruct((parts * rows, joint_width), BF), half, half),
        grid_spec=pltpu.PrefetchScalarGridSpec(
            num_scalar_prefetch=1,
            grid=(parts,),
            in_specs=[whole_block(*p.shape) for p in pieces]
            + [whole_block(*w_seq.shape), whole_block(*b_seq.shape)],
            out_specs=(pl.BlockSpec((rows, joint_width), lambda i, s: (i, 0)), half_block, half_block),
            scratch_shapes=[pltpu.VMEM((rows, width), BF)],
        ),
        compiler_params=params(),
        cost_estimate=cost(2 * parts * rows * width * joint_width, 12 * parts * rows * width),
        name="project",
    )(at, *pieces, w_seq, b_seq)


def first_head(rows):
    return lax.broadcasted_iota(jnp.int32, (rows, PAIR), 1) < HD


def one_head(values, head, fill=0.0):
    first = first_head(values.shape[0])
    filled = jnp.full(values.shape, fill, values.dtype)
    return jnp.where(first, filled, values) if head else jnp.where(first, values, filled)


def attn_forward_kernel(q_ref, k_ref, v_ref, *refs):
    outs, log_ref = refs[:-1], refs[-1]
    rows = q_ref.shape[0]
    mixed, log_sums = [], []
    for head in range(2):
        scores = against(one_head(q_ref[...], head), k_ref[...])
        top = jnp.max(scores, axis=-1, keepdims=True) * (SCALE * LOG2E)
        weights = jnp.exp2(scores * (SCALE * LOG2E) - top).astype(BF)
        both = product(weights, one_head(v_ref[...], head, 1.0))
        total = pltpu.roll(both, HD, 1)
        mixed.append(both / total)
        log_sums.append(top + jnp.log(total) * LOG2E)
    first = first_head(rows)
    value = jnp.where(first, mixed[0], mixed[1]).astype(BF)
    turned = jnp.where(first, log_sums[0], log_sums[1]).T
    log_ref[0, 0:1, :] = turned[0:1]
    log_ref[0, 1:2, :] = turned[HD : HD + 1]
    for j, out in enumerate(outs):

        @pl.when(pl.program_id(1) == j)
        def _(out=out):
            out[...] = value


def attn_forward(joint, parts):
    rows = joint.shape[0] // parts
    pairs = joint.shape[1] // (3 * PAIR)
    shape = jax.ShapeDtypeStruct((rows, pairs * PAIR), BF)
    result = pl.pallas_call(
        attn_forward_kernel,
        out_shape=(shape,) * parts + (jax.ShapeDtypeStruct((pairs, 8, parts * rows), F32),),
        grid=(pairs, parts),
        in_specs=[
            pl.BlockSpec((rows, PAIR), lambda g, i: (i, 3 * g)),
            pl.BlockSpec((parts * rows, PAIR), lambda g, i: (0, 3 * g + 1)),
            pl.BlockSpec((parts * rows, PAIR), lambda g, i: (0, 3 * g + 2)),
        ],
        out_specs=(pl.BlockSpec((rows, PAIR), lambda g, i: (0, g)),) * parts
        + (pl.BlockSpec((1, 8, rows), lambda g, i: (g, 0, i)),),
        compiler_params=params(),
        cost_estimate=cost(
            16 * joint.shape[0] ** 2 * pairs * PAIR, 3 * joint.size, 2 * pairs * joint.shape[0] ** 2
        ),
        name="attn_forward",
    )(joint, joint, joint)
    return result[:parts], result[parts]


def attn_backward_kernel(parts, q_ref, k_ref, v_ref, log_ref, *refs):
    pieces, heads = refs[:parts], refs[parts : 2 * parts]
    d_ref, g_ref, o_ref, kt_ref, dk_acc, dv_acc = refs[-6:]
    step = pl.program_id(0)
    rows = q_ref.shape[0]
    for j in range(parts):

        @pl.when(step == j)
        def _(j=j):
            g_ref[...] = pieces[j][...]
            o_ref[...] = heads[j][...]

    @pl.when(step == 0)
    def _():
        kt_ref[...] = k_ref[...].T
        dk_acc[...] = jnp.zeros_like(dk_acc)
        dv_acc[...] = jnp.zeros_like(dv_acc)

    row_dots = (g_ref[...].astype(F32) * o_ref[...].astype(F32)).T
    dq_parts = []
    for head in range(2):
        queries = one_head(q_ref[...], head)
        grads = one_head(g_ref[...], head)
        row_dot = jnp.sum(row_dots[head * HD : (head + 1) * HD], axis=0, keepdims=True)
        log_sum = log_ref[0, pl.ds(head, 1), :]
        scores = against(k_ref[...], queries)
        probs = jnp.exp2(scores * (SCALE * LOG2E) - log_sum)
        d_probs = against(v_ref[...], grads)
        d_scores = (probs * (d_probs - row_dot)).astype(BF)
        dv_acc[...] += product(probs.astype(BF), grads)
        dk_acc[...] += product(d_scores, queries)
        dq_parts.append(product(kt_ref[pl.ds(head * HD, HD), :], d_scores))
    d_ref[pl.ds(step * rows, rows), pl.ds(0, PAIR)] = (
        jnp.concatenate(dq_parts, axis=0).T * SCALE
    ).astype(BF)

    @pl.when(step == parts - 1)
    def _():
        d_ref[:, pl.ds(PAIR, PAIR)] = (dk_acc[...] * SCALE).astype(BF)
        d_ref[:, pl.ds(2 * PAIR, PAIR)] = dv_acc[...].astype(BF)


def attn_backward(joint, log_sums, pieces, heads, step, pair, kept):
    parts = len(pieces)
    rows = joint.shape[0] // parts
    return pl.pallas_call(
        functools.partial(attn_backward_kernel, parts),
        out_shape=jax.ShapeDtypeStruct(joint.shape, BF),
        grid=(parts,),
        in_specs=[
            pl.BlockSpec((rows, PAIR), lambda i: (i, 3 * pair)),
            pl.BlockSpec((parts * rows, PAIR), lambda i: (0, 3 * pair + 1)),
            pl.BlockSpec((parts * rows, PAIR), lambda i: (0, 3 * pair + 2)),
            pl.BlockSpec((1, 8, rows), lambda i: (pair, 0, i)),
        ]
        + [pl.BlockSpec((rows, PAIR), lambda i: (step, pair))] * parts
        + [pl.BlockSpec((rows, PAIR), lambda i: (0, pair))] * parts
        + [pl.BlockSpec(memory_space=pl.ANY)] * len(kept),
        out_specs=pl.BlockSpec((parts * rows, 3 * PAIR), lambda i: (0, pair)),
        scratch_shapes=[
            pltpu.VMEM((rows, PAIR), BF),
            pltpu.VMEM((rows, PAIR), BF),
            pltpu.VMEM((PAIR, parts * rows), BF),
            pltpu.VMEM((parts * rows, PAIR), F32),
            pltpu.VMEM((parts * rows, PAIR), F32),
        ],
        input_output_aliases={4 + 2 * parts + i: i for i in range(len(kept))},
        compiler_params=params(60),
        cost_estimate=cost(1, 1),
        name="attn_backward",
    )(joint, joint, joint, log_sums, *pieces, *heads, *kept)


def normed(values):
    row_mean = jnp.mean(values, axis=-1, keepdims=True)
    centred = values - row_mean
    row_var = jnp.mean(centred * centred, axis=-1, keepdims=True)
    scale = lax.rsqrt(row_var + EPSILON)
    return centred * scale, scale


def norm_backward(norm, scale, gain_vec, grads):
    d_norm = grads * gain_vec
    mean_d = jnp.mean(d_norm, axis=-1, keepdims=True)
    mean_dn = jnp.mean(d_norm * norm, axis=-1, keepdims=True)
    return (d_norm - mean_d - norm * mean_dn) * scale


def column_sums(sums_ref, *values):
    @pl.when(pl.program_id(0) == 0)
    def _():
        sums_ref[...] = jnp.zeros_like(sums_ref)

    for index, value in enumerate(values):
        sums_ref[pl.ds(index, 1), :] += jnp.sum(value, axis=0, keepdims=True)


def attend_kernel(micros, parts, at_ref, *refs):
    pieces, placed = refs[: micros * parts], refs[micros * parts : micros * (parts + 1)]
    mine_ref, other_ref, vec_ref, heads_ref, norm_ref, scale_ref, first_ref, low_ref, w_ref = refs[
        micros * (parts + 1) :
    ]

    @pl.when(pl.program_id(0) == 0)
    def _():
        shards_, rows = mine_ref.shape[:2]
        for shard in range(shards_):
            for half, core in ((mine_ref, at_ref[parts]), (other_ref, 1 - at_ref[parts])):
                row = pl.multiple_of((2 * shard + core) * rows, rows)
                w_ref[pl.ds(row, rows), :] = half[shard]

    for m in range(micros):

        @pl.when(pl.program_id(0) == m)
        def _(m=m):
            total = placed[m][...].astype(F32) + vec_ref[0:1, :]
            for j in range(parts):
                piece = pieces[m * parts + j][...]
                cols = piece.shape[1]
                at = pl.multiple_of(at_ref[j] * cols, cols)
                total = total + product(piece, w_ref[pl.ds(at, cols), :])
                heads_ref[:, pl.ds(at, cols)] = piece
            norm, scale = normed(total)
            first = norm * vec_ref[1:2, :] + vec_ref[2:3, :]
            norm_ref[...] = norm
            scale_ref[...] = jnp.broadcast_to(scale, scale_ref.shape)
            first_ref[...] = first + vec_ref[3:4, :]
            low_ref[...] = first.astype(BF)


def attend(at, pieces, placed, w_mine, w_other, vectors):
    micros, parts = len(pieces), len(pieces[0])
    rows, width = placed[0].shape
    flat = [p for group in pieces for p in group]

    def out(cols, dtype):
        return jax.ShapeDtypeStruct((micros * rows, cols), dtype)

    return pl.pallas_call(
        functools.partial(attend_kernel, micros, parts),
        out_shape=(
            out(width, BF),
            out(width, F32),
            out(128, F32),
            out(width, F32),
            out(width, BF),
            jax.ShapeDtypeStruct((width, width), BF),
        ),
        grid_spec=pltpu.PrefetchScalarGridSpec(
            num_scalar_prefetch=1,
            grid=(micros,),
            in_specs=[whole_block(*a.shape) for a in (*flat, *placed, w_mine, w_other, vectors)],
            out_specs=tuple(
                pl.BlockSpec((rows, cols), lambda i, s: (i, 0)) for cols in (width, width, 128, width, width)
            )
            + (whole_block(width, width),),
        ),
        compiler_params=params(60),
        cost_estimate=cost(2 * micros * rows * width * width, 20 * micros * rows * width),
        name="attend",
    )(at, *flat, *placed, w_mine, w_other, vectors)


def second_norm_kernel(pre_ref, cot_ref, vec_ref, out_ref, d_ref, low_ref, sums_ref):
    norm, scale = normed(pre_ref[...])
    cot = cot_ref[...]
    out_ref[...] = (norm * vec_ref[0:1, :] + vec_ref[1:2, :]).astype(BF)
    d_pre = norm_backward(norm, scale, vec_ref[0:1, :], cot)
    d_ref[...] = d_pre
    low_ref[...] = d_pre.astype(BF)
    column_sums(sums_ref, d_pre, cot * norm, cot)


def second_norm(pre, cot, vectors):
    rows, width = pre.shape
    block = pl.BlockSpec((128, width), lambda i: (i, 0))
    return pl.pallas_call(
        second_norm_kernel,
        out_shape=(
            jax.ShapeDtypeStruct((rows, width), BF),
            jax.ShapeDtypeStruct((rows, width), F32),
            jax.ShapeDtypeStruct((rows, width), BF),
            jax.ShapeDtypeStruct((8, width), F32),
        ),
        grid=(rows // 128,),
        in_specs=[block, block, whole_block(*vectors.shape)],
        out_specs=(block, block, block, whole_block(8, width)),
        compiler_params=params(),
        cost_estimate=cost(30 * rows * width, 16 * rows * width),
        name="second_norm",
    )(pre, cot, vectors)


def attend_back_kernel(parts, at_ref, d_first_ref, norm_ref, scale_ref, vec_ref, w_ref, *refs):
    d_ref, low_ref, sums_ref = refs[:3]
    outs, low_all = refs[3:-1], refs[-1]
    d_first, norm = d_first_ref[...], norm_ref[...]
    d_pre = norm_backward(norm, scale_ref[:, 0:1], vec_ref[1:2, :], d_first)
    low = d_pre.astype(BF)
    d_ref[...] = d_pre
    low_ref[...] = low
    column_sums(sums_ref, d_pre, d_first * norm, d_first)
    rows = low.shape[0]
    step = pl.program_id(0)
    low_all[pl.ds(pl.multiple_of(step * rows, rows), rows), :] = low

    @pl.when(step == pl.num_programs(0) - 1)
    def _():
        for j in range(parts):
            cols = outs[j].shape[1]
            at = pl.multiple_of(at_ref[j] * cols, cols)
            outs[j][...] = against(low_all[...], w_ref[pl.ds(at, cols), :]).astype(BF)


def attend_back(at, d_first, norm, scale, vectors, w_out, parts):
    rows, width = d_first.shape
    split = 4
    block = pl.BlockSpec((rows // split, width), lambda i, s: (i, 0))
    piece = (rows, width // parts)
    return pl.pallas_call(
        functools.partial(attend_back_kernel, parts),
        out_shape=(
            jax.ShapeDtypeStruct((rows, width), F32),
            jax.ShapeDtypeStruct((rows, width), BF),
            jax.ShapeDtypeStruct((8, width), F32),
        )
        + (jax.ShapeDtypeStruct(piece, BF),) * parts,
        grid_spec=pltpu.PrefetchScalarGridSpec(
            num_scalar_prefetch=1,
            grid=(split,),
            in_specs=[
                block,
                block,
                pl.BlockSpec((rows // split, 128), lambda i, s: (i, 0)),
                whole_block(*vectors.shape),
                whole_block(*w_out.shape),
            ],
            out_specs=(block, block, whole_block(8, width)) + (whole_block(*piece),) * parts,
            scratch_shapes=[pltpu.VMEM((rows, width), BF)],
        ),
        compiler_params=params(),
        cost_estimate=cost(2 * rows * width * width, 20 * rows * width),
        name="attend_back",
    )(at, d_first, norm, scale, vectors, w_out)


def next_blocks(blocks, buf, sem):
    step = pl.program_id(0)

    def start(index, slot):
        for h in range(2):
            pltpu.make_async_copy(blocks[2 * index + h], buf.at[slot, h], sem.at[slot, h]).start()

    @pl.when(step == 0)
    def _():
        start(0, 0)

    for index in range(1, len(blocks) // 2):

        @pl.when(step + 1 == index)
        def _(index=index):
            start(index, index % 2)

    slot = step % 2
    for h in range(2):
        pltpu.make_async_copy(blocks[0], buf.at[slot, h], sem.at[slot, h]).wait()
    return [buf.at[slot, h] for h in range(2)]


def upper_tail(size, falling):
    t = 1.0 / (1.0 + (0.3275911 * 0.5**0.5) * size)
    series = 0.5 * 1.061405429 * t - 0.5 * 1.453152027
    series = series * t + 0.5 * 1.421413741
    series = series * t - 0.5 * 0.284496736
    series = series * t + 0.5 * 0.254829592
    return series * t * falling


def ff_forward_kernel(ff_half, count, first_ref, init_ref, *refs):
    sum_ref, hidden_ref, slope_ref, buf, sem = refs[-5:]
    cut = ff_half + PAD

    @pl.when(pl.program_id(0) == 0)
    def _():
        sum_ref[...] = init_ref[...]

    total = 0.0
    for h, block in enumerate(next_blocks(refs[:count], buf, sem)):
        bias = block[pl.ds(ff_half, PAD), pl.ds(0, ff_half)][0:1].astype(F32)
        upper = against(first_ref[...], block[pl.ds(0, ff_half), :]) + bias
        falling = jnp.exp(-0.5 * upper * upper)
        tail = upper_tail(jnp.abs(upper), falling)
        big_phi = jnp.where(upper > 0.0, 1.0 - tail, tail)
        hidden = (upper * big_phi).astype(BF)
        lanes = pl.ds(h * ff_half, ff_half)
        hidden_ref[:, lanes] = hidden
        slope_ref[:, lanes] = big_phi + upper * (falling * 0.3989422804014327)
        total = total + product(hidden, block[pl.ds(cut, ff_half), :])
    sum_ref[...] += total


def ff_forward(first_low, init, blocks, ff_half):
    rows, width = first_low.shape
    count = len(blocks)
    column = pl.BlockSpec((rows, 2 * ff_half), lambda i: (0, i))
    return pl.pallas_call(
        functools.partial(ff_forward_kernel, ff_half, count),
        out_shape=(
            jax.ShapeDtypeStruct((rows, width), F32),
            jax.ShapeDtypeStruct((rows, count * ff_half), BF),
            jax.ShapeDtypeStruct((rows, count * ff_half), F32),
        ),
        grid=(count // 2,),
        in_specs=[whole_block(rows, width)] * 2 + [pl.BlockSpec(memory_space=pl.ANY)] * count,
        out_specs=(whole_block(rows, width), column, column),
        scratch_shapes=[
            pltpu.VMEM((2, 2) + blocks[0].shape, BF),
            pltpu.SemaphoreType.DMA((2, 2)),
        ],
        compiler_params=params(),
        cost_estimate=cost(
            8 * rows * width * ff_half * count,
            10 * rows * width + count * ff_half * (4 * width + 6 * rows),
            2 * rows * ff_half * count,
        ),
        name="ff_forward",
    )(first_low, init, *blocks)


def ff_backward_kernel(ff_half, count, d_fed_ref, init_ref, slope_ref, *refs):
    d_upper_ref, d_first_ref, column_ref, buf, sem = refs[-5:]
    cut = ff_half + PAD

    @pl.when(pl.program_id(0) == 0)
    def _():
        d_first_ref[...] = init_ref[...]

    total = 0.0
    for h, block in enumerate(next_blocks(refs[:count], buf, sem)):
        lanes = pl.ds(h * ff_half, ff_half)
        d_hidden = against(d_fed_ref[...], block[pl.ds(cut, ff_half), :])
        d_upper = (d_hidden * slope_ref[:, lanes]).astype(BF)
        d_upper_ref[:, lanes] = d_upper
        column_ref[0, :, lanes] = jnp.sum(d_upper.astype(F32), axis=0, keepdims=True)
        total = total + product(d_upper, block[pl.ds(0, ff_half), :])
    d_first_ref[...] += total


def ff_backward(d_fed, init, slope, blocks, ff_half):
    rows, width = d_fed.shape
    count = len(blocks)
    column = pl.BlockSpec((rows, 2 * ff_half), lambda i: (0, i))
    return pl.pallas_call(
        functools.partial(ff_backward_kernel, ff_half, count),
        out_shape=(
            jax.ShapeDtypeStruct(slope.shape, BF),
            jax.ShapeDtypeStruct((rows, width), F32),
            jax.ShapeDtypeStruct((count // 2, 1, 2 * ff_half), F32),
        ),
        grid=(count // 2,),
        in_specs=[whole_block(rows, width)] * 2 + [column] + [pl.BlockSpec(memory_space=pl.ANY)] * count,
        out_specs=(column, whole_block(rows, width), pl.BlockSpec((1, 1, 2 * ff_half), lambda i: (i, 0, 0))),
        scratch_shapes=[
            pltpu.VMEM((2, 2) + blocks[0].shape, BF),
            pltpu.SemaphoreType.DMA((2, 2)),
        ],
        compiler_params=params(),
        cost_estimate=cost(
            4 * rows * width * ff_half * count,
            10 * rows * width + count * ff_half * (4 * width + 6 * rows),
        ),
        name="ff_backward",
    )(d_fed, init, slope, *blocks)


def ff_grad_kernel(ff_half, spans, splits, joined, first_ref, fed_ref, up_ref, hidden_ref, *refs):
    count = len(spans)
    total = splits[-1]
    adds = list(refs[: sum(map(len, spans))])
    results = refs[len(adds) :]
    pieces = len(splits) - 1
    ups = over_rows(up_ref[...], first_ref[...])
    hiddens = over_rows(hidden_ref[...], fed_ref[...])
    for index in range(count):
        mine = [adds.pop(0) for _ in spans[index]]
        at = slice(index * ff_half, (index + 1) * ff_half)
        for low, high, share in ((0, ff_half, ups[at]), (ff_half, total, hiddens[at])):
            for (start, stop), add in zip(spans[index], mine):
                if start <= low and high <= stop:
                    share = share + add[pl.ds(low - start, high - low), :].astype(F32)
            for piece in range(pieces):
                if splits[piece] <= low and high <= splits[piece + 1]:
                    target = results[0 if joined else index * pieces + piece]
                    row = low - splits[piece] + joined * index * total
                    target[pl.ds(row, high - low), :] = share.astype(BF)


def ff_grad(d_upper, hidden, first_low, d_fed, place, adds, ff_half, cuts=(), joined=False, megabytes=24):
    rows, width = first_low.shape
    cols = width // 2
    count = len(adds)
    total = 2 * ff_half
    splits = (0, *cuts, total)
    lanes = pl.BlockSpec((rows, cols), lambda i: (0, i))
    column = pl.BlockSpec((rows, count * ff_half), lambda i: (0, place))
    spans = tuple(tuple((start, start + height) for start, height, _, _ in arrived) for arrived in adds)
    flat = [add for arrived in adds for add in arrived]

    def lane_block(height, at=0):
        return pl.BlockSpec((height, cols), lambda i: (at, i))

    heights = [count * total] if joined else [b - a for a, b in zip(splits, splits[1:])] * count
    return pl.pallas_call(
        functools.partial(ff_grad_kernel, ff_half, spans, splits, int(joined)),
        out_shape=tuple(jax.ShapeDtypeStruct((height, width), BF) for height in heights),
        grid=(2,),
        in_specs=[lanes, lanes, column, column] + [lane_block(height, at) for _, height, _, at in flat],
        out_specs=tuple(lane_block(height) for height in heights),
        compiler_params=params(megabytes),
        cost_estimate=cost(1, 1),
        name="ff_grad",
    )(first_low, d_fed, d_upper, hidden, *[array for _, _, array, _ in flat])


def combine_kernel(spans, *refs):
    arrays = list(refs[: sum(map(len, spans))])
    step = pl.program_id(0)
    for result, terms in zip(refs[len(arrays) :], spans):
        total = 0.0
        for low, high in terms:
            term = arrays.pop(0)[...].astype(F32)
            total = total + (term if (low, high) == terms[0] else jnp.where((low <= step) & (step < high), term, 0.0))
        result[...] = total.astype(BF)


def combine(*sums):
    height, width = sums[0][0][1].shape
    split = 4
    rows = height // split
    spans = tuple(tuple((low // rows, (low + array.shape[0]) // rows) for low, array in terms) for terms in sums)

    def row_block(low, high):
        return pl.BlockSpec((rows, width), lambda i: (jnp.clip(i - low, 0, high - low - 1), 0))

    return pl.pallas_call(
        functools.partial(combine_kernel, spans),
        out_shape=tuple(jax.ShapeDtypeStruct((height, width), BF) for _ in sums),
        grid=(split,),
        in_specs=[row_block(*span) for terms in spans for span in terms],
        out_specs=tuple(row_block(0, split) for _ in sums),
        compiler_params=params(60),
        cost_estimate=cost(1, 1),
        name="combine",
    )(*[array for terms in sums for _, array in terms])


def diagonal_kernel(d_ref, w_ref, two_ref, one_ref):
    share = against(d_ref[...], w_ref[...]).astype(BF)
    half = two_ref.shape[0]
    two_ref[...] = share[:half]
    one_ref[...] = share[half:]


def diagonal_share(d_joint, w_seq, parts):
    rows, joint_width = d_joint.shape[0] // parts, d_joint.shape[1]
    width = w_seq.shape[0]
    half = (rows // 2, width)
    return pl.pallas_call(
        diagonal_kernel,
        out_shape=(jax.ShapeDtypeStruct(half, BF),) * 2,
        grid=(1,),
        in_specs=[pl.BlockSpec((rows, joint_width), lambda i: (parts - 1, 0)), whole_block(*w_seq.shape)],
        out_specs=(whole_block(*half),) * 2,
        compiler_params=params(),
        cost_estimate=cost(1, 1),
        name="diagonal_share",
    )(d_joint, w_seq)


def side_kernel(one_ref, two_ref, w_ref, to_two_ref, to_one_ref, via_one_ref, via_two_ref):
    half = to_two_ref.shape[0]
    share = against(one_ref[...], w_ref[...])
    via_one_ref[pl.ds(0, half), :] = (share[:half] + to_two_ref[...].astype(F32)).astype(BF)
    via_one_ref[pl.ds(half, half), :] = share[half:].astype(BF)
    share = against(two_ref[...], w_ref[...])
    via_two_ref[pl.ds(0, half), :] = share[:half].astype(BF)
    via_two_ref[pl.ds(half, half), :] = (share[half:] + to_one_ref[...].astype(F32)).astype(BF)


def side_shares(d_joint, w_seq, to_two, to_one, parts):
    rows, joint_width = d_joint.shape[0] // parts, d_joint.shape[1]
    width = w_seq.shape[0]
    return pl.pallas_call(
        side_kernel,
        out_shape=(jax.ShapeDtypeStruct((rows, width), BF),) * 2,
        grid=(1,),
        in_specs=[
            pl.BlockSpec((rows, joint_width), lambda i: (1, 0)),
            pl.BlockSpec((rows, joint_width), lambda i: (2, 0)),
            whole_block(*w_seq.shape),
            whole_block(*to_two.shape),
            whole_block(*to_one.shape),
        ],
        out_specs=(whole_block(rows, width),) * 2,
        compiler_params=params(),
        cost_estimate=cost(1, 1),
        name="side_shares",
    )(d_joint, d_joint, w_seq, to_two, to_one)


def row_grad_kernel(micros, keep_ref, d_pre_ref, w_ref, *refs):
    joints, arrived, out_ref = refs[:micros], refs[micros:-1], refs[-1]
    for m in range(micros):

        @pl.when(pl.program_id(0) == m)
        def _(m=m):
            total = d_pre_ref[...] + against(joints[m][...], w_ref[...])
            total = total + arrived[2 * m][...].astype(F32) + arrived[2 * m + 1][...].astype(F32)
            out_ref[...] = jnp.where(keep_ref[:, 0:1] > 0.0, total, 0.0)


def row_grad(keep, d_pre, w_seq, d_joints, arrived, parts):
    micros = len(d_joints)
    rows, joint_width = d_joints[0].shape[0] // parts, d_joints[0].shape[1]
    width = w_seq.shape[0]
    block = pl.BlockSpec((rows, width), lambda i: (i, 0))
    return pl.pallas_call(
        functools.partial(row_grad_kernel, micros),
        out_shape=jax.ShapeDtypeStruct(d_pre.shape, F32),
        grid=(micros,),
        in_specs=[pl.BlockSpec((rows, 128), lambda i: (i, 0)), block, whole_block(*w_seq.shape)]
        + [whole_block(rows, joint_width)] * micros
        + [whole_block(rows, width)] * (2 * micros),
        out_specs=block,
        compiler_params=params(60),
        cost_estimate=cost(1, 1),
        name="row_grad",
    )(keep, d_pre, w_seq, *d_joints, *[a for pair in arrived for a in pair])


def shards(
    embedded,
    token_table,
    masked_pos,
    replace_ids,
    w_query,
    b_query,
    w_key,
    w_value,
    b_value,
    w_out,
    b_out,
    ln1_gain,
    ln1_bias,
    w_up,
    b_up,
    w_down,
    b_down,
    ln2_gain,
    ln2_bias,
    grad_masked,
):
    rank = lax.axis_index("tensor")
    count = lax.axis_size("tensor")
    dp_count = lax.axis_size("dp")
    core = lax.axis_index("dp") % 2
    micro_count, row_count, width = embedded.shape
    local_width = w_query.shape[1]
    ff_local = w_up.shape[1]
    vocab_count = token_table.shape[0]
    parts = LEN // row_count
    groups = count // parts
    part = rank % parts
    group = rank // parts
    part_width = width // parts
    pairs = part_width // PAIR
    half_count = row_count // 2
    half_rows = width // 2
    ff_half = ff_local // 2
    out_half = local_width // 2
    cut = ff_half + PAD
    own_first = core == 0
    micros = range(micro_count)

    def by_core(mine, other, axis=0):
        return jnp.where(
            own_first,
            jnp.concatenate([mine, other], axis=axis),
            jnp.concatenate([other, mine], axis=axis),
        )

    order = list(range(0, count, 2)) + list(range(count - 1, 0, -2))
    ring_fw = [(order[i], order[(i + 1) % count]) for i in range(count)]
    ring_bw = [(b, a) for a, b in ring_fw]
    far = count // 2
    ring_pos = jnp.where(rank % 2 == 0, rank // 2, count - 1 - rank // 2)
    offsets = [0] + [sign * s for s in range(1, far) for sign in (-1, 1)] + [far]

    def forward(values):
        return lax.ppermute(values, "tensor", ring_fw)

    def backward(values):
        return lax.ppermute(values, "tensor", ring_bw)

    part_order = jnp.stack([part ^ j for j in range(parts)]).astype(jnp.int32)

    slot_pos = lax.dynamic_index_in_dim(masked_pos, group, 1, keepdims=False)
    slot_ids = lax.dynamic_index_in_dim(replace_ids, group, 1, keepdims=False)
    slot_grads = lax.dynamic_index_in_dim(grad_masked, group, 1, keepdims=False)
    vocab_iota = jnp.arange(vocab_count, dtype=jnp.int32)

    def replacement(positions, step):
        matches = positions[:, None] == slot_pos[step][None, :]
        replaced = jnp.any(matches, axis=1)
        row_ids = jnp.sum(jnp.where(matches, slot_ids[step][None, :], 0), axis=1)
        hot = (row_ids[:, None] == vocab_iota[None, :]) & replaced[:, None]
        return matches, replaced, hot

    row_iota = jnp.arange(row_count, dtype=jnp.int32)
    placed, replaced_list, hots, cots, seq_hots = [], [], [], [], []
    for step in micros:
        matches, replaced, hot = replacement(part * row_count + row_iota, step)
        inserted = product(hot.astype(BF), token_table)
        placed.append(jnp.where(replaced[:, None], inserted, embedded[step].astype(F32)).astype(BF))
        replaced_list.append(replaced)
        hots.append(hot.astype(F32))
        cots.append(product(matches.astype(BF), slot_grads[step]))
        seq_pos = jnp.concatenate([(part ^ j) * row_count + row_iota for j in range(parts)])
        seq_hot = replacement(seq_pos, step)[2].astype(BF)
        seq_hots.append(jnp.concatenate([seq_hot, jnp.ones_like(seq_hot[:, :2])], axis=1))

    joint_half = jnp.concatenate(
        [
            lax.dynamic_slice_in_dim(
                jnp.concatenate([w_query, w_key, w_value], axis=1), core * half_rows, half_rows, 0
            ),
            jnp.pad(
                jnp.concatenate([b_query, jnp.zeros_like(b_query), b_value])[None, :],
                ((0, PAD - 1), (0, 0)),
            ),
        ],
        axis=0,
    )
    spread = [
        [(groups * p + i, p + parts * ((i + k) % groups)) for p in range(parts) for i in range(groups)]
        for k in range(groups)
    ]
    piece = jnp.concatenate(
        [
            lax.dynamic_slice_in_dim(w_up.T, core * ff_half, ff_half, 0),
            jnp.pad(
                lax.dynamic_slice_in_dim(b_up, core * ff_half, ff_half, 0)[None, :],
                ((0, PAD - 1), (0, width - ff_half)),
            ),
            lax.dynamic_slice_in_dim(w_down, core * ff_half, ff_half, 0),
        ],
        axis=0,
    )

    w_mine = [lax.ppermute(joint_half, "tensor", spread[k]) for k in range(groups)]
    ones = [swap(placed[0], "tensor", 1)]
    twos = [swap(placed[0], "tensor", 2)]
    ones, twos, w_mine, placed, piece, cots, w_out = fence(ones, twos, w_mine, placed, piece, cots, w_out)
    w_out_half = lax.all_gather(
        lax.dynamic_slice_in_dim(w_out, core * out_half, out_half, 0), "tensor", axis=0
    )
    w_other = [swap(w, "dp", 1) for w in w_mine]
    w_seq, b_seq = assemble(
        jnp.stack([core] + [(group - i) % groups for i in range(groups)]).astype(jnp.int32),
        w_mine,
        w_other,
        local_width,
    )

    joints, x_mine, x_other, heads, log_sums, own_heads = [], [], [], [], [], []
    near = [piece[:cut], piece[cut:]]
    arrived = []
    at_core = core[None].astype(jnp.int32)
    for step in micros:
        threes = (swap(ones[step][:half_count], "tensor", 2), swap(twos[step][half_count:], "tensor", 1))
        rows = [placed[step], ones[step], twos[step], *threes]
        if step + 1 < micro_count:
            ones.append(swap(placed[step + 1], "tensor", 1))
            twos.append(swap(placed[step + 1], "tensor", 2))
        moved = (forward(near[step]), backward(near[step]))
        joint, mine, other = project(at_core, rows, w_seq, b_seq)
        pieces, sums = attn_forward(joint, parts)
        joints.append(joint)
        log_sums.append(sums)
        own_heads.append(pieces)
        x_mine.append(mine)
        x_other.append(other)
        ones, twos, moved, pieces, near = fence(ones, twos, moved, pieces, near)
        arrived.append(moved)
        heads.append([pieces[0]] + [swap(pieces[j], "tensor", j) for j in range(1, parts)])
    fw, bw = (jnp.concatenate([arrived[0][d], arrived[1][d]], axis=0) for d in range(2))
    heads, fw, bw, w_out_half = fence(heads, fw, bw, w_out_half)
    w_out_other = swap(w_out_half, "dp", 1)
    blocks = [piece, swap(piece, "dp", 1), fw, bw, swap(fw, "dp", 1), swap(bw, "dp", 1)]

    vectors_one = jnp.stack([b_out, ln1_gain, ln1_bias, b_down] + [b_out] * 4).astype(F32)
    heads_out, norm_one, scale_one, pre_two, first_low, w_out_all = attend(
        jnp.concatenate([part_order, at_core]), heads, placed, w_out_half, w_out_other, vectors_one
    )

    step_blocks = [blocks[:2], blocks[2:6]]
    hidden_low, slopes = [None] * (far + 1), [None] * (far + 1)
    for s in range(2, far + 1):
        if s < far:
            moved = [forward(fw), backward(bw)]
        else:
            moved = [jnp.concatenate([forward(fw[:cut]), backward(bw[cut:])], axis=0)]
        for t in (0, 1) if s == 2 else (s - 1,):
            pre_two, hidden_low[t], slopes[t] = ff_forward(first_low, pre_two, step_blocks[t], ff_half)
        if s < far:
            if s < far - 1:
                moved, pre_two = fence(moved, pre_two)
            fw, bw = moved
        step_blocks.append(moved + [swap(block, "dp", 1) for block in moved])
    pre_two, hidden_low[far], slopes[far] = ff_forward(first_low, pre_two, step_blocks[far], ff_half)

    vectors_two = jnp.stack([ln2_gain, ln2_bias] + [ln2_bias] * 6).astype(F32)
    layer_out, d_pre_two, d_fed, sums_two = second_norm(pre_two, jnp.concatenate(cots, axis=0), vectors_two)
    total = 2 * ff_half

    def ff_blocks(offsets_, other, adds=None, cuts=(), megabytes=24):
        s = abs(offsets_[0])
        result = ff_grad(
            d_uppers[s], hidden_low[s], first_low, d_fed, other, adds or [[] for _ in offsets_], ff_half, cuts,
            bool(other), megabytes,
        )
        return result[0] if other else result

    def both(s):
        return [-s, s] if s else [0]

    def summed(s, others, megabytes=24):
        return ff_blocks(both(s), 0, [[(0, total, others, i)] for i in range(len(both(s)))], (), megabytes)

    d_uppers, column_sums_ = [None] * (far + 1), [None] * (far + 1)

    def back(s, d_first):
        d_uppers[s], d_first, sums = ff_backward(d_fed, d_first, slopes[s], step_blocks[s], ff_half)
        column_sums_[s] = sums.reshape(2, -1, ff_half)
        return d_first

    d_first = back(far, d_pre_two)
    others = ff_blocks([far], 1)
    others, d_uppers[far], d_first = fence(others, d_uppers[far], d_first)
    others = swap(others, "dp", 1)
    d_first = back(far - 1, d_first)
    others, d_uppers[far], d_first = fence(others, d_uppers[far], d_first)
    parcel = ff_blocks([far], 0, [[(0, total, others, 0)]], (ff_half,))
    next_others = ff_blocks(both(far - 1), 1)
    parcel, next_others, d_uppers[far - 1], d_first = fence(parcel, next_others, d_uppers[far - 1], d_first)
    moved = [forward(parcel[0]), backward(parcel[1])]
    others = swap(next_others, "dp", 1)
    for s in range(far - 2, -1, -1):
        d_first = back(s, d_first)
    rel_b_up = jnp.concatenate(column_sums_, axis=1)
    d_pre_one, d_attended, sums_one, *d_heads = attend_back(
        part_order, d_first, norm_one, scale_one, vectors_one, w_out_all, parts
    )
    others, d_uppers[far - 1], d_heads = fence(others, d_uppers[far - 1], d_heads)
    seq_grads = [d_heads[0]] + [swap(d_heads[j], "tensor", j) for j in range(1, parts)]
    share = summed(far - 1, others)
    next_others = ff_blocks(both(far - 2), 1)

    d_out = over_rows(heads_out, d_attended).astype(BF).reshape(count, 2, out_half, width)
    out_other = lax.dynamic_index_in_dim(d_out, 1 - core, 1, keepdims=False).reshape(-1, width)
    out_mine = lax.dynamic_index_in_dim(d_out, core, 1, keepdims=False).reshape(-1, width)
    moved, share, seq_grads, next_others, out_other = fence(moved, share, seq_grads, next_others, out_other)
    parcel = combine([(0, share[0]), (ff_half, moved[1])], [(0, share[1]), (0, moved[0])])
    parcel, next_others, seq_grads, out_other = fence(parcel, next_others, seq_grads, out_other)

    d_joints = [jnp.zeros((), BF) for _ in micros]
    work = [(m, g) for m in micros for g in range(pairs)]

    def over_dp(values):
        bit = 2
        while bit < dp_count:
            values = (values.astype(F32) + swap(values, "dp", bit).astype(F32)).astype(BF)
            bit *= 2
        return values

    def diagonal(step):
        to_two, to_one = diagonal_share(d_joints[step], w_seq, parts)
        return (swap(to_two, "tensor", 2), swap(to_one, "tensor", 1))

    def side_parcels(step, arrived):
        return side_shares(d_joints[step], w_seq, *arrived, parts)

    def sides(parcels):
        return (swap(parcels[0], "tensor", 1), swap(parcels[1], "tensor", 2))

    def own_table(d_rows):
        return lax.dot_general(
            jnp.concatenate(hots, axis=0),
            d_rows,
            ROWS_DIMS,
            precision=lax.Precision.HIGHEST,
            preferred_element_type=F32,
        )

    partial, stage = [() for _ in micros], [0 for _ in micros]
    d_w = []
    table = own_table(d_pre_one)
    plan = [[pair] for pair in work[:-pairs]] + [work[-pairs:]]
    for index in range(far - 1):
        s = far - 1 - index
        if index:
            parcel = combine([(0, share[0]), (0, moved[1])], [(0, share[1]), (0, moved[0])])
        joints, d_joints, d_fed, parcel, next_others = fence(joints, d_joints, d_fed, parcel, next_others)
        moved = [forward(parcel[1]), backward(parcel[0])]
        others = swap(next_others, "dp", 1)
        if index == 0:
            out_mine = (out_mine.astype(F32) + swap(out_other, "dp", 1).astype(F32)).astype(BF)
            out_sum = lax.psum_scatter(out_mine, "tensor", scatter_dimension=0, tiled=True)
        for m in micros:
            ready = max(i for i, pairs_ in enumerate(plan) if (m, pairs - 1) in pairs_) + 1
            if index == ready:
                partial[m], stage[m] = diagonal(m), 1
            elif index == ready + 1:
                partial[m], stage[m] = side_parcels(m, partial[m]), 2
        if index == len(plan) - 1:
            d_w = [(over_rows(x_other[m], d_joints[m]), over_rows(x_mine[m], d_joints[m])) for m in micros[:-1]]
        next_others = ()
        if s > 1:
            next_others = ff_blocks(both(s - 2), 1, megabytes=60)
        for m, g in plan[index] if index < len(plan) else ():
            d_joints[m] = attn_backward(
                joints[m], log_sums[m], seq_grads, own_heads[m], m, g, (d_joints[m],) if g else ()
            )
        share = summed(s - 1, others, 60)
        moved, share, next_others, d_joints, partial, table, d_w = fence(
            moved, share, next_others, d_joints, partial, table, d_w
        )

    last = micro_count - 1
    parcel = combine([(0, share[0]), (0, moved[0]), (0, moved[1])])[0]
    ff_up, ff_down = parcel[:ff_half], parcel[ff_half:]
    for m in micros:
        if stage[m] == 1:
            partial[m], stage[m] = side_parcels(m, partial[m]), 2
    d_w.append((over_rows(x_other[last], d_joints[last]), None))
    other_half = sum(other for other, _ in d_w).astype(BF)
    other_half, d_joints, partial, ff_up, ff_down = fence(other_half, d_joints, partial, ff_up, ff_down)
    other_half = swap(other_half, "dp", 1)
    ff_up = over_dp(ff_up)
    for m in micros:
        if stage[m] == 2:
            partial[m], stage[m] = sides(partial[m]), 4
        else:
            partial[m] = diagonal(m)

    def over_bits(values, axis, low, high):
        while low < high:
            bits = (low, 2 * low, 3 * low) if 2 * low < high else (low,)
            sent = values.astype(BF)
            terms = [sent.astype(F32)] + [swap(sent, axis, bit).astype(F32) for bit in bits]
            while len(terms) > 1:
                terms = [a + b for a, b in zip(terms[::2], terms[1::2])]
            values = terms[0]
            low *= 4
        return values

    rel_b_up = jnp.swapaxes(rel_b_up, 0, 1)
    rel_b_up = jnp.where(own_first, rel_b_up, rel_b_up[:, ::-1]).reshape(count, ff_local)
    slot_of = [0] * count
    for slot, o in enumerate(offsets):
        slot_of[o % count] = slot
    place = jnp.array([order.index(s) for s in range(count)], jnp.int32)
    wanted = jnp.array(slot_of, jnp.int32)[(place - ring_pos) % count]
    all_b_up = rel_b_up[wanted].reshape(-1, width)
    b_rows = all_b_up.shape[0]
    hot_sum = sum(over_rows(seq_hots[m], d_joints[m]) for m in micros)
    d_b_seq = hot_sum[vocab_count]
    rest, thirds = hot_sum, []
    for _ in range(3):
        thirds.append(rest.astype(BF))
        rest = rest - thirds[-1].astype(F32)
    table_rows = hot_sum.shape[0]
    shares = against(jnp.concatenate(thirds, axis=0), w_seq).reshape(3, table_rows, width)
    table = jnp.pad(table, ((0, table_rows - vocab_count), (0, 0))) + ((shares[2] + shares[1]) + shares[0])
    empty = jnp.zeros((width,), F32)
    d_b_query, d_b_value = (
        lax.dynamic_update_slice_in_dim(
            empty,
            jnp.concatenate([d_b_seq[(3 * g + a) * PAIR : (3 * g + a + 1) * PAIR] for g in range(pairs)]),
            part * part_width,
            0,
        )
        for a in (0, 2)
    )
    place_row = lax.broadcasted_iota(jnp.int32, table.shape, 0)
    table = jnp.where(place_row == vocab_count, d_b_query[None], table)
    table = jnp.where(place_row == vocab_count + 1, d_b_value[None], table)
    small = jnp.concatenate([table, sums_one, sums_two, jnp.pad(all_b_up, ((0, -b_rows % 8), (0, 0)))], axis=0)

    my_half = sum(mine for _, mine in d_w[: len(d_w)] if mine is not None)
    my_half = my_half + sum(over_rows(x_mine[m], d_joints[m]) for m in micros if d_w[m][1] is None)
    my_half = (my_half + other_half.astype(F32)).astype(BF)
    my_half, small, partial, ff_up, ff_down = fence(my_half, small, partial, ff_up, ff_down)

    if local_width != PAIR:
        columns = [
            jnp.concatenate(
                [my_half[:, (3 * g + a) * PAIR : (3 * g + a + 1) * PAIR] for g in range(pairs)], axis=1
            )
            for a in range(3)
        ]
        my_half = jnp.concatenate(
            [c[:, i * local_width : (i + 1) * local_width] for i in range(groups) for c in columns], axis=1
        )
    joint_sum = sum(
        lax.ppermute(
            lax.dynamic_slice_in_dim(
                my_half, (group - k) % groups * 3 * local_width, 3 * local_width, 1
            ),
            "tensor",
            [(b, a) for a, b in spread[k]],
        ).astype(F32)
        for k in range(groups)
    ).astype(BF)
    small = over_bits(small, "dp", 1, dp_count)
    ff_down = over_dp(ff_down)
    out_sum = over_dp(out_sum)
    if stage[last] < 4:
        partial[last] = side_parcels(last, partial[last])
    joint_sum, small, ff_up, ff_down, out_sum, partial = fence(
        joint_sum, small, ff_up, ff_down, out_sum, partial
    )

    joint_sum = over_dp(joint_sum)
    ff_other = swap(jnp.concatenate([ff_up, ff_down, out_sum], axis=0), "dp", 1)
    if stage[last] < 4:
        partial[last] = sides(partial[last])
    small = over_bits(small, "tensor", 1, min(4, count))
    grad_w_up = by_core(ff_up, ff_other[:ff_half]).astype(F32).T
    grad_w_down = by_core(ff_down, ff_other[ff_half : 2 * ff_half]).astype(F32)
    grad_w_out = by_core(out_sum, ff_other[2 * ff_half :]).astype(F32)
    joint_sum, small, partial, grad_w_up, grad_w_down, grad_w_out = fence(
        joint_sum, small, partial, grad_w_up, grad_w_down, grad_w_out
    )
    joint_other = swap(joint_sum, "dp", 1)
    small = over_bits(small, "tensor", 4, count)
    keep = 1.0 - jnp.concatenate(replaced_list).astype(F32)
    grad_rows = row_grad(
        jnp.broadcast_to(keep[:, None], (keep.shape[0], 128)), d_pre_one, w_seq, d_joints, partial, parts
    )
    grad_joint = by_core(joint_sum, joint_other).astype(F32)
    grad_b_query, grad_b_value = (
        lax.dynamic_slice_in_dim(small[vocab_count + i], rank * local_width, local_width, 0) for i in range(2)
    )
    sums_at = (table_rows, table_rows + 8)
    grad_b_out, grad_gone, grad_bone, grad_b_down, grad_gtwo, grad_btwo = (
        small[at + i] for at in sums_at for i in range(3)
    )
    all_b_up = small[table_rows + 16 : table_rows + 16 + b_rows]
    grad_b_up = lax.dynamic_slice_in_dim(all_b_up.reshape(-1), rank * ff_local, ff_local, 0)

    return (
        layer_out.reshape(micro_count, row_count, width),
        grad_rows.reshape(micro_count, row_count, width),
        small[:vocab_count],
        grad_joint[:, :local_width],
        grad_b_query,
        grad_joint[:, local_width : 2 * local_width],
        grad_joint[:, 2 * local_width :],
        grad_b_value,
        grad_w_out,
        grad_b_out,
        grad_gone,
        grad_bone,
        grad_w_up,
        grad_b_up,
        grad_w_down,
        grad_b_down,
        grad_gtwo,
        grad_btwo,
    )


def solution(mesh):
    return jax.shard_map(
        shards,
        mesh=mesh,
        in_specs=(
            P(None, ("dp", "tensor"), None),
            P(),
            P(None, "dp", None),
            P(None, "dp", None),
            P(None, "tensor"),
            P("tensor"),
            P(None, "tensor"),
            P(None, "tensor"),
            P("tensor"),
            P("tensor", None),
            P(),
            P(),
            P(),
            P(None, "tensor"),
            P("tensor"),
            P("tensor", None),
            P(),
            P(),
            P(),
            P(None, "dp", None, None),
        ),
        out_specs=(
            P(None, ("dp", "tensor"), None),
            P(None, ("dp", "tensor"), None),
            P(),
            P(None, "tensor"),
            P("tensor"),
            P(None, "tensor"),
            P(None, "tensor"),
            P("tensor"),
            P("tensor", None),
            P(),
            P(),
            P(),
            P(None, "tensor"),
            P("tensor"),
            P("tensor", None),
            P(),
            P(),
            P(),
        ),
        check_vma=False,
    )
```

```python
import functools

import jax
import jax.numpy as jnp
from jax import lax
from jax.experimental import pallas as pl
from jax.experimental.pallas import tpu as pltpu
from jax.sharding import PartitionSpec as P

HD = 64
LEN = 1024
EPSILON = 1e-12
SCALE = HD ** (-0.5)
ROWS_DIMS = (((0,), (0,)), ((), ()))
LAST_DIMS = (((1,), (1,)), ((), ()))
BF = jnp.bfloat16
F32 = jnp.float32
PAD = 16
PAIR = 2 * HD
LOG2E = 1.4426950408889634


def product(left_mat, right_mat):
    return jnp.dot(left_mat, right_mat, preferred_element_type=F32)


def over_rows(left_mat, right_mat):
    return lax.dot_general(left_mat, right_mat, ROWS_DIMS, preferred_element_type=F32)


def against(left_mat, right_mat):
    return lax.dot_general(left_mat, right_mat, LAST_DIMS, preferred_element_type=F32)


def swap(values, axis, bit):
    count = lax.axis_size(axis)
    return lax.ppermute(values, axis, [(i, i ^ bit) for i in range(count)])


def fence(*trees):
    return lax.optimization_barrier(trees)


def whole_block(*shape):
    return pl.BlockSpec(shape, lambda *_: (0,) * len(shape))


def params(megabytes=24):
    return pltpu.CompilerParams(vmem_limit_bytes=megabytes * 1024 * 1024)


def cost(flops, nbytes, transcendentals=0):
    return pl.CostEstimate(flops=flops, bytes_accessed=nbytes, transcendentals=transcendentals)


def assemble_kernel(groups, local, half, at_ref, *refs):
    mines, others = refs[:groups], refs[groups : 2 * groups]
    w_ref, b_ref = refs[2 * groups :]
    for i in range(groups):
        for k in range(groups):

            @pl.when(at_ref[1 + i] == k)
            def _(i=i, k=k):
                for a in range(3):
                    source = pl.ds(a * local, local)
                    lane = (3 * (i * local // PAIR) + a) * PAIR + i * local % PAIR
                    target = pl.ds(lane, local)
                    top = pl.multiple_of(at_ref[0] * half, half)
                    low = pl.multiple_of((1 - at_ref[0]) * half, half)
                    w_ref[pl.ds(top, half), target] = mines[k][pl.ds(0, half), source]
                    w_ref[pl.ds(low, half), target] = others[k][pl.ds(0, half), source]
                    b_ref[:, target] = mines[k][pl.ds(half, PAD), source][0:1].astype(F32)


def assemble(at, mines, others, local):
    groups = len(mines)
    half, width3 = others[0].shape[0] - PAD, others[0].shape[1]
    return pl.pallas_call(
        functools.partial(assemble_kernel, groups, local, half),
        out_shape=(
            jax.ShapeDtypeStruct((2 * half, groups * width3), BF),
            jax.ShapeDtypeStruct((1, groups * width3), F32),
        ),
        grid_spec=pltpu.PrefetchScalarGridSpec(
            num_scalar_prefetch=1,
            grid=(1,),
            in_specs=[whole_block(*m.shape) for m in (*mines, *others)],
            out_specs=(whole_block(2 * half, groups * width3), whole_block(1, groups * width3)),
        ),
        compiler_params=params(),
        cost_estimate=cost(0, 8 * half * groups * width3),
        name="assemble",
    )(at, *mines, *others)


def project_kernel(parts, at_ref, *refs):
    pieces = refs[: parts + 1]
    w_ref, b_ref, joint_ref, mine_ref, other_ref, x_ref = refs[parts + 1 :]
    step = pl.program_id(0)
    for j in range(parts - 1):

        @pl.when(step == j)
        def _(j=j):
            x_ref[...] = pieces[j][...]

    @pl.when(step == parts - 1)
    def _():
        rows = pieces[-1].shape[0]
        x_ref[pl.ds(0, rows), :] = pieces[-2][...]
        x_ref[pl.ds(rows, rows), :] = pieces[-1][...]

    joint_ref[...] = (product(x_ref[...], w_ref[...]) + b_ref[...]).astype(BF)
    half = mine_ref.shape[1]
    mine_ref[...] = x_ref[:, pl.ds(pl.multiple_of(at_ref[0] * half, half), half)]
    other_ref[...] = x_ref[:, pl.ds(pl.multiple_of((1 - at_ref[0]) * half, half), half)]


def project(at, pieces, w_seq, b_seq):
    parts = len(pieces) - 1
    rows, width = pieces[0].shape
    joint_width = w_seq.shape[1]
    half = jax.ShapeDtypeStruct((parts * rows, width // 2), BF)
    half_block = pl.BlockSpec((rows, width // 2), lambda i, s: (i, 0))
    return pl.pallas_call(
        functools.partial(project_kernel, parts),
        out_shape=(jax.ShapeDtypeStruct((parts * rows, joint_width), BF), half, half),
        grid_spec=pltpu.PrefetchScalarGridSpec(
            num_scalar_prefetch=1,
            grid=(parts,),
            in_specs=[whole_block(*p.shape) for p in pieces]
            + [whole_block(*w_seq.shape), whole_block(*b_seq.shape)],
            out_specs=(pl.BlockSpec((rows, joint_width), lambda i, s: (i, 0)), half_block, half_block),
            scratch_shapes=[pltpu.VMEM((rows, width), BF)],
        ),
        compiler_params=params(),
        cost_estimate=cost(2 * parts * rows * width * joint_width, 12 * parts * rows * width),
        name="project",
    )(at, *pieces, w_seq, b_seq)


def first_head(rows):
    return lax.broadcasted_iota(jnp.int32, (rows, PAIR), 1) < HD


def one_head(values, head, fill=0.0):
    first = first_head(values.shape[0])
    filled = jnp.full(values.shape, fill, values.dtype)
    return jnp.where(first, filled, values) if head else jnp.where(first, values, filled)


def attn_forward_kernel(q_ref, k_ref, v_ref, *refs):
    outs, all_ref, log_ref = refs[:-2], refs[-2], refs[-1]
    rows = q_ref.shape[0]
    mixed, log_sums = [], []
    scores = [against(one_head(q_ref[...], head), k_ref[...]) for head in range(2)]
    tops = [jnp.max(score, axis=-1, keepdims=True) * (SCALE * LOG2E) for score in scores]
    weights = [jnp.exp2(score * (SCALE * LOG2E) - top).astype(BF) for score, top in zip(scores, tops)]
    for head in range(2):
        both = product(weights[head], one_head(v_ref[...], head, 1.0))
        total = pltpu.roll(both, HD, 1)
        mixed.append(both / total)
        log_sums.append(tops[head] + jnp.log(total) * LOG2E)
    first = first_head(rows)
    value = jnp.where(first, mixed[0], mixed[1]).astype(BF)
    turned = jnp.where(first, log_sums[0], log_sums[1]).T
    log_ref[0, 0:1, :] = turned[0:1]
    log_ref[0, 1:2, :] = turned[HD : HD + 1]
    all_ref[...] = value
    for j, out in enumerate(outs):

        @pl.when(pl.program_id(1) == j)
        def _(out=out):
            out[...] = value


def attn_forward(joint, parts):
    rows = joint.shape[0] // parts
    pairs = joint.shape[1] // (3 * PAIR)
    shape = jax.ShapeDtypeStruct((rows, pairs * PAIR), BF)
    result = pl.pallas_call(
        attn_forward_kernel,
        out_shape=(shape,) * parts
        + (
            jax.ShapeDtypeStruct((parts * rows, pairs * PAIR), BF),
            jax.ShapeDtypeStruct((pairs, 8, parts * rows), F32),
        ),
        grid=(pairs, parts),
        in_specs=[
            pl.BlockSpec((rows, PAIR), lambda g, i: (i, 3 * g)),
            pl.BlockSpec((parts * rows, PAIR), lambda g, i: (0, 3 * g + 1)),
            pl.BlockSpec((parts * rows, PAIR), lambda g, i: (0, 3 * g + 2)),
        ],
        out_specs=(pl.BlockSpec((rows, PAIR), lambda g, i: (0, g)),) * parts
        + (pl.BlockSpec((rows, PAIR), lambda g, i: (i, g)), pl.BlockSpec((1, 8, rows), lambda g, i: (g, 0, i))),
        compiler_params=params(),
        cost_estimate=cost(
            16 * joint.shape[0] ** 2 * pairs * PAIR, 3 * joint.size, 2 * pairs * joint.shape[0] ** 2
        ),
        name="attn_forward",
    )(joint, joint, joint)
    return result[:parts], result[parts], result[parts + 1]


def attn_backward_kernel(parts, q_ref, k_ref, v_ref, log_ref, g_ref, o_ref, *refs):
    d_ref, kt_ref, dk_acc, dv_acc = refs[-4:]
    step = pl.program_id(0)
    rows = q_ref.shape[0]

    @pl.when(step == 0)
    def _():
        kt_ref[...] = k_ref[...].T
        dk_acc[...] = jnp.zeros_like(dk_acc)
        dv_acc[...] = jnp.zeros_like(dv_acc)

    row_dots = (g_ref[...].astype(F32) * o_ref[...].astype(F32)).T
    dq_parts = []
    for head in range(2):
        queries = one_head(q_ref[...], head)
        grads = one_head(g_ref[...], head)
        row_dot = jnp.sum(row_dots[head * HD : (head + 1) * HD], axis=0, keepdims=True)
        log_sum = log_ref[0, pl.ds(head, 1), :]
        scores = against(k_ref[...], queries)
        probs = jnp.exp2(scores * (SCALE * LOG2E) - log_sum)
        d_probs = against(v_ref[...], grads)
        d_scores = (probs * (d_probs - row_dot)).astype(BF)
        dv_acc[...] += product(probs.astype(BF), grads)
        dk_acc[...] += product(d_scores, queries)
        dq_parts.append(product(kt_ref[pl.ds(head * HD, HD), :], d_scores))
    d_ref[pl.ds(step * rows, rows), pl.ds(0, PAIR)] = (
        jnp.concatenate(dq_parts, axis=0).T * SCALE
    ).astype(BF)

    @pl.when(step == parts - 1)
    def _():
        d_ref[:, pl.ds(PAIR, PAIR)] = (dk_acc[...] * SCALE).astype(BF)
        d_ref[:, pl.ds(2 * PAIR, PAIR)] = dv_acc[...].astype(BF)


def attn_backward(joint, log_sums, grads, heads, parts, step, micros, pair, kept):
    rows = joint.shape[0] // parts
    return pl.pallas_call(
        functools.partial(attn_backward_kernel, parts),
        out_shape=jax.ShapeDtypeStruct(joint.shape, BF),
        grid=(parts,),
        in_specs=[
            pl.BlockSpec((rows, PAIR), lambda i: (i, 3 * pair)),
            pl.BlockSpec((parts * rows, PAIR), lambda i: (0, 3 * pair + 1)),
            pl.BlockSpec((parts * rows, PAIR), lambda i: (0, 3 * pair + 2)),
            pl.BlockSpec((1, 8, rows), lambda i: (pair, 0, i)),
            pl.BlockSpec((rows, PAIR), lambda i: (i * micros + step, pair)),
            pl.BlockSpec((rows, PAIR), lambda i: (i, pair)),
        ]
        + [pl.BlockSpec(memory_space=pl.ANY)] * len(kept),
        out_specs=pl.BlockSpec((parts * rows, 3 * PAIR), lambda i: (0, pair)),
        scratch_shapes=[
            pltpu.VMEM((PAIR, parts * rows), BF),
            pltpu.VMEM((parts * rows, PAIR), F32),
            pltpu.VMEM((parts * rows, PAIR), F32),
        ],
        input_output_aliases={6 + i: i for i in range(len(kept))},
        compiler_params=params(),
        cost_estimate=cost(1, 1),
        name="attn_backward",
    )(joint, joint, joint, log_sums, grads, heads, *kept)


def normed(values):
    row_mean = jnp.mean(values, axis=-1, keepdims=True)
    centred = values - row_mean
    row_var = jnp.mean(centred * centred, axis=-1, keepdims=True)
    scale = lax.rsqrt(row_var + EPSILON)
    return centred * scale, scale


def norm_backward(norm, scale, gain_vec, grads):
    d_norm = grads * gain_vec
    mean_d = jnp.mean(d_norm, axis=-1, keepdims=True)
    mean_dn = jnp.mean(d_norm * norm, axis=-1, keepdims=True)
    return (d_norm - mean_d - norm * mean_dn) * scale


def column_sums(sums_ref, *values):
    @pl.when(pl.program_id(0) == 0)
    def _():
        sums_ref[...] = jnp.zeros_like(sums_ref)

    for index, value in enumerate(values):
        sums_ref[pl.ds(index, 1), :] += jnp.sum(value, axis=0, keepdims=True)


def attend_kernel(micros, parts, at_ref, *refs):
    pieces, placed = refs[: micros * parts], refs[micros * parts : micros * (parts + 1)]
    mine_ref, other_ref, vec_ref, heads_ref, norm_ref, scale_ref, first_ref, low_ref, w_ref = refs[
        micros * (parts + 1) :
    ]

    @pl.when(pl.program_id(0) == 0)
    def _():
        shards_, rows = mine_ref.shape[:2]
        for shard in range(shards_):
            for half, core in ((mine_ref, at_ref[parts]), (other_ref, 1 - at_ref[parts])):
                row = pl.multiple_of((2 * shard + core) * rows, rows)
                w_ref[pl.ds(row, rows), :] = half[shard]

    for m in range(micros):

        @pl.when(pl.program_id(0) == m)
        def _(m=m):
            total = placed[m][...].astype(F32) + vec_ref[0:1, :]
            for j in range(parts):
                piece = pieces[m * parts + j][...]
                cols = piece.shape[1]
                at = pl.multiple_of(at_ref[j] * cols, cols)
                total = total + product(piece, w_ref[pl.ds(at, cols), :])
                heads_ref[:, pl.ds(at, cols)] = piece
            norm, scale = normed(total)
            first = norm * vec_ref[1:2, :] + vec_ref[2:3, :]
            norm_ref[...] = norm
            scale_ref[...] = jnp.broadcast_to(scale, scale_ref.shape)
            first_ref[...] = first + vec_ref[3:4, :]
            low_ref[...] = first.astype(BF)


def attend(at, pieces, placed, w_mine, w_other, vectors):
    micros, parts = len(pieces), len(pieces[0])
    rows, width = placed[0].shape
    flat = [p for group in pieces for p in group]

    def out(cols, dtype):
        return jax.ShapeDtypeStruct((micros * rows, cols), dtype)

    return pl.pallas_call(
        functools.partial(attend_kernel, micros, parts),
        out_shape=(
            out(width, BF),
            out(width, F32),
            out(128, F32),
            out(width, F32),
            out(width, BF),
            jax.ShapeDtypeStruct((width, width), BF),
        ),
        grid_spec=pltpu.PrefetchScalarGridSpec(
            num_scalar_prefetch=1,
            grid=(micros,),
            in_specs=[whole_block(*a.shape) for a in (*flat, *placed, w_mine, w_other, vectors)],
            out_specs=tuple(
                pl.BlockSpec((rows, cols), lambda i, s: (i, 0)) for cols in (width, width, 128, width, width)
            )
            + (whole_block(width, width),),
        ),
        compiler_params=params(60),
        cost_estimate=cost(2 * micros * rows * width * width, 20 * micros * rows * width),
        name="attend",
    )(at, *flat, *placed, w_mine, w_other, vectors)


def second_norm_kernel(pre_ref, cot_ref, vec_ref, out_ref, d_ref, low_ref, sums_ref):
    norm, scale = normed(pre_ref[...])
    cot = cot_ref[...]
    out_ref[...] = (norm * vec_ref[0:1, :] + vec_ref[1:2, :]).astype(BF)
    d_pre = norm_backward(norm, scale, vec_ref[0:1, :], cot)
    d_ref[...] = d_pre
    low_ref[...] = d_pre.astype(BF)
    column_sums(sums_ref, d_pre, cot * norm, cot)


def second_norm(pre, cot, vectors):
    rows, width = pre.shape
    block = pl.BlockSpec((128, width), lambda i: (i, 0))
    return pl.pallas_call(
        second_norm_kernel,
        out_shape=(
            jax.ShapeDtypeStruct((rows, width), BF),
            jax.ShapeDtypeStruct((rows, width), F32),
            jax.ShapeDtypeStruct((rows, width), BF),
            jax.ShapeDtypeStruct((8, width), F32),
        ),
        grid=(rows // 128,),
        in_specs=[block, block, whole_block(*vectors.shape)],
        out_specs=(block, block, block, whole_block(8, width)),
        compiler_params=params(),
        cost_estimate=cost(30 * rows * width, 16 * rows * width),
        name="second_norm",
    )(pre, cot, vectors)


def attend_back_kernel(parts, at_ref, d_first_ref, norm_ref, scale_ref, vec_ref, w_ref, *refs):
    d_ref, low_ref, sums_ref = refs[:3]
    outs, low_all = refs[3:-1], refs[-1]
    d_first, norm = d_first_ref[...], norm_ref[...]
    d_pre = norm_backward(norm, scale_ref[:, 0:1], vec_ref[1:2, :], d_first)
    low = d_pre.astype(BF)
    d_ref[...] = d_pre
    low_ref[...] = low
    column_sums(sums_ref, d_pre, d_first * norm, d_first)
    rows = low.shape[0]
    step = pl.program_id(0)
    low_all[pl.ds(pl.multiple_of(step * rows, rows), rows), :] = low

    @pl.when(step == pl.num_programs(0) - 1)
    def _():
        for j in range(parts):
            cols = outs[j].shape[1]
            at = pl.multiple_of(at_ref[j] * cols, cols)
            outs[j][...] = against(low_all[...], w_ref[pl.ds(at, cols), :]).astype(BF)


def attend_back(at, d_first, norm, scale, vectors, w_out, parts):
    rows, width = d_first.shape
    split = 4
    block = pl.BlockSpec((rows // split, width), lambda i, s: (i, 0))
    piece = (rows, width // parts)
    return pl.pallas_call(
        functools.partial(attend_back_kernel, parts),
        out_shape=(
            jax.ShapeDtypeStruct((rows, width), F32),
            jax.ShapeDtypeStruct((rows, width), BF),
            jax.ShapeDtypeStruct((8, width), F32),
        )
        + (jax.ShapeDtypeStruct(piece, BF),) * parts,
        grid_spec=pltpu.PrefetchScalarGridSpec(
            num_scalar_prefetch=1,
            grid=(split,),
            in_specs=[
                block,
                block,
                pl.BlockSpec((rows // split, 128), lambda i, s: (i, 0)),
                whole_block(*vectors.shape),
                whole_block(*w_out.shape),
            ],
            out_specs=(block, block, whole_block(8, width)) + (whole_block(*piece),) * parts,
            scratch_shapes=[pltpu.VMEM((rows, width), BF)],
        ),
        compiler_params=params(),
        cost_estimate=cost(2 * rows * width * width, 20 * rows * width),
        name="attend_back",
    )(at, d_first, norm, scale, vectors, w_out)


def next_blocks(blocks, buf, sem):
    step = pl.program_id(0)

    def start(index, slot):
        for h in range(2):
            pltpu.make_async_copy(blocks[2 * index + h], buf.at[slot, h], sem.at[slot, h]).start()

    @pl.when(step == 0)
    def _():
        start(0, 0)

    for index in range(1, len(blocks) // 2):

        @pl.when(step + 1 == index)
        def _(index=index):
            start(index, index % 2)

    slot = step % 2
    for h in range(2):
        pltpu.make_async_copy(blocks[0], buf.at[slot, h], sem.at[slot, h]).wait()
    return [buf.at[slot, h] for h in range(2)]


def upper_tail(size, falling):
    t = 1.0 / (1.0 + (0.3275911 * 0.5**0.5) * size)
    series = 0.5 * 1.061405429 * t - 0.5 * 1.453152027
    series = series * t + 0.5 * 1.421413741
    series = series * t - 0.5 * 0.284496736
    series = series * t + 0.5 * 0.254829592
    return series * t * falling


def ff_forward_kernel(ff_half, count, first_ref, init_ref, *refs):
    sum_ref, hidden_ref, slope_ref, buf, sem = refs[-5:]
    cut = ff_half + PAD

    @pl.when(pl.program_id(0) == 0)
    def _():
        sum_ref[...] = init_ref[...]

    total = 0.0
    for h, block in enumerate(next_blocks(refs[:count], buf, sem)):
        bias = block[pl.ds(ff_half, PAD), pl.ds(0, ff_half)][0:1].astype(F32)
        upper = against(first_ref[...], block[pl.ds(0, ff_half), :]) + bias
        falling = jnp.exp(-0.5 * upper * upper)
        tail = upper_tail(jnp.abs(upper), falling)
        big_phi = jnp.where(upper > 0.0, 1.0 - tail, tail)
        hidden = (upper * big_phi).astype(BF)
        lanes = pl.ds(h * ff_half, ff_half)
        hidden_ref[:, lanes] = hidden
        slope_ref[:, lanes] = big_phi + upper * (falling * 0.3989422804014327)
        total = total + product(hidden, block[pl.ds(cut, ff_half), :])
    sum_ref[...] += total


def ff_forward(first_low, init, blocks, ff_half):
    rows, width = first_low.shape
    count = len(blocks)
    column = pl.BlockSpec((rows, 2 * ff_half), lambda i: (0, i))
    return pl.pallas_call(
        functools.partial(ff_forward_kernel, ff_half, count),
        out_shape=(
            jax.ShapeDtypeStruct((rows, width), F32),
            jax.ShapeDtypeStruct((rows, count * ff_half), BF),
            jax.ShapeDtypeStruct((rows, count * ff_half), F32),
        ),
        grid=(count // 2,),
        in_specs=[whole_block(rows, width)] * 2 + [pl.BlockSpec(memory_space=pl.ANY)] * count,
        out_specs=(whole_block(rows, width), column, column),
        scratch_shapes=[
            pltpu.VMEM((2, 2) + blocks[0].shape, BF),
            pltpu.SemaphoreType.DMA((2, 2)),
        ],
        compiler_params=params(),
        cost_estimate=cost(1, 1),
        name="ff_forward",
    )(first_low, init, *blocks)


def ff_backward_kernel(ff_half, count, base, d_fed_ref, init_ref, slope_ref, *refs):
    d_upper_ref, d_first_ref, column_ref, buf, sem = refs[-5:]
    cut = ff_half + PAD

    @pl.when(pl.program_id(0) == 0)
    def _():
        d_first_ref[...] = init_ref[...]
        column_ref[...] = refs[count][...]

    total = 0.0
    for h, block in enumerate(next_blocks(refs[:count], buf, sem)):
        lanes = pl.ds(h * ff_half, ff_half)
        d_hidden = against(d_fed_ref[...], block[pl.ds(cut, ff_half), :])
        d_upper = (d_hidden * slope_ref[:, lanes]).astype(BF)
        d_upper_ref[:, lanes] = d_upper
        row = base + 2 * pl.program_id(0) + h
        column_ref[pl.ds(row, 1), :] = jnp.sum(d_upper.astype(F32), axis=0, keepdims=True)
        total = total + product(d_upper, block[pl.ds(0, ff_half), :])
    d_first_ref[...] += total


def ff_backward(d_fed, init, slope, blocks, columns, base, ff_half):
    rows, width = d_fed.shape
    count = len(blocks)
    column = pl.BlockSpec((rows, 2 * ff_half), lambda i: (0, i))
    return pl.pallas_call(
        functools.partial(ff_backward_kernel, ff_half, count, base),
        out_shape=(
            jax.ShapeDtypeStruct(slope.shape, BF),
            jax.ShapeDtypeStruct((rows, width), F32),
            jax.ShapeDtypeStruct(columns.shape, F32),
        ),
        grid=(count // 2,),
        in_specs=[whole_block(rows, width)] * 2 + [column]
        + [pl.BlockSpec(memory_space=pl.ANY)] * count
        + [whole_block(*columns.shape)],
        out_specs=(column, whole_block(rows, width), whole_block(*columns.shape)),
        scratch_shapes=[
            pltpu.VMEM((2, 2) + blocks[0].shape, BF),
            pltpu.SemaphoreType.DMA((2, 2)),
        ],
        compiler_params=params(),
        cost_estimate=cost(
            4 * rows * width * ff_half * count,
            10 * rows * width + count * ff_half * (4 * width + 6 * rows),
        ),
        name="ff_backward",
    )(d_fed, init, slope, *blocks, columns)


def ff_grad_kernel(ff_half, spans, splits, joined, first_ref, fed_ref, up_ref, hidden_ref, *refs):
    count = len(spans)
    total = splits[-1]
    adds = list(refs[: sum(map(len, spans))])
    results = refs[len(adds) :]
    pieces = len(splits) - 1
    ups = over_rows(up_ref[...], first_ref[...])
    hiddens = over_rows(hidden_ref[...], fed_ref[...])
    for index in range(count):
        mine = [adds.pop(0) for _ in spans[index]]
        at = slice(index * ff_half, (index + 1) * ff_half)
        for low, high, share in ((0, ff_half, ups[at]), (ff_half, total, hiddens[at])):
            for (start, stop), add in zip(spans[index], mine):
                if start <= low and high <= stop:
                    share = share + add[pl.ds(low - start, high - low), :].astype(F32)
            for piece in range(pieces):
                if splits[piece] <= low and high <= splits[piece + 1]:
                    target = results[0 if joined else index * pieces + piece]
                    row = low - splits[piece] + joined * index * total
                    target[pl.ds(row, high - low), :] = share.astype(BF)


def ff_grad(d_upper, hidden, first_low, d_fed, place, adds, ff_half, cuts=(), joined=False, megabytes=24):
    rows, width = first_low.shape
    cols = width // 2
    count = len(adds)
    total = 2 * ff_half
    splits = (0, *cuts, total)
    lanes = pl.BlockSpec((rows, cols), lambda i: (0, i))
    column = pl.BlockSpec((rows, count * ff_half), lambda i: (0, place))
    spans = tuple(tuple((start, start + height) for start, height, _, _ in arrived) for arrived in adds)
    flat = [add for arrived in adds for add in arrived]

    def lane_block(height, at=0):
        return pl.BlockSpec((height, cols), lambda i: (at, i))

    heights = [count * total] if joined else [b - a for a, b in zip(splits, splits[1:])] * count
    return pl.pallas_call(
        functools.partial(ff_grad_kernel, ff_half, spans, splits, int(joined)),
        out_shape=tuple(jax.ShapeDtypeStruct((height, width), BF) for height in heights),
        grid=(2,),
        in_specs=[lanes, lanes, column, column] + [lane_block(height, at) for _, height, _, at in flat],
        out_specs=tuple(lane_block(height) for height in heights),
        compiler_params=params(megabytes),
        cost_estimate=cost(1, 1),
        name="ff_grad",
    )(first_low, d_fed, d_upper, hidden, *[array for _, _, array, _ in flat])


def combine_kernel(spans, *refs):
    arrays = list(refs[: sum(map(len, spans))])
    step = pl.program_id(0)
    for result, terms in zip(refs[len(arrays) :], spans):
        total = 0.0
        for low, high in terms:
            term = arrays.pop(0)[...].astype(F32)
            total = total + (term if (low, high) == terms[0] else jnp.where((low <= step) & (step < high), term, 0.0))
        result[...] = total.astype(BF)


def combine(*sums):
    height, width = sums[0][0][1].shape
    split = 4
    rows = height // split
    spans = tuple(tuple((low // rows, (low + array.shape[0]) // rows) for low, array in terms) for terms in sums)

    def row_block(low, high):
        return pl.BlockSpec((rows, width), lambda i: (jnp.clip(i - low, 0, high - low - 1), 0))

    return pl.pallas_call(
        functools.partial(combine_kernel, spans),
        out_shape=tuple(jax.ShapeDtypeStruct((height, width), BF) for _ in sums),
        grid=(split,),
        in_specs=[row_block(*span) for terms in spans for span in terms],
        out_specs=tuple(row_block(0, split) for _ in sums),
        compiler_params=params(),
        cost_estimate=cost(1, 1),
        name="combine",
    )(*[array for terms in sums for _, array in terms])


def diagonal_kernel(d_ref, w_ref, two_ref, one_ref):
    share = against(d_ref[...], w_ref[...]).astype(BF)
    half = two_ref.shape[0]
    two_ref[...] = share[:half]
    one_ref[...] = share[half:]


def diagonal_share(d_joint, w_seq, parts):
    rows, joint_width = d_joint.shape[0] // parts, d_joint.shape[1]
    width = w_seq.shape[0]
    half = (rows // 2, width)
    return pl.pallas_call(
        diagonal_kernel,
        out_shape=(jax.ShapeDtypeStruct(half, BF),) * 2,
        grid=(1,),
        in_specs=[pl.BlockSpec((rows, joint_width), lambda i: (parts - 1, 0)), whole_block(*w_seq.shape)],
        out_specs=(whole_block(*half),) * 2,
        compiler_params=params(),
        cost_estimate=cost(1, 1),
        name="diagonal_share",
    )(d_joint, w_seq)


def side_kernel(one_ref, two_ref, w_ref, to_two_ref, to_one_ref, via_one_ref, via_two_ref):
    half = to_two_ref.shape[0]
    share = against(one_ref[...], w_ref[...])
    via_one_ref[pl.ds(0, half), :] = (share[:half] + to_two_ref[...].astype(F32)).astype(BF)
    via_one_ref[pl.ds(half, half), :] = share[half:].astype(BF)
    share = against(two_ref[...], w_ref[...])
    via_two_ref[pl.ds(0, half), :] = share[:half].astype(BF)
    via_two_ref[pl.ds(half, half), :] = (share[half:] + to_one_ref[...].astype(F32)).astype(BF)


def side_shares(d_joint, w_seq, to_two, to_one, parts):
    rows, joint_width = d_joint.shape[0] // parts, d_joint.shape[1]
    width = w_seq.shape[0]
    return pl.pallas_call(
        side_kernel,
        out_shape=(jax.ShapeDtypeStruct((rows, width), BF),) * 2,
        grid=(1,),
        in_specs=[
            pl.BlockSpec((rows, joint_width), lambda i: (1, 0)),
            pl.BlockSpec((rows, joint_width), lambda i: (2, 0)),
            whole_block(*w_seq.shape),
            whole_block(*to_two.shape),
            whole_block(*to_one.shape),
        ],
        out_specs=(whole_block(rows, width),) * 2,
        compiler_params=params(),
        cost_estimate=cost(1, 1),
        name="side_shares",
    )(d_joint, d_joint, w_seq, to_two, to_one)


def row_grad_kernel(micros, d_pre_ref, w_ref, *refs):
    joints, arrived, out_ref = refs[:micros], refs[micros:-1], refs[-1]
    for m in range(micros):

        @pl.when(pl.program_id(0) == m)
        def _(m=m):
            total = d_pre_ref[...] + against(joints[m][...], w_ref[...])
            for term in arrived[2 * m : 2 * m + 2]:
                total = total + term[...].astype(F32)
            out_ref[...] = total


def row_grad(d_pre, w_seq, d_joints, arrived, parts):
    micros = len(d_joints)
    rows, joint_width = d_joints[0].shape[0] // parts, d_joints[0].shape[1]
    width = w_seq.shape[0]
    block = pl.BlockSpec((rows, width), lambda i: (i, 0))
    flat = [a for pair in arrived for a in pair]
    return pl.pallas_call(
        functools.partial(row_grad_kernel, micros),
        out_shape=jax.ShapeDtypeStruct(d_pre.shape, F32),
        grid=(micros,),
        in_specs=[block, whole_block(*w_seq.shape)]
        + [whole_block(rows, joint_width)] * micros
        + [whole_block(rows, width)] * len(flat),
        out_specs=block,
        compiler_params=params(),
        cost_estimate=cost(1, 1),
        name="row_grad",
    )(d_pre, w_seq, *d_joints, *flat)


def shards(
    embedded,
    token_table,
    masked_pos,
    replace_ids,
    w_query,
    b_query,
    w_key,
    w_value,
    b_value,
    w_out,
    b_out,
    ln1_gain,
    ln1_bias,
    w_up,
    b_up,
    w_down,
    b_down,
    ln2_gain,
    ln2_bias,
    grad_masked,
):
    rank = lax.axis_index("tensor")
    count = lax.axis_size("tensor")
    dp_count = lax.axis_size("dp")
    core = lax.axis_index("dp") % 2
    row_part = lax.axis_index("dp") // 2 % 2
    micro_count, row_count, width = embedded.shape
    local_width = w_query.shape[1]
    ff_local = w_up.shape[1]
    vocab_count = token_table.shape[0]
    parts = LEN // row_count
    groups = count // parts
    part = rank % parts
    group = rank // parts
    part_width = width // parts
    pairs = part_width // PAIR
    half_count = row_count // 2
    half_rows = width // 2
    ff_half = ff_local // 2
    out_half = local_width // 2
    cut = ff_half + PAD
    own_first = core == 0
    micros = range(micro_count)

    def by_core(mine, other, axis=0, first=None):
        return jnp.where(
            own_first if first is None else first,
            jnp.concatenate([mine, other], axis=axis),
            jnp.concatenate([other, mine], axis=axis),
        )

    order = list(range(0, count, 2)) + list(range(count - 1, 0, -2))
    ring_fw = [(order[i], order[(i + 1) % count]) for i in range(count)]
    ring_bw = [(b, a) for a, b in ring_fw]
    far = count // 2
    ring_pos = jnp.where(rank % 2 == 0, rank // 2, count - 1 - rank // 2)
    offsets = [0] + [sign * s for s in range(1, far) for sign in (-1, 1)] + [far]

    def forward(values):
        return lax.ppermute(values, "tensor", ring_fw)

    def backward(values):
        return lax.ppermute(values, "tensor", ring_bw)

    part_order = jnp.stack([part ^ j for j in range(parts)]).astype(jnp.int32)

    slot_pos = lax.dynamic_index_in_dim(masked_pos, group, 1, keepdims=False)
    slot_ids = lax.dynamic_index_in_dim(replace_ids, group, 1, keepdims=False)
    slot_grads = lax.dynamic_index_in_dim(grad_masked, group, 1, keepdims=False)
    vocab_iota = jnp.arange(vocab_count, dtype=jnp.int32)

    def replacement(positions, step):
        matches = positions[:, None] == slot_pos[step][None, :]
        replaced = jnp.any(matches, axis=1)
        row_ids = jnp.sum(jnp.where(matches, slot_ids[step][None, :], 0), axis=1)
        hot = (row_ids[:, None] == vocab_iota[None, :]) & replaced[:, None]
        return matches, replaced, hot

    row_iota = jnp.arange(row_count, dtype=jnp.int32)
    placed, replaced_list, hots, cots, seq_hots = [], [], [], [], []
    for step in micros:
        matches, replaced, hot = replacement(part * row_count + row_iota, step)
        inserted = product(hot.astype(BF), token_table)
        placed.append(jnp.where(replaced[:, None], inserted, embedded[step].astype(F32)).astype(BF))
        replaced_list.append(replaced)
        hots.append(hot.astype(F32))
        cots.append(product(matches.astype(BF), slot_grads[step]))
        seq_pos = jnp.concatenate([(part ^ j) * row_count + row_iota for j in range(parts)])
        seq_hot = replacement(seq_pos, step)[2].astype(BF)
        seq_hots.append(jnp.concatenate([seq_hot, jnp.ones_like(seq_hot[:, :2])], axis=1))

    joint_half = jnp.concatenate(
        [
            lax.dynamic_slice_in_dim(
                jnp.concatenate([w_query, w_key, w_value], axis=1), core * half_rows, half_rows, 0
            ),
            jnp.pad(
                jnp.concatenate([b_query, jnp.zeros_like(b_query), b_value])[None, :],
                ((0, PAD - 1), (0, 0)),
            ),
        ],
        axis=0,
    )
    spread = [
        [(groups * p + i, p + parts * ((i + k) % groups)) for p in range(parts) for i in range(groups)]
        for k in range(groups)
    ]
    piece = jnp.concatenate(
        [
            lax.dynamic_slice_in_dim(w_up.T, core * ff_half, ff_half, 0),
            jnp.pad(
                lax.dynamic_slice_in_dim(b_up, core * ff_half, ff_half, 0)[None, :],
                ((0, PAD - 1), (0, width - ff_half)),
            ),
            lax.dynamic_slice_in_dim(w_down, core * ff_half, ff_half, 0),
        ],
        axis=0,
    )

    w_mine = [lax.ppermute(joint_half, "tensor", spread[k]) for k in range(groups)]
    ones = [swap(placed[0], "tensor", 1)]
    twos = [swap(placed[0], "tensor", 2)]
    ones, twos, w_mine, placed, piece, cots, w_out, hots, seq_hots, replaced_list = fence(
        ones, twos, w_mine, placed, piece, cots, w_out, hots, seq_hots, replaced_list
    )
    w_out_half = lax.all_gather(
        lax.dynamic_slice_in_dim(w_out, core * out_half, out_half, 0), "tensor", axis=0
    )
    w_other = [swap(w, "dp", 1) for w in w_mine]
    w_seq, b_seq = assemble(
        jnp.stack([core] + [(group - i) % groups for i in range(groups)]).astype(jnp.int32),
        w_mine,
        w_other,
        local_width,
    )

    joints, x_mine, x_other, heads, log_sums, own_heads = [], [], [], [], [], []
    near = [piece[:cut], piece[cut:]]
    arrived = []
    at_core = core[None].astype(jnp.int32)
    for step in micros:
        threes = (swap(ones[step][:half_count], "tensor", 2), swap(twos[step][half_count:], "tensor", 1))
        rows = [placed[step], ones[step], twos[step], *threes]
        if step + 1 < micro_count:
            ones.append(swap(placed[step + 1], "tensor", 1))
            twos.append(swap(placed[step + 1], "tensor", 2))
        moved = (forward(near[step]), backward(near[step]))
        joint, mine, other = project(at_core, rows, w_seq, b_seq)
        pieces, whole, sums = attn_forward(joint, parts)
        joints.append(joint)
        log_sums.append(sums)
        own_heads.append(whole)
        x_mine.append(mine)
        x_other.append(other)
        ones, twos, moved, pieces, near = fence(ones, twos, moved, pieces, near)
        arrived.append(moved)
        heads.append([pieces[0]] + [swap(pieces[j], "tensor", j) for j in range(1, parts)])
    fw, bw = (jnp.concatenate([arrived[0][d], arrived[1][d]], axis=0) for d in range(2))
    heads, fw, bw, w_out_half = fence(heads, fw, bw, w_out_half)
    w_out_other = swap(w_out_half, "dp", 1)
    blocks = [piece, swap(piece, "dp", 1), fw, bw, swap(fw, "dp", 1), swap(bw, "dp", 1)]

    vectors_one = jnp.stack([b_out, ln1_gain, ln1_bias, b_down] + [b_out] * 4).astype(F32)
    heads_out, norm_one, scale_one, pre_two, first_low, w_out_all = attend(
        jnp.concatenate([part_order, at_core]), heads, placed, w_out_half, w_out_other, vectors_one
    )

    step_blocks = [blocks[:2], blocks[2:6]]
    hidden_low, slopes = [None] * (far + 1), [None] * (far + 1)
    for s in range(2, far + 1):
        if s < far:
            moved = [forward(fw), backward(bw)]
        else:
            moved = [forward(fw[:cut]), backward(bw[cut:])]
        for t in (0, 1) if s == 2 else (s - 1,):
            pre_two, hidden_low[t], slopes[t] = ff_forward(first_low, pre_two, step_blocks[t], ff_half)
        moved, pre_two = fence(moved, pre_two)
        if s == far:
            moved = [jnp.concatenate(moved, axis=0)]
        else:
            fw, bw = moved
        step_blocks.append(moved + [swap(block, "dp", 1) for block in moved])
    pre_two, hidden_low[far], slopes[far] = ff_forward(first_low, pre_two, step_blocks[far], ff_half)

    vectors_two = jnp.stack([ln2_gain, ln2_bias] + [ln2_bias] * 6).astype(F32)
    layer_out, d_pre_two, d_fed, sums_two = second_norm(pre_two, jnp.concatenate(cots, axis=0), vectors_two)
    total = 2 * ff_half

    def ff_blocks(offsets_, other, adds=None, cuts=(), megabytes=24):
        s = abs(offsets_[0])
        result = ff_grad(
            d_uppers[s], hidden_low[s], first_low, d_fed, other, adds or [[] for _ in offsets_], ff_half, cuts,
            bool(other), megabytes,
        )
        return result[0] if other else result

    def both(s):
        return [-s, s] if s else [0]

    def summed(s, others, megabytes=24):
        return ff_blocks(both(s), 0, [[(0, total, others, i)] for i in range(len(both(s)))], (), megabytes)

    d_uppers = [None] * (far + 1)
    rel_b_up = jnp.zeros((2 * count, ff_half), F32)

    def back(s, d_first):
        nonlocal rel_b_up
        base = 4 * s - 2 if s else 0
        d_uppers[s], d_first, rel_b_up = ff_backward(
            d_fed, d_first, slopes[s], step_blocks[s], rel_b_up, base, ff_half
        )
        return d_first

    d_first = back(far, d_pre_two)
    others = ff_blocks([far], 1)
    others, d_uppers[far], d_first = fence(others, d_uppers[far], d_first)
    others = swap(others, "dp", 1)
    d_first = back(far - 1, d_first)
    others, d_uppers[far], d_first = fence(others, d_uppers[far], d_first)
    parcel = ff_blocks([far], 0, [[(0, total, others, 0)]], (ff_half,))
    next_others = ff_blocks(both(far - 1), 1)
    parcel, next_others, d_uppers[far - 1], d_first = fence(parcel, next_others, d_uppers[far - 1], d_first)
    moved = [forward(parcel[0]), backward(parcel[1])]
    others = swap(next_others, "dp", 1)
    for s in range(far - 2, far // 2 - 1, -1):
        d_first = back(s, d_first)
    others, d_uppers[far - 1], d_first = fence(others, d_uppers[far - 1], d_first)
    share = summed(far - 1, others)
    next_others = ff_blocks(both(far - 2), 1)
    moved, share, next_others, d_first = fence(moved, share, next_others, d_first)
    parcel = combine([(0, share[0]), (ff_half, moved[1])], [(0, share[1]), (0, moved[0])])
    parcel, next_others, d_first = fence(parcel, next_others, d_first)
    moved = [forward(parcel[1]), backward(parcel[0])]
    others = swap(next_others, "dp", 1)
    for s in range(far // 2 - 1, -1, -1):
        d_first = back(s, d_first)
    d_pre_one, d_attended, sums_one, *d_heads = attend_back(
        part_order, d_first, norm_one, scale_one, vectors_one, w_out_all, parts
    )
    others, d_uppers[far - 2], d_heads = fence(others, d_uppers[far - 2], d_heads)
    seq_grads = [d_heads[0]] + [swap(d_heads[j], "tensor", j) for j in range(1, parts)]
    share = summed(far - 2, others)
    next_others = ff_blocks(both(far - 3), 1)

    d_out = over_rows(heads_out, d_attended).astype(BF).reshape(count, 2, out_half, width)
    out_other = lax.dynamic_index_in_dim(d_out, 1 - core, 1, keepdims=False).reshape(-1, width)
    out_mine = lax.dynamic_index_in_dim(d_out, core, 1, keepdims=False).reshape(-1, width)
    moved, share, seq_grads, next_others, out_other = fence(moved, share, seq_grads, next_others, out_other)
    seq_grads = jnp.concatenate(seq_grads, axis=0)

    d_joints = [jnp.zeros((), BF) for _ in micros]
    work = [(m, g) for m in micros for g in range(pairs)]

    def over_dp(values, bit=2):
        while bit < dp_count:
            values = (values.astype(F32) + swap(values, "dp", bit).astype(F32)).astype(BF)
            bit *= 2
        return values

    def diagonal(step):
        to_two, to_one = diagonal_share(d_joints[step], w_seq, parts)
        return (swap(to_two, "tensor", 2), swap(to_one, "tensor", 1))

    def side_parcels(step, arrived):
        return side_shares(d_joints[step], w_seq, *arrived, parts)

    def sides(parcels):
        return (swap(parcels[0], "tensor", 1), swap(parcels[1], "tensor", 2))

    def own_table(d_rows):
        return lax.dot_general(
            jnp.concatenate(hots, axis=0),
            d_rows,
            ROWS_DIMS,
            precision=lax.Precision.HIGHEST,
            preferred_element_type=F32,
        )

    partial, stage = [() for _ in micros], [0 for _ in micros]
    d_w = []
    table = own_table(d_pre_one)
    plan = [work[:pairs], work[pairs:-1], work[-1:]]
    for index in range(max(far - 1, len(plan))):
        s = far - 2 - index
        if s > 0:
            parcel = combine([(0, share[0]), (0, moved[1])], [(0, share[1]), (0, moved[0])])
            joints, d_joints, d_fed, parcel, next_others = fence(joints, d_joints, d_fed, parcel, next_others)
            moved = [forward(parcel[1]), backward(parcel[0])]
            others = swap(next_others, "dp", 1)
        elif s == 0:
            parcel = combine([(0, share[0]), (0, moved[0]), (0, moved[1])])[0]
            ff_up, ff_down = parcel[:ff_half], parcel[ff_half:]
            joints, d_joints, ff_up, ff_down = fence(joints, d_joints, ff_up, ff_down)
            ff_up = over_dp(ff_up)
        if index == 0:
            out_mine = (out_mine.astype(F32) + swap(out_other, "dp", 1).astype(F32)).astype(BF)
            out_mine = out_mine.reshape(count, 2, out_half // 2, width)
            out_other = lax.dynamic_index_in_dim(out_mine, 1 - row_part, 1, keepdims=False).reshape(-1, width)
            out_mine = lax.dynamic_index_in_dim(out_mine, row_part, 1, keepdims=False).reshape(-1, width)
            out_mine = (out_mine.astype(F32) + swap(out_other, "dp", 2).astype(F32)).astype(BF)
        elif index == 1:
            out_sum = lax.psum_scatter(out_mine, "tensor", scatter_dimension=0, tiled=True)
        for m in micros:
            ready = max(i for i, pairs_ in enumerate(plan) if (m, pairs - 1) in pairs_) + 1
            if index == ready:
                partial[m], stage[m] = diagonal(m), 1
            elif index == ready + 1:
                partial[m], stage[m] = sides(side_parcels(m, partial[m])), 2
        if index == len(plan) - 1:
            d_w = [(over_rows(x_other[m], d_joints[m]), over_rows(x_mine[m], d_joints[m])) for m in micros[:-1]]
        next_others = ()
        if s > 1:
            next_others = ff_blocks(both(s - 2), 1)
        for m, g in plan[index] if index < len(plan) else ():
            d_joints[m] = attn_backward(
                joints[m], log_sums[m], seq_grads, own_heads[m], parts, m, micro_count, g, (d_joints[m],) if g else ()
            )
        if s > 0:
            share = summed(s - 1, others)
            moved, share, next_others, d_joints, partial, table, d_w, out_mine = fence(
                moved, share, next_others, d_joints, partial, table, d_w, out_mine
            )
        elif s == 0:
            ff_up, d_joints, partial, table, d_w = fence(ff_up, d_joints, partial, table, d_w)

    last = micro_count - 1
    d_w.append((over_rows(x_other[last], d_joints[last]), None))
    other_half = sum(other for other, _ in d_w).astype(BF)
    other_half, d_joints, partial, ff_up, ff_down = fence(other_half, d_joints, partial, ff_up, ff_down)
    other_half = swap(other_half, "dp", 1)
    for m in micros:
        if stage[m] == 0:
            partial[m] = diagonal(m)
        elif stage[m] == 1:
            partial[m] = sides(side_parcels(m, partial[m]))

    def over_bits(values, axis, low, high):
        while low < high:
            bits = (low, 2 * low, 3 * low) if 2 * low < high else (low,)
            sent = values.astype(BF)
            terms = [sent.astype(F32)] + [swap(sent, axis, bit).astype(F32) for bit in bits]
            while len(terms) > 1:
                terms = [a + b for a, b in zip(terms[::2], terms[1::2])]
            values = terms[0]
            low *= 4
        return values

    row_offset, row_other = [0, 0], [0, 1]
    for s in range(1, far):
        row_offset += [-s % count, s, -s % count, s]
        row_other += [0, 0, 1, 1]
    row_offset, row_other = jnp.array(row_offset + [far, far]), jnp.array(row_other + [0, 1])
    place = jnp.repeat(jnp.array([order.index(i) for i in range(count)]), 2)
    half_of = jnp.tile(jnp.arange(2), count)
    chosen = (((place - ring_pos) % count)[:, None] == row_offset[None, :]) & (
        (half_of != core)[:, None] == (row_other[None, :] == 1)
    )
    all_b_up = jnp.dot(
        chosen.astype(F32), rel_b_up, precision=lax.Precision.HIGHEST, preferred_element_type=F32
    )
    all_b_up = jnp.pad(all_b_up, ((0, 0), (0, width - ff_half)))
    hot_sum = sum(over_rows(seq_hots[m], d_joints[m]) for m in micros)
    d_b_seq = hot_sum[vocab_count]
    rest, thirds = hot_sum, []
    for _ in range(3):
        thirds.append(rest.astype(BF))
        rest = rest - thirds[-1].astype(F32)
    table_rows = hot_sum.shape[0]
    shares = against(jnp.concatenate(thirds, axis=0), w_seq).reshape(3, table_rows, width)
    table = jnp.pad(table, ((0, table_rows - vocab_count), (0, 0))) + ((shares[2] + shares[1]) + shares[0])
    empty = jnp.zeros((width,), F32)
    d_b_query, d_b_value = (
        lax.dynamic_update_slice_in_dim(
            empty,
            jnp.concatenate([d_b_seq[(3 * g + a) * PAIR : (3 * g + a + 1) * PAIR] for g in range(pairs)]),
            part * part_width,
            0,
        )
        for a in (0, 2)
    )
    place_row = lax.broadcasted_iota(jnp.int32, table.shape, 0)
    table = jnp.where(place_row == vocab_count, d_b_query[None], table)
    table = jnp.where(place_row == vocab_count + 1, d_b_value[None], table)
    small = jnp.concatenate([table, sums_one, sums_two, all_b_up], axis=0)

    my_half = sum(mine for _, mine in d_w[: len(d_w)] if mine is not None)
    my_half = my_half + sum(over_rows(x_mine[m], d_joints[m]) for m in micros if d_w[m][1] is None)
    my_half = (my_half + other_half.astype(F32)).astype(BF)
    my_half, small, ff_up, ff_down, partial = fence(my_half, small, ff_up, ff_down, partial)

    if local_width != PAIR:
        columns = [
            jnp.concatenate(
                [my_half[:, (3 * g + a) * PAIR : (3 * g + a + 1) * PAIR] for g in range(pairs)], axis=1
            )
            for a in range(3)
        ]
        my_half = jnp.concatenate(
            [c[:, i * local_width : (i + 1) * local_width] for i in range(groups) for c in columns], axis=1
        )
    joint_sum = sum(
        lax.ppermute(
            lax.dynamic_slice_in_dim(
                my_half, (group - k) % groups * 3 * local_width, 3 * local_width, 1
            ),
            "tensor",
            [(b, a) for a, b in spread[k]],
        ).astype(F32)
        for k in range(groups)
    ).astype(BF)
    small = over_bits(small, "dp", 1, dp_count)
    ff_down = over_dp(ff_down)
    ff_up = ff_up.T
    up_other = swap(ff_up, "dp", 1)
    if stage[last] == 0:
        partial[last] = side_parcels(last, partial[last])
    grad_rows = row_grad(d_pre_one, w_seq, d_joints, partial[:last], parts)
    joint_sum, small, ff_up, ff_down, up_other, out_sum, partial[last], grad_rows = fence(
        joint_sum, small, ff_up, ff_down, up_other, out_sum, partial[last], grad_rows
    )

    joint_sum = over_dp(joint_sum)
    out_sum = over_dp(out_sum, 4)
    out_sum = by_core(out_sum, swap(out_sum, "dp", 2), 0, row_part == 0)
    down_other = swap(ff_down, "dp", 1)
    if stage[last] == 0:
        partial[last] = sides(partial[last])
    small = over_bits(small, "tensor", 1, min(4, count))
    grad_w_up = by_core(ff_up, up_other, 1).astype(F32)
    grad_w_down = by_core(ff_down, down_other).astype(F32)
    joint_sum, out_sum, grad_w_up, grad_w_down = fence(joint_sum, out_sum, grad_w_up, grad_w_down)
    out_other = swap(out_sum, "dp", 1)
    grad_w_out = by_core(out_sum, out_other).astype(F32)
    joint_other = swap(joint_sum, "dp", 1)
    small = over_bits(small, "tensor", 4, count)
    late = jnp.concatenate([partial[last][0], partial[last][1]], axis=1).astype(F32)
    late = late[:, :width] + late[:, width:]
    late = jnp.concatenate([jnp.zeros((row_count * last, width), F32), late], axis=0)
    grad_rows = jnp.where(jnp.concatenate(replaced_list)[:, None], 0.0, grad_rows + late)
    grad_joint = by_core(joint_sum, joint_other).astype(F32)
    grad_b_query, grad_b_value = (
        lax.dynamic_slice_in_dim(small[vocab_count + i], rank * local_width, local_width, 0) for i in range(2)
    )
    sums_at = (table_rows, table_rows + 8)
    grad_b_out, grad_gone, grad_bone, grad_b_down, grad_gtwo, grad_btwo = (
        small[at + i] for at in sums_at for i in range(3)
    )
    grad_b_up = lax.dynamic_slice_in_dim(small, table_rows + 16 + 2 * rank, 2, 0)[:, :ff_half].reshape(-1)

    return (
        layer_out.reshape(micro_count, row_count, width),
        grad_rows.reshape(micro_count, row_count, width),
        small[:vocab_count],
        grad_joint[:, :local_width],
        grad_b_query,
        grad_joint[:, local_width : 2 * local_width],
        grad_joint[:, 2 * local_width :],
        grad_b_value,
        grad_w_out,
        grad_b_out,
        grad_gone,
        grad_bone,
        grad_w_up,
        grad_b_up,
        grad_w_down,
        grad_b_down,
        grad_gtwo,
        grad_btwo,
    )


def solution(mesh):
    return jax.shard_map(
        shards,
        mesh=mesh,
        in_specs=(
            P(None, ("dp", "tensor"), None),
            P(),
            P(None, "dp", None),
            P(None, "dp", None),
            P(None, "tensor"),
            P("tensor"),
            P(None, "tensor"),
            P(None, "tensor"),
            P("tensor"),
            P("tensor", None),
            P(),
            P(),
            P(),
            P(None, "tensor"),
            P("tensor"),
            P("tensor", None),
            P(),
            P(),
            P(),
            P(None, "dp", None, None),
        ),
        out_specs=(
            P(None, ("dp", "tensor"), None),
            P(None, ("dp", "tensor"), None),
            P(),
            P(None, "tensor"),
            P("tensor"),
            P(None, "tensor"),
            P(None, "tensor"),
            P("tensor"),
            P("tensor", None),
            P(),
            P(),
            P(),
            P(None, "tensor"),
            P("tensor"),
            P("tensor", None),
            P(),
            P(),
            P(),
        ),
        check_vma=False,
    )
```

```python
import functools

import jax
import jax.numpy as jnp
from jax import lax
from jax.experimental import pallas as pl
from jax.experimental.pallas import tpu as pltpu
from jax.sharding import PartitionSpec as P

HD = 64
LEN = 1024
EPSILON = 1e-12
SCALE = HD ** (-0.5)
ROWS_DIMS = (((0,), (0,)), ((), ()))
LAST_DIMS = (((1,), (1,)), ((), ()))
BF = jnp.bfloat16
F32 = jnp.float32
PAD = 16
PAIR = 2 * HD
LOG2E = 1.4426950408889634


def product(left_mat, right_mat):
    return jnp.dot(left_mat, right_mat, preferred_element_type=F32)


def over_rows(left_mat, right_mat):
    return lax.dot_general(left_mat, right_mat, ROWS_DIMS, preferred_element_type=F32)


def against(left_mat, right_mat):
    return lax.dot_general(left_mat, right_mat, LAST_DIMS, preferred_element_type=F32)


def swap(values, axis, bit):
    count = lax.axis_size(axis)
    return lax.ppermute(values, axis, [(i, i ^ bit) for i in range(count)])


def fence(*trees):
    return lax.optimization_barrier(trees)


def whole_block(*shape):
    return pl.BlockSpec(shape, lambda *_: (0,) * len(shape))


def params(megabytes=24):
    return pltpu.CompilerParams(vmem_limit_bytes=megabytes * 1024 * 1024)


def cost(flops, nbytes, transcendentals=0):
    return pl.CostEstimate(flops=flops, bytes_accessed=nbytes, transcendentals=transcendentals)


def assemble_kernel(groups, local, half, at_ref, *refs):
    mines, others = refs[:groups], refs[groups : 2 * groups]
    w_ref, b_ref = refs[2 * groups :]
    for i in range(groups):
        for k in range(groups):

            @pl.when(at_ref[1 + i] == k)
            def _(i=i, k=k):
                for a in range(3):
                    source = pl.ds(a * local, local)
                    lane = (3 * (i * local // PAIR) + a) * PAIR + i * local % PAIR
                    target = pl.ds(lane, local)
                    top = pl.multiple_of(at_ref[0] * half, half)
                    low = pl.multiple_of((1 - at_ref[0]) * half, half)
                    w_ref[pl.ds(top, half), target] = mines[k][pl.ds(0, half), source]
                    w_ref[pl.ds(low, half), target] = others[k][pl.ds(0, half), source]
                    b_ref[:, target] = mines[k][pl.ds(half, PAD), source][0:1].astype(F32)


def assemble(at, mines, others, local):
    groups = len(mines)
    half, width3 = others[0].shape[0] - PAD, others[0].shape[1]
    return pl.pallas_call(
        functools.partial(assemble_kernel, groups, local, half),
        out_shape=(
            jax.ShapeDtypeStruct((2 * half, groups * width3), BF),
            jax.ShapeDtypeStruct((1, groups * width3), F32),
        ),
        grid_spec=pltpu.PrefetchScalarGridSpec(
            num_scalar_prefetch=1,
            grid=(1,),
            in_specs=[whole_block(*m.shape) for m in (*mines, *others)],
            out_specs=(whole_block(2 * half, groups * width3), whole_block(1, groups * width3)),
        ),
        compiler_params=params(),
        cost_estimate=cost(0, 8 * half * groups * width3),
        name="assemble",
    )(at, *mines, *others)


def project_kernel(parts, at_ref, *refs):
    pieces = refs[: parts + 1]
    w_ref, b_ref, joint_ref, mine_ref, other_ref, x_ref = refs[parts + 1 :]
    step = pl.program_id(0)
    for j in range(parts - 1):

        @pl.when(step == j)
        def _(j=j):
            x_ref[...] = pieces[j][...]

    @pl.when(step == parts - 1)
    def _():
        rows = pieces[-1].shape[0]
        x_ref[pl.ds(0, rows), :] = pieces[-2][...]
        x_ref[pl.ds(rows, rows), :] = pieces[-1][...]

    joint_ref[...] = (product(x_ref[...], w_ref[...]) + b_ref[...]).astype(BF)
    half = mine_ref.shape[1]
    mine_ref[...] = x_ref[:, pl.ds(pl.multiple_of(at_ref[0] * half, half), half)]
    other_ref[...] = x_ref[:, pl.ds(pl.multiple_of((1 - at_ref[0]) * half, half), half)]


def project(at, pieces, w_seq, b_seq):
    parts = len(pieces) - 1
    rows, width = pieces[0].shape
    joint_width = w_seq.shape[1]
    half = jax.ShapeDtypeStruct((parts * rows, width // 2), BF)
    half_block = pl.BlockSpec((rows, width // 2), lambda i, s: (i, 0))
    return pl.pallas_call(
        functools.partial(project_kernel, parts),
        out_shape=(jax.ShapeDtypeStruct((parts * rows, joint_width), BF), half, half),
        grid_spec=pltpu.PrefetchScalarGridSpec(
            num_scalar_prefetch=1,
            grid=(parts,),
            in_specs=[whole_block(*p.shape) for p in pieces]
            + [whole_block(*w_seq.shape), whole_block(*b_seq.shape)],
            out_specs=(pl.BlockSpec((rows, joint_width), lambda i, s: (i, 0)), half_block, half_block),
            scratch_shapes=[pltpu.VMEM((rows, width), BF)],
        ),
        compiler_params=params(),
        cost_estimate=cost(2 * parts * rows * width * joint_width, 12 * parts * rows * width),
        name="project",
    )(at, *pieces, w_seq, b_seq)


def first_head(rows):
    return lax.broadcasted_iota(jnp.int32, (rows, PAIR), 1) < HD


def one_head(values, head, fill=0.0):
    first = first_head(values.shape[0])
    filled = jnp.full(values.shape, fill, values.dtype)
    return jnp.where(first, filled, values) if head else jnp.where(first, values, filled)


def attn_forward_kernel(q_ref, k_ref, v_ref, *refs):
    outs, all_ref, log_ref = refs[:-2], refs[-2], refs[-1]
    rows = q_ref.shape[0]
    mixed, log_sums = [], []
    scores = [against(one_head(q_ref[...], head), k_ref[...]) for head in range(2)]
    tops = [jnp.max(score, axis=-1, keepdims=True) * (SCALE * LOG2E) for score in scores]
    weights = [jnp.exp2(score * (SCALE * LOG2E) - top).astype(BF) for score, top in zip(scores, tops)]
    for head in range(2):
        both = product(weights[head], one_head(v_ref[...], head, 1.0))
        total = pltpu.roll(both, HD, 1)
        mixed.append(both / total)
        log_sums.append(tops[head] + jnp.log(total) * LOG2E)
    first = first_head(rows)
    value = jnp.where(first, mixed[0], mixed[1]).astype(BF)
    turned = jnp.where(first, log_sums[0], log_sums[1]).T
    log_ref[0, 0:1, :] = turned[0:1]
    log_ref[0, 1:2, :] = turned[HD : HD + 1]
    all_ref[...] = value
    for j, out in enumerate(outs):

        @pl.when(pl.program_id(1) == j)
        def _(out=out):
            out[...] = value


def attn_forward(joint, parts):
    rows = joint.shape[0] // parts
    pairs = joint.shape[1] // (3 * PAIR)
    shape = jax.ShapeDtypeStruct((rows, pairs * PAIR), BF)
    result = pl.pallas_call(
        attn_forward_kernel,
        out_shape=(shape,) * parts
        + (
            jax.ShapeDtypeStruct((parts * rows, pairs * PAIR), BF),
            jax.ShapeDtypeStruct((pairs, 8, parts * rows), F32),
        ),
        grid=(pairs, parts),
        in_specs=[
            pl.BlockSpec((rows, PAIR), lambda g, i: (i, 3 * g)),
            pl.BlockSpec((parts * rows, PAIR), lambda g, i: (0, 3 * g + 1)),
            pl.BlockSpec((parts * rows, PAIR), lambda g, i: (0, 3 * g + 2)),
        ],
        out_specs=(pl.BlockSpec((rows, PAIR), lambda g, i: (0, g)),) * parts
        + (pl.BlockSpec((rows, PAIR), lambda g, i: (i, g)), pl.BlockSpec((1, 8, rows), lambda g, i: (g, 0, i))),
        compiler_params=params(),
        cost_estimate=cost(
            16 * joint.shape[0] ** 2 * pairs * PAIR, 3 * joint.size, 2 * pairs * joint.shape[0] ** 2
        ),
        name="attn_forward",
    )(joint, joint, joint)
    return result[:parts], result[parts], result[parts + 1]


def attn_backward_kernel(parts, q_ref, k_ref, v_ref, log_ref, g_ref, o_ref, *refs):
    d_ref, kt_ref, dk_acc, dv_acc = refs[-4:]
    step = pl.program_id(0)
    rows = q_ref.shape[0]

    @pl.when(step == 0)
    def _():
        kt_ref[...] = k_ref[...].T
        dk_acc[...] = jnp.zeros_like(dk_acc)
        dv_acc[...] = jnp.zeros_like(dv_acc)

    row_dots = (g_ref[...].astype(F32) * o_ref[...].astype(F32)).T
    dq_parts = []
    for head in range(2):
        queries = one_head(q_ref[...], head)
        grads = one_head(g_ref[...], head)
        row_dot = jnp.sum(row_dots[head * HD : (head + 1) * HD], axis=0, keepdims=True)
        log_sum = log_ref[0, pl.ds(head, 1), :]
        scores = against(k_ref[...], queries)
        probs = jnp.exp2(scores * (SCALE * LOG2E) - log_sum)
        d_probs = against(v_ref[...], grads)
        d_scores = (probs * (d_probs - row_dot)).astype(BF)
        dv_acc[...] += product(probs.astype(BF), grads)
        dk_acc[...] += product(d_scores, queries)
        dq_parts.append(product(kt_ref[pl.ds(head * HD, HD), :], d_scores))
    d_ref[pl.ds(step * rows, rows), pl.ds(0, PAIR)] = (
        jnp.concatenate(dq_parts, axis=0).T * SCALE
    ).astype(BF)

    @pl.when(step == parts - 1)
    def _():
        d_ref[:, pl.ds(PAIR, PAIR)] = (dk_acc[...] * SCALE).astype(BF)
        d_ref[:, pl.ds(2 * PAIR, PAIR)] = dv_acc[...].astype(BF)


def attn_backward(joint, log_sums, grads, heads, parts, step, micros, pair, kept):
    rows = joint.shape[0] // parts
    return pl.pallas_call(
        functools.partial(attn_backward_kernel, parts),
        out_shape=jax.ShapeDtypeStruct(joint.shape, BF),
        grid=(parts,),
        in_specs=[
            pl.BlockSpec((rows, PAIR), lambda i: (i, 3 * pair)),
            pl.BlockSpec((parts * rows, PAIR), lambda i: (0, 3 * pair + 1)),
            pl.BlockSpec((parts * rows, PAIR), lambda i: (0, 3 * pair + 2)),
            pl.BlockSpec((1, 8, rows), lambda i: (pair, 0, i)),
            pl.BlockSpec((rows, PAIR), lambda i: (i * micros + step, pair)),
            pl.BlockSpec((rows, PAIR), lambda i: (i, pair)),
        ]
        + [pl.BlockSpec(memory_space=pl.ANY)] * len(kept),
        out_specs=pl.BlockSpec((parts * rows, 3 * PAIR), lambda i: (0, pair)),
        scratch_shapes=[
            pltpu.VMEM((PAIR, parts * rows), BF),
            pltpu.VMEM((parts * rows, PAIR), F32),
            pltpu.VMEM((parts * rows, PAIR), F32),
        ],
        input_output_aliases={6 + i: i for i in range(len(kept))},
        compiler_params=params(),
        cost_estimate=cost(1, 1),
        name="attn_backward",
    )(joint, joint, joint, log_sums, grads, heads, *kept)


def normed(values):
    row_mean = jnp.mean(values, axis=-1, keepdims=True)
    centred = values - row_mean
    row_var = jnp.mean(centred * centred, axis=-1, keepdims=True)
    scale = lax.rsqrt(row_var + EPSILON)
    return centred * scale, scale


def norm_backward(norm, scale, gain_vec, grads):
    d_norm = grads * gain_vec
    mean_d = jnp.mean(d_norm, axis=-1, keepdims=True)
    mean_dn = jnp.mean(d_norm * norm, axis=-1, keepdims=True)
    return (d_norm - mean_d - norm * mean_dn) * scale


def column_sums(sums_ref, *values):
    @pl.when(pl.program_id(0) == 0)
    def _():
        sums_ref[...] = jnp.zeros_like(sums_ref)

    for index, value in enumerate(values):
        sums_ref[pl.ds(index, 1), :] += jnp.sum(value, axis=0, keepdims=True)


def attend_kernel(micros, parts, at_ref, *refs):
    pieces, placed = refs[: micros * parts], refs[micros * parts : micros * (parts + 1)]
    mine_ref, other_ref, vec_ref, heads_ref, norm_ref, scale_ref, first_ref, low_ref, w_ref = refs[
        micros * (parts + 1) :
    ]

    @pl.when(pl.program_id(0) == 0)
    def _():
        shards_, rows = mine_ref.shape[:2]
        for shard in range(shards_):
            for half, core in ((mine_ref, at_ref[parts]), (other_ref, 1 - at_ref[parts])):
                row = pl.multiple_of((2 * shard + core) * rows, rows)
                w_ref[pl.ds(row, rows), :] = half[shard]

    for m in range(micros):

        @pl.when(pl.program_id(0) == m)
        def _(m=m):
            total = placed[m][...].astype(F32) + vec_ref[0:1, :]
            for j in range(parts):
                piece = pieces[m * parts + j][...]
                cols = piece.shape[1]
                at = pl.multiple_of(at_ref[j] * cols, cols)
                total = total + product(piece, w_ref[pl.ds(at, cols), :])
                heads_ref[:, pl.ds(at, cols)] = piece
            norm, scale = normed(total)
            first = norm * vec_ref[1:2, :] + vec_ref[2:3, :]
            norm_ref[...] = norm
            scale_ref[...] = jnp.broadcast_to(scale, scale_ref.shape)
            first_ref[...] = first + vec_ref[3:4, :]
            low_ref[...] = first.astype(BF)


def attend(at, pieces, placed, w_mine, w_other, vectors):
    micros, parts = len(pieces), len(pieces[0])
    rows, width = placed[0].shape
    flat = [p for group in pieces for p in group]

    def out(cols, dtype):
        return jax.ShapeDtypeStruct((micros * rows, cols), dtype)

    return pl.pallas_call(
        functools.partial(attend_kernel, micros, parts),
        out_shape=(
            out(width, BF),
            out(width, F32),
            out(128, F32),
            out(width, F32),
            out(width, BF),
            jax.ShapeDtypeStruct((width, width), BF),
        ),
        grid_spec=pltpu.PrefetchScalarGridSpec(
            num_scalar_prefetch=1,
            grid=(micros,),
            in_specs=[whole_block(*a.shape) for a in (*flat, *placed, w_mine, w_other, vectors)],
            out_specs=tuple(
                pl.BlockSpec((rows, cols), lambda i, s: (i, 0)) for cols in (width, width, 128, width, width)
            )
            + (whole_block(width, width),),
        ),
        compiler_params=params(60),
        cost_estimate=cost(2 * micros * rows * width * width, 20 * micros * rows * width),
        name="attend",
    )(at, *flat, *placed, w_mine, w_other, vectors)


def second_norm_kernel(pre_ref, cot_ref, vec_ref, out_ref, d_ref, low_ref, sums_ref):
    norm, scale = normed(pre_ref[...])
    cot = cot_ref[...]
    out_ref[...] = (norm * vec_ref[0:1, :] + vec_ref[1:2, :]).astype(BF)
    d_pre = norm_backward(norm, scale, vec_ref[0:1, :], cot)
    d_ref[...] = d_pre
    low_ref[...] = d_pre.astype(BF)
    column_sums(sums_ref, d_pre, cot * norm, cot)


def second_norm(pre, cot, vectors):
    rows, width = pre.shape
    block = pl.BlockSpec((128, width), lambda i: (i, 0))
    return pl.pallas_call(
        second_norm_kernel,
        out_shape=(
            jax.ShapeDtypeStruct((rows, width), BF),
            jax.ShapeDtypeStruct((rows, width), F32),
            jax.ShapeDtypeStruct((rows, width), BF),
            jax.ShapeDtypeStruct((8, width), F32),
        ),
        grid=(rows // 128,),
        in_specs=[block, block, whole_block(*vectors.shape)],
        out_specs=(block, block, block, whole_block(8, width)),
        compiler_params=params(),
        cost_estimate=cost(30 * rows * width, 16 * rows * width),
        name="second_norm",
    )(pre, cot, vectors)


def attend_back_kernel(parts, at_ref, d_first_ref, norm_ref, scale_ref, vec_ref, w_ref, *refs):
    d_ref, low_ref, sums_ref = refs[:3]
    outs, low_all = refs[3:-1], refs[-1]
    d_first, norm = d_first_ref[...], norm_ref[...]
    d_pre = norm_backward(norm, scale_ref[:, 0:1], vec_ref[1:2, :], d_first)
    low = d_pre.astype(BF)
    d_ref[...] = d_pre
    low_ref[...] = low
    column_sums(sums_ref, d_pre, d_first * norm, d_first)
    rows = low.shape[0]
    step = pl.program_id(0)
    low_all[pl.ds(pl.multiple_of(step * rows, rows), rows), :] = low

    @pl.when(step == pl.num_programs(0) - 1)
    def _():
        for j in range(parts):
            cols = outs[j].shape[1]
            at = pl.multiple_of(at_ref[j] * cols, cols)
            outs[j][...] = against(low_all[...], w_ref[pl.ds(at, cols), :]).astype(BF)


def attend_back(at, d_first, norm, scale, vectors, w_out, parts):
    rows, width = d_first.shape
    split = 4
    block = pl.BlockSpec((rows // split, width), lambda i, s: (i, 0))
    piece = (rows, width // parts)
    return pl.pallas_call(
        functools.partial(attend_back_kernel, parts),
        out_shape=(
            jax.ShapeDtypeStruct((rows, width), F32),
            jax.ShapeDtypeStruct((rows, width), BF),
            jax.ShapeDtypeStruct((8, width), F32),
        )
        + (jax.ShapeDtypeStruct(piece, BF),) * parts,
        grid_spec=pltpu.PrefetchScalarGridSpec(
            num_scalar_prefetch=1,
            grid=(split,),
            in_specs=[
                block,
                block,
                pl.BlockSpec((rows // split, 128), lambda i, s: (i, 0)),
                whole_block(*vectors.shape),
                whole_block(*w_out.shape),
            ],
            out_specs=(block, block, whole_block(8, width)) + (whole_block(*piece),) * parts,
            scratch_shapes=[pltpu.VMEM((rows, width), BF)],
        ),
        compiler_params=params(),
        cost_estimate=cost(2 * rows * width * width, 20 * rows * width),
        name="attend_back",
    )(at, d_first, norm, scale, vectors, w_out)


def next_blocks(blocks, buf, sem):
    step = pl.program_id(0)

    def start(index, slot):
        for h in range(2):
            pltpu.make_async_copy(blocks[2 * index + h], buf.at[slot, h], sem.at[slot, h]).start()

    @pl.when(step == 0)
    def _():
        start(0, 0)

    for index in range(1, len(blocks) // 2):

        @pl.when(step + 1 == index)
        def _(index=index):
            start(index, index % 2)

    slot = step % 2
    for h in range(2):
        pltpu.make_async_copy(blocks[0], buf.at[slot, h], sem.at[slot, h]).wait()
    return [buf.at[slot, h] for h in range(2)]


def upper_tail(size, falling):
    t = 1.0 / (1.0 + (0.3275911 * 0.5**0.5) * size)
    series = 0.5 * 1.061405429 * t - 0.5 * 1.453152027
    series = series * t + 0.5 * 1.421413741
    series = series * t - 0.5 * 0.284496736
    series = series * t + 0.5 * 0.254829592
    return series * t * falling


def ff_forward_kernel(ff_half, count, first_ref, init_ref, *refs):
    sum_ref, hidden_ref, slope_ref, buf, sem = refs[-5:]
    cut = ff_half + PAD

    @pl.when(pl.program_id(0) == 0)
    def _():
        sum_ref[...] = init_ref[...]

    total = 0.0
    for h, block in enumerate(next_blocks(refs[:count], buf, sem)):
        bias = block[pl.ds(ff_half, PAD), pl.ds(0, ff_half)][0:1].astype(F32)
        upper = against(first_ref[...], block[pl.ds(0, ff_half), :]) + bias
        falling = jnp.exp(-0.5 * upper * upper)
        tail = upper_tail(jnp.abs(upper), falling)
        big_phi = jnp.where(upper > 0.0, 1.0 - tail, tail)
        hidden = (upper * big_phi).astype(BF)
        lanes = pl.ds(h * ff_half, ff_half)
        hidden_ref[:, lanes] = hidden
        slope_ref[:, lanes] = big_phi + upper * (falling * 0.3989422804014327)
        total = total + product(hidden, block[pl.ds(cut, ff_half), :])
    sum_ref[...] += total


def ff_forward(first_low, init, blocks, ff_half):
    rows, width = first_low.shape
    count = len(blocks)
    column = pl.BlockSpec((rows, 2 * ff_half), lambda i: (0, i))
    return pl.pallas_call(
        functools.partial(ff_forward_kernel, ff_half, count),
        out_shape=(
            jax.ShapeDtypeStruct((rows, width), F32),
            jax.ShapeDtypeStruct((rows, count * ff_half), BF),
            jax.ShapeDtypeStruct((rows, count * ff_half), F32),
        ),
        grid=(count // 2,),
        in_specs=[whole_block(rows, width)] * 2 + [pl.BlockSpec(memory_space=pl.ANY)] * count,
        out_specs=(whole_block(rows, width), column, column),
        scratch_shapes=[
            pltpu.VMEM((2, 2) + blocks[0].shape, BF),
            pltpu.SemaphoreType.DMA((2, 2)),
        ],
        compiler_params=params(),
        cost_estimate=cost(1, 1),
        name="ff_forward",
    )(first_low, init, *blocks)


def ff_backward_kernel(ff_half, count, base, d_fed_ref, init_ref, slope_ref, *refs):
    d_upper_ref, d_first_ref, column_ref, buf, sem = refs[-5:]
    cut = ff_half + PAD

    @pl.when(pl.program_id(0) == 0)
    def _():
        d_first_ref[...] = init_ref[...]
        column_ref[...] = refs[count][...]

    total = 0.0
    for h, block in enumerate(next_blocks(refs[:count], buf, sem)):
        lanes = pl.ds(h * ff_half, ff_half)
        d_hidden = against(d_fed_ref[...], block[pl.ds(cut, ff_half), :])
        d_upper = (d_hidden * slope_ref[:, lanes]).astype(BF)
        d_upper_ref[:, lanes] = d_upper
        row = base + 2 * pl.program_id(0) + h
        column_ref[pl.ds(row, 1), :] = jnp.sum(d_upper.astype(F32), axis=0, keepdims=True)
        total = total + product(d_upper, block[pl.ds(0, ff_half), :])
    d_first_ref[...] += total


def ff_backward(d_fed, init, slope, blocks, columns, base, ff_half):
    rows, width = d_fed.shape
    count = len(blocks)
    column = pl.BlockSpec((rows, 2 * ff_half), lambda i: (0, i))
    return pl.pallas_call(
        functools.partial(ff_backward_kernel, ff_half, count, base),
        out_shape=(
            jax.ShapeDtypeStruct(slope.shape, BF),
            jax.ShapeDtypeStruct((rows, width), F32),
            jax.ShapeDtypeStruct(columns.shape, F32),
        ),
        grid=(count // 2,),
        in_specs=[whole_block(rows, width)] * 2 + [column]
        + [pl.BlockSpec(memory_space=pl.ANY)] * count
        + [whole_block(*columns.shape)],
        out_specs=(column, whole_block(rows, width), whole_block(*columns.shape)),
        scratch_shapes=[
            pltpu.VMEM((2, 2) + blocks[0].shape, BF),
            pltpu.SemaphoreType.DMA((2, 2)),
        ],
        compiler_params=params(),
        cost_estimate=cost(
            4 * rows * width * ff_half * count,
            10 * rows * width + count * ff_half * (4 * width + 6 * rows),
        ),
        name="ff_backward",
    )(d_fed, init, slope, *blocks, columns)


def ff_grad_kernel(ff_half, spans, splits, joined, first_ref, fed_ref, up_ref, hidden_ref, *refs):
    count = len(spans)
    total = splits[-1]
    adds = list(refs[: sum(map(len, spans))])
    results = refs[len(adds) :]
    pieces = len(splits) - 1
    ups = over_rows(up_ref[...], first_ref[...])
    hiddens = over_rows(hidden_ref[...], fed_ref[...])
    for index in range(count):
        mine = [adds.pop(0) for _ in spans[index]]
        at = slice(index * ff_half, (index + 1) * ff_half)
        for low, high, share in ((0, ff_half, ups[at]), (ff_half, total, hiddens[at])):
            for (start, stop), add in zip(spans[index], mine):
                if start <= low and high <= stop:
                    share = share + add[pl.ds(low - start, high - low), :].astype(F32)
            for piece in range(pieces):
                if splits[piece] <= low and high <= splits[piece + 1]:
                    target = results[0 if joined else index * pieces + piece]
                    row = low - splits[piece] + joined * index * total
                    target[pl.ds(row, high - low), :] = share.astype(BF)


def ff_grad(d_upper, hidden, first_low, d_fed, place, adds, ff_half, cuts=(), joined=False, megabytes=24):
    rows, width = first_low.shape
    cols = width
    count = len(adds)
    total = 2 * ff_half
    splits = (0, *cuts, total)
    lanes = pl.BlockSpec((rows, cols), lambda i: (0, i))
    column = pl.BlockSpec((rows, count * ff_half), lambda i: (0, place))
    spans = tuple(tuple((start, start + height) for start, height, _, _ in arrived) for arrived in adds)
    flat = [add for arrived in adds for add in arrived]

    def lane_block(height, at=0):
        return pl.BlockSpec((height, cols), lambda i: (at, i))

    heights = [count * total] if joined else [b - a for a, b in zip(splits, splits[1:])] * count
    return pl.pallas_call(
        functools.partial(ff_grad_kernel, ff_half, spans, splits, int(joined)),
        out_shape=tuple(jax.ShapeDtypeStruct((height, width), BF) for height in heights),
        grid=(1,),
        in_specs=[lanes, lanes, column, column] + [lane_block(height, at) for _, height, _, at in flat],
        out_specs=tuple(lane_block(height) for height in heights),
        compiler_params=params(megabytes),
        cost_estimate=cost(1, 1),
        name="ff_grad",
    )(first_low, d_fed, d_upper, hidden, *[array for _, _, array, _ in flat])


def turn_kernel(in_ref, out_ref):
    out_ref[...] = in_ref[...].T


def turned(values):
    height, width = values.shape
    return pl.pallas_call(
        turn_kernel,
        out_shape=jax.ShapeDtypeStruct((width, height), values.dtype),
        grid=(1,),
        in_specs=[whole_block(height, width)],
        out_specs=whole_block(width, height),
        compiler_params=params(),
        cost_estimate=cost(1, 1),
        name="turned",
    )(values)


def combine_kernel(spans, *refs):
    arrays = list(refs[: sum(map(len, spans))])
    step = pl.program_id(0)
    for result, terms in zip(refs[len(arrays) :], spans):
        total = 0.0
        for low, high in terms:
            term = arrays.pop(0)[...].astype(F32)
            total = total + (term if (low, high) == terms[0] else jnp.where((low <= step) & (step < high), term, 0.0))
        result[...] = total.astype(BF)


def combine(*sums):
    height, width = sums[0][0][1].shape
    split = 2
    rows = height // split
    spans = tuple(tuple((low // rows, (low + array.shape[0]) // rows) for low, array in terms) for terms in sums)

    def row_block(low, high):
        return pl.BlockSpec((rows, width), lambda i: (jnp.clip(i - low, 0, high - low - 1), 0))

    return pl.pallas_call(
        functools.partial(combine_kernel, spans),
        out_shape=tuple(jax.ShapeDtypeStruct((height, width), BF) for _ in sums),
        grid=(split,),
        in_specs=[row_block(*span) for terms in spans for span in terms],
        out_specs=tuple(row_block(0, split) for _ in sums),
        compiler_params=params(),
        cost_estimate=cost(1, 1),
        name="combine",
    )(*[array for terms in sums for _, array in terms])


def diagonal_kernel(d_ref, w_ref, two_ref, one_ref):
    share = against(d_ref[...], w_ref[...]).astype(BF)
    half = two_ref.shape[0]
    two_ref[...] = share[:half]
    one_ref[...] = share[half:]


def diagonal_share(d_joint, w_seq, parts):
    rows, joint_width = d_joint.shape[0] // parts, d_joint.shape[1]
    width = w_seq.shape[0]
    half = (rows // 2, width)
    return pl.pallas_call(
        diagonal_kernel,
        out_shape=(jax.ShapeDtypeStruct(half, BF),) * 2,
        grid=(1,),
        in_specs=[pl.BlockSpec((rows, joint_width), lambda i: (parts - 1, 0)), whole_block(*w_seq.shape)],
        out_specs=(whole_block(*half),) * 2,
        compiler_params=params(),
        cost_estimate=cost(1, 1),
        name="diagonal_share",
    )(d_joint, w_seq)


def side_kernel(one_ref, two_ref, w_ref, to_two_ref, to_one_ref, via_one_ref, via_two_ref):
    half = to_two_ref.shape[0]
    share = against(one_ref[...], w_ref[...])
    via_one_ref[pl.ds(0, half), :] = (share[:half] + to_two_ref[...].astype(F32)).astype(BF)
    via_one_ref[pl.ds(half, half), :] = share[half:].astype(BF)
    share = against(two_ref[...], w_ref[...])
    via_two_ref[pl.ds(0, half), :] = share[:half].astype(BF)
    via_two_ref[pl.ds(half, half), :] = (share[half:] + to_one_ref[...].astype(F32)).astype(BF)


def side_shares(d_joint, w_seq, to_two, to_one, parts):
    rows, joint_width = d_joint.shape[0] // parts, d_joint.shape[1]
    width = w_seq.shape[0]
    return pl.pallas_call(
        side_kernel,
        out_shape=(jax.ShapeDtypeStruct((rows, width), BF),) * 2,
        grid=(1,),
        in_specs=[
            pl.BlockSpec((rows, joint_width), lambda i: (1, 0)),
            pl.BlockSpec((rows, joint_width), lambda i: (2, 0)),
            whole_block(*w_seq.shape),
            whole_block(*to_two.shape),
            whole_block(*to_one.shape),
        ],
        out_specs=(whole_block(rows, width),) * 2,
        compiler_params=params(),
        cost_estimate=cost(1, 1),
        name="side_shares",
    )(d_joint, d_joint, w_seq, to_two, to_one)


def row_grad_kernel(micros, d_pre_ref, w_ref, *refs):
    joints, arrived, out_ref = refs[:micros], refs[micros:-1], refs[-1]
    for m in range(micros):

        @pl.when(pl.program_id(0) == m)
        def _(m=m):
            total = d_pre_ref[...] + against(joints[m][...], w_ref[...])
            for term in arrived[2 * m : 2 * m + 2]:
                total = total + term[...].astype(F32)
            out_ref[...] = total


def row_grad(d_pre, w_seq, d_joints, arrived, parts):
    micros = len(d_joints)
    rows, joint_width = d_joints[0].shape[0] // parts, d_joints[0].shape[1]
    width = w_seq.shape[0]
    block = pl.BlockSpec((rows, width), lambda i: (i, 0))
    flat = [a for pair in arrived for a in pair]
    return pl.pallas_call(
        functools.partial(row_grad_kernel, micros),
        out_shape=jax.ShapeDtypeStruct(d_pre.shape, F32),
        grid=(micros,),
        in_specs=[block, whole_block(*w_seq.shape)]
        + [whole_block(rows, joint_width)] * micros
        + [whole_block(rows, width)] * len(flat),
        out_specs=block,
        compiler_params=params(),
        cost_estimate=cost(1, 1),
        name="row_grad",
    )(d_pre, w_seq, *d_joints, *flat)


def shards(
    embedded,
    token_table,
    masked_pos,
    replace_ids,
    w_query,
    b_query,
    w_key,
    w_value,
    b_value,
    w_out,
    b_out,
    ln1_gain,
    ln1_bias,
    w_up,
    b_up,
    w_down,
    b_down,
    ln2_gain,
    ln2_bias,
    grad_masked,
):
    rank = lax.axis_index("tensor")
    count = lax.axis_size("tensor")
    dp_count = lax.axis_size("dp")
    core = lax.axis_index("dp") % 2
    row_part = lax.axis_index("dp") // 2 % 2
    micro_count, row_count, width = embedded.shape
    local_width = w_query.shape[1]
    ff_local = w_up.shape[1]
    vocab_count = token_table.shape[0]
    parts = LEN // row_count
    groups = count // parts
    part = rank % parts
    group = rank // parts
    part_width = width // parts
    pairs = part_width // PAIR
    half_count = row_count // 2
    half_rows = width // 2
    ff_half = ff_local // 2
    out_half = local_width // 2
    cut = ff_half + PAD
    own_first = core == 0
    micros = range(micro_count)

    def by_core(mine, other, axis=0, first=None):
        return jnp.where(
            own_first if first is None else first,
            jnp.concatenate([mine, other], axis=axis),
            jnp.concatenate([other, mine], axis=axis),
        )

    order = list(range(0, count, 2)) + list(range(count - 1, 0, -2))
    ring_fw = [(order[i], order[(i + 1) % count]) for i in range(count)]
    ring_bw = [(b, a) for a, b in ring_fw]
    far = count // 2
    ring_pos = jnp.where(rank % 2 == 0, rank // 2, count - 1 - rank // 2)
    offsets = [0] + [sign * s for s in range(1, far) for sign in (-1, 1)] + [far]

    def forward(values):
        return lax.ppermute(values, "tensor", ring_fw)

    def backward(values):
        return lax.ppermute(values, "tensor", ring_bw)

    part_order = jnp.stack([part ^ j for j in range(parts)]).astype(jnp.int32)

    slot_pos = lax.dynamic_index_in_dim(masked_pos, group, 1, keepdims=False)
    slot_ids = lax.dynamic_index_in_dim(replace_ids, group, 1, keepdims=False)
    slot_grads = lax.dynamic_index_in_dim(grad_masked, group, 1, keepdims=False)
    vocab_iota = jnp.arange(vocab_count, dtype=jnp.int32)

    def replacement(positions, step):
        matches = positions[:, None] == slot_pos[step][None, :]
        replaced = jnp.any(matches, axis=1)
        row_ids = jnp.sum(jnp.where(matches, slot_ids[step][None, :], 0), axis=1)
        hot = (row_ids[:, None] == vocab_iota[None, :]) & replaced[:, None]
        return matches, replaced, hot

    row_iota = jnp.arange(row_count, dtype=jnp.int32)
    placed, replaced_list, hots, cots, seq_hots = [], [], [], [], []
    for step in micros:
        matches, replaced, hot = replacement(part * row_count + row_iota, step)
        inserted = product(hot.astype(BF), token_table)
        placed.append(jnp.where(replaced[:, None], inserted, embedded[step].astype(F32)).astype(BF))
        replaced_list.append(replaced)
        hots.append(hot.astype(F32))
        cots.append(product(matches.astype(BF), slot_grads[step]))
        seq_pos = jnp.concatenate([(part ^ j) * row_count + row_iota for j in range(parts)])
        seq_hot = replacement(seq_pos, step)[2].astype(BF)
        seq_hots.append(jnp.concatenate([seq_hot, jnp.ones_like(seq_hot[:, :2])], axis=1))

    joint_half = jnp.concatenate(
        [
            lax.dynamic_slice_in_dim(
                jnp.concatenate([w_query, w_key, w_value], axis=1), core * half_rows, half_rows, 0
            ),
            jnp.pad(
                jnp.concatenate([b_query, jnp.zeros_like(b_query), b_value])[None, :],
                ((0, PAD - 1), (0, 0)),
            ),
        ],
        axis=0,
    )
    spread = [
        [(groups * p + i, p + parts * ((i + k) % groups)) for p in range(parts) for i in range(groups)]
        for k in range(groups)
    ]
    piece = jnp.concatenate(
        [
            lax.dynamic_slice_in_dim(w_up.T, core * ff_half, ff_half, 0),
            jnp.pad(
                lax.dynamic_slice_in_dim(b_up, core * ff_half, ff_half, 0)[None, :],
                ((0, PAD - 1), (0, width - ff_half)),
            ),
            lax.dynamic_slice_in_dim(w_down, core * ff_half, ff_half, 0),
        ],
        axis=0,
    )

    w_mine = [lax.ppermute(joint_half, "tensor", spread[k]) for k in range(groups)]
    ones = [swap(placed[0], "tensor", 1)]
    twos = [swap(placed[0], "tensor", 2)]
    ones, twos, w_mine, placed, piece, cots, w_out, hots, seq_hots, replaced_list = fence(
        ones, twos, w_mine, placed, piece, cots, w_out, hots, seq_hots, replaced_list
    )
    w_out_half = lax.all_gather(
        lax.dynamic_slice_in_dim(w_out, core * out_half, out_half, 0), "tensor", axis=0
    )
    w_other = [swap(w, "dp", 1) for w in w_mine]
    w_seq, b_seq = assemble(
        jnp.stack([core] + [(group - i) % groups for i in range(groups)]).astype(jnp.int32),
        w_mine,
        w_other,
        local_width,
    )

    joints, x_mine, x_other, heads, log_sums, own_heads = [], [], [], [], [], []
    near = [piece[:cut], piece[cut:]]
    arrived = []
    at_core = core[None].astype(jnp.int32)
    for step in micros:
        threes = (swap(ones[step][:half_count], "tensor", 2), swap(twos[step][half_count:], "tensor", 1))
        rows = [placed[step], ones[step], twos[step], *threes]
        if step + 1 < micro_count:
            ones.append(swap(placed[step + 1], "tensor", 1))
            twos.append(swap(placed[step + 1], "tensor", 2))
        moved = (forward(near[step]), backward(near[step]))
        joint, mine, other = project(at_core, rows, w_seq, b_seq)
        pieces, whole, sums = attn_forward(joint, parts)
        joints.append(joint)
        log_sums.append(sums)
        own_heads.append(whole)
        x_mine.append(mine)
        x_other.append(other)
        ones, twos, moved, pieces, near = fence(ones, twos, moved, pieces, near)
        arrived.append(moved)
        heads.append([pieces[0]] + [swap(pieces[j], "tensor", j) for j in range(1, parts)])
    fw, bw = (jnp.concatenate([arrived[0][d], arrived[1][d]], axis=0) for d in range(2))
    heads, fw, bw, w_out_half = fence(heads, fw, bw, w_out_half)
    w_out_other = swap(w_out_half, "dp", 1)
    blocks = [piece, swap(piece, "dp", 1), fw, bw, swap(fw, "dp", 1), swap(bw, "dp", 1)]

    vectors_one = jnp.stack([b_out, ln1_gain, ln1_bias, b_down] + [b_out] * 4).astype(F32)
    heads_out, norm_one, scale_one, pre_two, first_low, w_out_all = attend(
        jnp.concatenate([part_order, at_core]), heads, placed, w_out_half, w_out_other, vectors_one
    )

    step_blocks = [blocks[:2], blocks[2:6]]
    hidden_low, slopes = [None] * (far + 1), [None] * (far + 1)
    for s in range(2, far + 1):
        if s < far:
            moved = [forward(fw), backward(bw)]
        else:
            moved = [forward(fw[:cut]), backward(bw[cut:])]
        for t in (0, 1) if s == 2 else (s - 1,):
            pre_two, hidden_low[t], slopes[t] = ff_forward(first_low, pre_two, step_blocks[t], ff_half)
        moved, pre_two = fence(moved, pre_two)
        if s == far:
            moved = [jnp.concatenate(moved, axis=0)]
        else:
            fw, bw = moved
        step_blocks.append(moved + [swap(block, "dp", 1) for block in moved])
    pre_two, hidden_low[far], slopes[far] = ff_forward(first_low, pre_two, step_blocks[far], ff_half)

    vectors_two = jnp.stack([ln2_gain, ln2_bias] + [ln2_bias] * 6).astype(F32)
    layer_out, d_pre_two, d_fed, sums_two = second_norm(pre_two, jnp.concatenate(cots, axis=0), vectors_two)
    total = 2 * ff_half

    def ff_blocks(offsets_, other, adds=None, cuts=(), megabytes=24):
        s = abs(offsets_[0])
        result = ff_grad(
            d_uppers[s], hidden_low[s], first_low, d_fed, other, adds or [[] for _ in offsets_], ff_half, cuts,
            bool(other), megabytes,
        )
        return result[0] if other else result

    def both(s):
        return [-s, s] if s else [0]

    def summed(s, others, megabytes=24):
        return ff_blocks(both(s), 0, [[(0, total, others, i)] for i in range(len(both(s)))], (), megabytes)

    d_uppers = [None] * (far + 1)
    rel_b_up = jnp.zeros((2 * count, ff_half), F32)

    def back(s, d_first):
        nonlocal rel_b_up
        base = 4 * s - 2 if s else 0
        d_uppers[s], d_first, rel_b_up = ff_backward(
            d_fed, d_first, slopes[s], step_blocks[s], rel_b_up, base, ff_half
        )
        return d_first

    d_first = back(far, d_pre_two)
    others = ff_blocks([far], 1)
    others, d_uppers[far], d_first = fence(others, d_uppers[far], d_first)
    others = swap(others, "dp", 1)
    d_first = back(far - 1, d_first)
    others, d_uppers[far], d_first = fence(others, d_uppers[far], d_first)
    parcel = ff_blocks([far], 0, [[(0, total, others, 0)]], (ff_half,))
    next_others = ff_blocks(both(far - 1), 1)
    parcel, next_others, d_uppers[far - 1], d_first = fence(parcel, next_others, d_uppers[far - 1], d_first)
    moved = [forward(parcel[0]), backward(parcel[1])]
    others = swap(next_others, "dp", 1)
    for s in range(far - 2, far // 2 - 1, -1):
        d_first = back(s, d_first)
    others, d_uppers[far - 1], d_first = fence(others, d_uppers[far - 1], d_first)
    share = summed(far - 1, others)
    next_others = ff_blocks(both(far - 2), 1)
    moved, share, next_others, d_first = fence(moved, share, next_others, d_first)
    parcel = combine([(0, share[0]), (ff_half, moved[1])], [(0, share[1]), (0, moved[0])])
    parcel, next_others, d_first = fence(parcel, next_others, d_first)
    moved = [forward(parcel[1]), backward(parcel[0])]
    others = swap(next_others, "dp", 1)
    for s in range(far // 2 - 1, -1, -1):
        d_first = back(s, d_first)
    d_pre_one, d_attended, sums_one, *d_heads = attend_back(
        part_order, d_first, norm_one, scale_one, vectors_one, w_out_all, parts
    )
    others, d_uppers[far - 2], d_heads = fence(others, d_uppers[far - 2], d_heads)
    seq_grads = [d_heads[0]] + [swap(d_heads[j], "tensor", j) for j in range(1, parts)]
    share = summed(far - 2, others)
    next_others = ff_blocks(both(far - 3), 1)

    d_out = over_rows(heads_out, d_attended).astype(BF).reshape(count, 2, out_half, width)
    out_other = lax.dynamic_index_in_dim(d_out, 1 - core, 1, keepdims=False).reshape(-1, width)
    out_mine = lax.dynamic_index_in_dim(d_out, core, 1, keepdims=False).reshape(-1, width)
    moved, share, seq_grads, next_others, out_other = fence(moved, share, seq_grads, next_others, out_other)
    seq_grads = jnp.concatenate(seq_grads, axis=0)

    d_joints = [jnp.zeros((), BF) for _ in micros]
    work = [(m, g) for m in micros for g in range(pairs)]

    def over_dp(values, bit=2):
        while bit < dp_count:
            values = (values.astype(F32) + swap(values, "dp", bit).astype(F32)).astype(BF)
            bit *= 2
        return values

    def diagonal(step):
        to_two, to_one = diagonal_share(d_joints[step], w_seq, parts)
        return (swap(to_two, "tensor", 2), swap(to_one, "tensor", 1))

    def side_parcels(step, arrived):
        return side_shares(d_joints[step], w_seq, *arrived, parts)

    def sides(parcels):
        return (swap(parcels[0], "tensor", 1), swap(parcels[1], "tensor", 2))

    def own_table(d_rows):
        return lax.dot_general(
            jnp.concatenate(hots, axis=0),
            d_rows,
            ROWS_DIMS,
            precision=lax.Precision.HIGHEST,
            preferred_element_type=F32,
        )

    partial, stage = [() for _ in micros], [0 for _ in micros]
    d_w = []
    table = own_table(d_pre_one)
    plan = [work[:pairs], work[pairs:-1], work[-1:]]
    for index in range(max(far - 1, len(plan))):
        s = far - 2 - index
        if s > 0:
            parcel = combine([(0, share[0]), (0, moved[1])], [(0, share[1]), (0, moved[0])])
            joints, d_joints, d_fed, parcel, next_others = fence(joints, d_joints, d_fed, parcel, next_others)
            moved = [forward(parcel[1]), backward(parcel[0])]
            others = swap(next_others, "dp", 1)
        elif s == 0:
            parcel = combine([(0, share[0]), (0, moved[0]), (0, moved[1])])[0]
            ff_up, ff_down = parcel[:ff_half], parcel[ff_half:]
            joints, d_joints, ff_up, ff_down = fence(joints, d_joints, ff_up, ff_down)
            ff_up = over_dp(ff_up)
        if index == 0:
            out_mine = (out_mine.astype(F32) + swap(out_other, "dp", 1).astype(F32)).astype(BF)
            out_mine = out_mine.reshape(count, 2, out_half // 2, width)
            out_other = lax.dynamic_index_in_dim(out_mine, 1 - row_part, 1, keepdims=False).reshape(-1, width)
            out_mine = lax.dynamic_index_in_dim(out_mine, row_part, 1, keepdims=False).reshape(-1, width)
            out_mine = (out_mine.astype(F32) + swap(out_other, "dp", 2).astype(F32)).astype(BF)
        elif index == 1:
            out_sum = lax.psum_scatter(out_mine, "tensor", scatter_dimension=0, tiled=True)
        for m in micros:
            ready = max(i for i, pairs_ in enumerate(plan) if (m, pairs - 1) in pairs_) + 1
            if index == ready:
                partial[m], stage[m] = diagonal(m), 1
            elif index == ready + 1:
                partial[m], stage[m] = sides(side_parcels(m, partial[m])), 2
        if index == len(plan) - 1:
            d_w = [(over_rows(x_other[m], d_joints[m]), over_rows(x_mine[m], d_joints[m])) for m in micros[:-1]]
        next_others = ()
        if s > 1:
            next_others = ff_blocks(both(s - 2), 1)
        for m, g in plan[index] if index < len(plan) else ():
            d_joints[m] = attn_backward(
                joints[m], log_sums[m], seq_grads, own_heads[m], parts, m, micro_count, g, (d_joints[m],) if g else ()
            )
        if s > 0:
            share = summed(s - 1, others)
            moved, share, next_others, d_joints, partial, table, d_w, out_mine = fence(
                moved, share, next_others, d_joints, partial, table, d_w, out_mine
            )
        elif s == 0:
            ff_up, d_joints, partial, table, d_w = fence(ff_up, d_joints, partial, table, d_w)

    last = micro_count - 1
    d_w.append((over_rows(x_other[last], d_joints[last]), None))
    other_half = sum(other for other, _ in d_w).astype(BF)
    other_half, d_joints, partial, ff_up, ff_down = fence(other_half, d_joints, partial, ff_up, ff_down)
    other_half = swap(other_half, "dp", 1)
    for m in micros:
        if stage[m] == 0:
            partial[m] = diagonal(m)
        elif stage[m] == 1:
            partial[m] = sides(side_parcels(m, partial[m]))

    def over_bits(values, axis, low, high):
        while low < high:
            bits = (low, 2 * low, 3 * low) if 2 * low < high else (low,)
            sent = values.astype(BF)
            terms = [sent.astype(F32)] + [swap(sent, axis, bit).astype(F32) for bit in bits]
            while len(terms) > 1:
                terms = [a + b for a, b in zip(terms[::2], terms[1::2])]
            values = terms[0]
            low *= 4
        return values

    row_offset, row_other = [0, 0], [0, 1]
    for s in range(1, far):
        row_offset += [-s % count, s, -s % count, s]
        row_other += [0, 0, 1, 1]
    row_offset, row_other = jnp.array(row_offset + [far, far]), jnp.array(row_other + [0, 1])
    place = jnp.repeat(jnp.array([order.index(i) for i in range(count)]), 2)
    half_of = jnp.tile(jnp.arange(2), count)
    chosen = (((place - ring_pos) % count)[:, None] == row_offset[None, :]) & (
        (half_of != core)[:, None] == (row_other[None, :] == 1)
    )
    all_b_up = jnp.dot(
        chosen.astype(F32), rel_b_up, precision=lax.Precision.HIGHEST, preferred_element_type=F32
    )
    all_b_up = jnp.pad(all_b_up, ((0, 0), (0, width - ff_half)))
    hot_sum = sum(over_rows(seq_hots[m], d_joints[m]) for m in micros)
    d_b_seq = hot_sum[vocab_count]
    rest, thirds = hot_sum, []
    for _ in range(3):
        thirds.append(rest.astype(BF))
        rest = rest - thirds[-1].astype(F32)
    table_rows = hot_sum.shape[0]
    shares = against(jnp.concatenate(thirds, axis=0), w_seq).reshape(3, table_rows, width)
    table = jnp.pad(table, ((0, table_rows - vocab_count), (0, 0))) + ((shares[2] + shares[1]) + shares[0])
    empty = jnp.zeros((width,), F32)
    d_b_query, d_b_value = (
        lax.dynamic_update_slice_in_dim(
            empty,
            jnp.concatenate([d_b_seq[(3 * g + a) * PAIR : (3 * g + a + 1) * PAIR] for g in range(pairs)]),
            part * part_width,
            0,
        )
        for a in (0, 2)
    )
    place_row = lax.broadcasted_iota(jnp.int32, table.shape, 0)
    table = jnp.where(place_row == vocab_count, d_b_query[None], table)
    table = jnp.where(place_row == vocab_count + 1, d_b_value[None], table)
    small = jnp.concatenate([table, sums_one, sums_two, all_b_up], axis=0)

    my_half = sum(mine for _, mine in d_w[: len(d_w)] if mine is not None)
    my_half = my_half + sum(over_rows(x_mine[m], d_joints[m]) for m in micros if d_w[m][1] is None)
    my_half = (my_half + other_half.astype(F32)).astype(BF)
    my_half, small, ff_up, ff_down, partial = fence(my_half, small, ff_up, ff_down, partial)

    if local_width != PAIR:
        columns = [
            jnp.concatenate(
                [my_half[:, (3 * g + a) * PAIR : (3 * g + a + 1) * PAIR] for g in range(pairs)], axis=1
            )
            for a in range(3)
        ]
        my_half = jnp.concatenate(
            [c[:, i * local_width : (i + 1) * local_width] for i in range(groups) for c in columns], axis=1
        )
    joint_sum = sum(
        lax.ppermute(
            lax.dynamic_slice_in_dim(
                my_half, (group - k) % groups * 3 * local_width, 3 * local_width, 1
            ),
            "tensor",
            [(b, a) for a, b in spread[k]],
        ).astype(F32)
        for k in range(groups)
    ).astype(BF)
    small = over_bits(small, "dp", 1, dp_count)
    ff_down = over_dp(ff_down)
    ff_up = turned(ff_up)
    up_other = swap(ff_up, "dp", 1)
    if stage[last] == 0:
        partial[last] = side_parcels(last, partial[last])
    grad_rows = row_grad(d_pre_one, w_seq, d_joints, partial[:last], parts)
    joint_sum, small, ff_up, ff_down, up_other, out_sum, partial[last], grad_rows = fence(
        joint_sum, small, ff_up, ff_down, up_other, out_sum, partial[last], grad_rows
    )

    joint_sum = over_dp(joint_sum)
    out_sum = over_dp(out_sum, 4)
    out_sum = by_core(out_sum, swap(out_sum, "dp", 2), 0, row_part == 0)
    down_other = swap(ff_down, "dp", 1)
    if stage[last] == 0:
        partial[last] = sides(partial[last])
    small = over_bits(small, "tensor", 1, min(4, count))
    grad_w_up = by_core(ff_up, up_other, 1).astype(F32)
    grad_w_down = by_core(ff_down, down_other).astype(F32)
    joint_sum, partial[last], out_sum, grad_w_up, grad_w_down = fence(
        joint_sum, partial[last], out_sum, grad_w_up, grad_w_down
    )
    out_other = swap(out_sum, "dp", 1)
    grad_w_out = by_core(out_sum, out_other).astype(F32)
    joint_other = swap(joint_sum, "dp", 1)
    small = over_bits(small, "tensor", 4, count)
    late = jnp.concatenate([partial[last][0], partial[last][1]], axis=1).astype(F32)
    late = late[:, :width] + late[:, width:]
    late = jnp.concatenate([jnp.zeros((row_count * last, width), F32), late], axis=0)
    grad_rows = jnp.where(jnp.concatenate(replaced_list)[:, None], 0.0, grad_rows + late)
    grad_query, grad_key, grad_value = (
        by_core(joint_sum[:, at : at + local_width], joint_other[:, at : at + local_width]).astype(F32)
        for at in (0, local_width, 2 * local_width)
    )
    grad_b_query, grad_b_value = (
        lax.dynamic_slice_in_dim(small[vocab_count + i], rank * local_width, local_width, 0) for i in range(2)
    )
    sums_at = (table_rows, table_rows + 8)
    grad_b_out, grad_gone, grad_bone, grad_b_down, grad_gtwo, grad_btwo = (
        small[at + i] for at in sums_at for i in range(3)
    )
    grad_b_up = lax.dynamic_slice_in_dim(small, table_rows + 16 + 2 * rank, 2, 0)[:, :ff_half].reshape(-1)

    return (
        layer_out.reshape(micro_count, row_count, width),
        grad_rows.reshape(micro_count, row_count, width),
        small[:vocab_count],
        grad_query,
        grad_b_query,
        grad_key,
        grad_value,
        grad_b_value,
        grad_w_out,
        grad_b_out,
        grad_gone,
        grad_bone,
        grad_w_up,
        grad_b_up,
        grad_w_down,
        grad_b_down,
        grad_gtwo,
        grad_btwo,
    )


def solution(mesh):
    return jax.shard_map(
        shards,
        mesh=mesh,
        in_specs=(
            P(None, ("dp", "tensor"), None),
            P(),
            P(None, "dp", None),
            P(None, "dp", None),
            P(None, "tensor"),
            P("tensor"),
            P(None, "tensor"),
            P(None, "tensor"),
            P("tensor"),
            P("tensor", None),
            P(),
            P(),
            P(),
            P(None, "tensor"),
            P("tensor"),
            P("tensor", None),
            P(),
            P(),
            P(),
            P(None, "dp", None, None),
        ),
        out_specs=(
            P(None, ("dp", "tensor"), None),
            P(None, ("dp", "tensor"), None),
            P(),
            P(None, "tensor"),
            P("tensor"),
            P(None, "tensor"),
            P(None, "tensor"),
            P("tensor"),
            P("tensor", None),
            P(),
            P(),
            P(),
            P(None, "tensor"),
            P("tensor"),
            P("tensor", None),
            P(),
            P(),
            P(),
        ),
        check_vma=False,
    )
```

```python
import functools

import jax
import jax.numpy as jnp
from jax import lax
from jax.experimental import pallas as pl
from jax.experimental.pallas import tpu as pltpu
from jax.sharding import PartitionSpec as P

HD = 64
LEN = 1024
EPSILON = 1e-12
SCALE = HD ** (-0.5)
ROWS_DIMS = (((0,), (0,)), ((), ()))
LAST_DIMS = (((1,), (1,)), ((), ()))
BF = jnp.bfloat16
F32 = jnp.float32
PAD = 16
PAIR = 2 * HD
LOG2E = 1.4426950408889634


def product(left_mat, right_mat):
    return jnp.dot(left_mat, right_mat, preferred_element_type=F32)


def over_rows(left_mat, right_mat):
    return lax.dot_general(left_mat, right_mat, ROWS_DIMS, preferred_element_type=F32)


def against(left_mat, right_mat):
    return lax.dot_general(left_mat, right_mat, LAST_DIMS, preferred_element_type=F32)


def swap(values, axis, bit):
    count = lax.axis_size(axis)
    return lax.ppermute(values, axis, [(i, i ^ bit) for i in range(count)])


def fence(*trees):
    return lax.optimization_barrier(trees)


def whole_block(*shape):
    return pl.BlockSpec(shape, lambda *_: (0,) * len(shape))


def params(megabytes=24):
    return pltpu.CompilerParams(vmem_limit_bytes=megabytes * 1024 * 1024)


def cost(flops, nbytes, transcendentals=0):
    return pl.CostEstimate(flops=flops, bytes_accessed=nbytes, transcendentals=transcendentals)


def assemble_kernel(groups, local, half, at_ref, *refs):
    mines, others = refs[:groups], refs[groups : 2 * groups]
    w_ref, b_ref = refs[2 * groups :]
    for i in range(groups):
        for k in range(groups):

            @pl.when(at_ref[1 + i] == k)
            def _(i=i, k=k):
                for a in range(3):
                    source = pl.ds(a * local, local)
                    lane = (3 * (i * local // PAIR) + a) * PAIR + i * local % PAIR
                    target = pl.ds(lane, local)
                    top = pl.multiple_of(at_ref[0] * half, half)
                    low = pl.multiple_of((1 - at_ref[0]) * half, half)
                    w_ref[pl.ds(top, half), target] = mines[k][pl.ds(0, half), source]
                    w_ref[pl.ds(low, half), target] = others[k][pl.ds(0, half), source]
                    b_ref[:, target] = mines[k][pl.ds(half, PAD), source][0:1].astype(F32)


def assemble(at, mines, others, local):
    groups = len(mines)
    half, width3 = others[0].shape[0] - PAD, others[0].shape[1]
    return pl.pallas_call(
        functools.partial(assemble_kernel, groups, local, half),
        out_shape=(
            jax.ShapeDtypeStruct((2 * half, groups * width3), BF),
            jax.ShapeDtypeStruct((1, groups * width3), F32),
        ),
        grid_spec=pltpu.PrefetchScalarGridSpec(
            num_scalar_prefetch=1,
            grid=(1,),
            in_specs=[whole_block(*m.shape) for m in (*mines, *others)],
            out_specs=(whole_block(2 * half, groups * width3), whole_block(1, groups * width3)),
        ),
        compiler_params=params(),
        cost_estimate=cost(0, 8 * half * groups * width3),
        name="assemble",
    )(at, *mines, *others)


def project_kernel(parts, at_ref, *refs):
    pieces = refs[: parts + 1]
    w_ref, b_ref, joint_ref, mine_ref, other_ref, x_ref = refs[parts + 1 :]
    step = pl.program_id(0)
    for j in range(parts - 1):

        @pl.when(step == j)
        def _(j=j):
            x_ref[...] = pieces[j][...]

    @pl.when(step == parts - 1)
    def _():
        rows = pieces[-1].shape[0]
        x_ref[pl.ds(0, rows), :] = pieces[-2][...]
        x_ref[pl.ds(rows, rows), :] = pieces[-1][...]

    joint_ref[...] = (product(x_ref[...], w_ref[...]) + b_ref[...]).astype(BF)
    half = mine_ref.shape[1]
    mine_ref[...] = x_ref[:, pl.ds(pl.multiple_of(at_ref[0] * half, half), half)]
    other_ref[...] = x_ref[:, pl.ds(pl.multiple_of((1 - at_ref[0]) * half, half), half)]


def project(at, pieces, w_seq, b_seq):
    parts = len(pieces) - 1
    rows, width = pieces[0].shape
    joint_width = w_seq.shape[1]
    half = jax.ShapeDtypeStruct((parts * rows, width // 2), BF)
    half_block = pl.BlockSpec((rows, width // 2), lambda i, s: (i, 0))
    return pl.pallas_call(
        functools.partial(project_kernel, parts),
        out_shape=(jax.ShapeDtypeStruct((parts * rows, joint_width), BF), half, half),
        grid_spec=pltpu.PrefetchScalarGridSpec(
            num_scalar_prefetch=1,
            grid=(parts,),
            in_specs=[whole_block(*p.shape) for p in pieces]
            + [whole_block(*w_seq.shape), whole_block(*b_seq.shape)],
            out_specs=(pl.BlockSpec((rows, joint_width), lambda i, s: (i, 0)), half_block, half_block),
            scratch_shapes=[pltpu.VMEM((rows, width), BF)],
        ),
        compiler_params=params(),
        cost_estimate=cost(2 * parts * rows * width * joint_width, 12 * parts * rows * width),
        name="project",
    )(at, *pieces, w_seq, b_seq)


def first_head(rows):
    return lax.broadcasted_iota(jnp.int32, (rows, PAIR), 1) < HD


def one_head(values, head, fill=0.0):
    first = first_head(values.shape[0])
    filled = jnp.full(values.shape, fill, values.dtype)
    return jnp.where(first, filled, values) if head else jnp.where(first, values, filled)


def attn_forward_kernel(q_ref, k_ref, v_ref, *refs):
    outs, all_ref, log_ref = refs[:-2], refs[-2], refs[-1]
    rows = q_ref.shape[0]
    mixed, log_sums = [], []
    scores = [against(one_head(q_ref[...], head), k_ref[...]) for head in range(2)]
    tops = [jnp.max(score, axis=-1, keepdims=True) * (SCALE * LOG2E) for score in scores]
    weights = [jnp.exp2(score * (SCALE * LOG2E) - top).astype(BF) for score, top in zip(scores, tops)]
    for head in range(2):
        both = product(weights[head], one_head(v_ref[...], head, 1.0))
        total = pltpu.roll(both, HD, 1)
        mixed.append(both / total)
        log_sums.append(tops[head] + jnp.log(total) * LOG2E)
    first = first_head(rows)
    value = jnp.where(first, mixed[0], mixed[1]).astype(BF)
    turned = jnp.where(first, log_sums[0], log_sums[1]).T
    log_ref[0, 0:1, :] = turned[0:1]
    log_ref[0, 1:2, :] = turned[HD : HD + 1]
    all_ref[...] = value
    for j, out in enumerate(outs):

        @pl.when(pl.program_id(1) == j)
        def _(out=out):
            out[...] = value


def attn_forward(joint, parts):
    rows = joint.shape[0] // parts
    pairs = joint.shape[1] // (3 * PAIR)
    shape = jax.ShapeDtypeStruct((rows, pairs * PAIR), BF)
    result = pl.pallas_call(
        attn_forward_kernel,
        out_shape=(shape,) * parts
        + (
            jax.ShapeDtypeStruct((parts * rows, pairs * PAIR), BF),
            jax.ShapeDtypeStruct((pairs, 8, parts * rows), F32),
        ),
        grid=(pairs, parts),
        in_specs=[
            pl.BlockSpec((rows, PAIR), lambda g, i: (i, 3 * g)),
            pl.BlockSpec((parts * rows, PAIR), lambda g, i: (0, 3 * g + 1)),
            pl.BlockSpec((parts * rows, PAIR), lambda g, i: (0, 3 * g + 2)),
        ],
        out_specs=(pl.BlockSpec((rows, PAIR), lambda g, i: (0, g)),) * parts
        + (pl.BlockSpec((rows, PAIR), lambda g, i: (i, g)), pl.BlockSpec((1, 8, rows), lambda g, i: (g, 0, i))),
        compiler_params=params(),
        cost_estimate=cost(
            16 * joint.shape[0] ** 2 * pairs * PAIR, 3 * joint.size, 2 * pairs * joint.shape[0] ** 2
        ),
        name="attn_forward",
    )(joint, joint, joint)
    return result[:parts], result[parts], result[parts + 1]


def attn_backward_kernel(parts, q_ref, k_ref, v_ref, log_ref, g_ref, o_ref, *refs):
    d_ref, kt_ref, dk_acc, dv_acc = refs[-4:]
    step = pl.program_id(0)
    rows = q_ref.shape[0]

    @pl.when(step == 0)
    def _():
        kt_ref[...] = k_ref[...].T
        dk_acc[...] = jnp.zeros_like(dk_acc)
        dv_acc[...] = jnp.zeros_like(dv_acc)

    row_dots = (g_ref[...].astype(F32) * o_ref[...].astype(F32)).T
    dq_parts = []
    for head in range(2):
        queries = one_head(q_ref[...], head)
        grads = one_head(g_ref[...], head)
        row_dot = jnp.sum(row_dots[head * HD : (head + 1) * HD], axis=0, keepdims=True)
        log_sum = log_ref[0, pl.ds(head, 1), :]
        scores = against(k_ref[...], queries)
        probs = jnp.exp2(scores * (SCALE * LOG2E) - log_sum)
        d_probs = against(v_ref[...], grads)
        d_scores = (probs * (d_probs - row_dot)).astype(BF)
        dv_acc[...] += product(probs.astype(BF), grads)
        dk_acc[...] += product(d_scores, queries)
        dq_parts.append(product(kt_ref[pl.ds(head * HD, HD), :], d_scores))
    d_ref[pl.ds(step * rows, rows), pl.ds(0, PAIR)] = (
        jnp.concatenate(dq_parts, axis=0).T * SCALE
    ).astype(BF)

    @pl.when(step == parts - 1)
    def _():
        d_ref[:, pl.ds(PAIR, PAIR)] = (dk_acc[...] * SCALE).astype(BF)
        d_ref[:, pl.ds(2 * PAIR, PAIR)] = dv_acc[...].astype(BF)


def attn_backward(joint, log_sums, grads, heads, parts, step, micros, pair, kept):
    rows = joint.shape[0] // parts
    return pl.pallas_call(
        functools.partial(attn_backward_kernel, parts),
        out_shape=jax.ShapeDtypeStruct(joint.shape, BF),
        grid=(parts,),
        in_specs=[
            pl.BlockSpec((rows, PAIR), lambda i: (i, 3 * pair)),
            pl.BlockSpec((parts * rows, PAIR), lambda i: (0, 3 * pair + 1)),
            pl.BlockSpec((parts * rows, PAIR), lambda i: (0, 3 * pair + 2)),
            pl.BlockSpec((1, 8, rows), lambda i: (pair, 0, i)),
            pl.BlockSpec((rows, PAIR), lambda i: (i * micros + step, pair)),
            pl.BlockSpec((rows, PAIR), lambda i: (i, pair)),
        ]
        + [pl.BlockSpec(memory_space=pl.ANY)] * len(kept),
        out_specs=pl.BlockSpec((parts * rows, 3 * PAIR), lambda i: (0, pair)),
        scratch_shapes=[
            pltpu.VMEM((PAIR, parts * rows), BF),
            pltpu.VMEM((parts * rows, PAIR), F32),
            pltpu.VMEM((parts * rows, PAIR), F32),
        ],
        input_output_aliases={6 + i: i for i in range(len(kept))},
        compiler_params=params(),
        cost_estimate=cost(1, 1),
        name="attn_backward",
    )(joint, joint, joint, log_sums, grads, heads, *kept)


def normed(values):
    row_mean = jnp.mean(values, axis=-1, keepdims=True)
    centred = values - row_mean
    row_var = jnp.mean(centred * centred, axis=-1, keepdims=True)
    scale = lax.rsqrt(row_var + EPSILON)
    return centred * scale, scale


def norm_backward(norm, scale, gain_vec, grads):
    d_norm = grads * gain_vec
    mean_d = jnp.mean(d_norm, axis=-1, keepdims=True)
    mean_dn = jnp.mean(d_norm * norm, axis=-1, keepdims=True)
    return (d_norm - mean_d - norm * mean_dn) * scale


def column_sums(sums_ref, *values):
    @pl.when(pl.program_id(0) == 0)
    def _():
        sums_ref[...] = jnp.zeros_like(sums_ref)

    for index, value in enumerate(values):
        sums_ref[pl.ds(index, 1), :] += jnp.sum(value, axis=0, keepdims=True)


def attend_kernel(micros, parts, at_ref, *refs):
    pieces, placed = refs[: micros * parts], refs[micros * parts : micros * (parts + 1)]
    mine_ref, other_ref, vec_ref, heads_ref, norm_ref, scale_ref, first_ref, low_ref, w_ref = refs[
        micros * (parts + 1) :
    ]

    @pl.when(pl.program_id(0) == 0)
    def _():
        shards_, rows = mine_ref.shape[:2]
        for shard in range(shards_):
            for half, core in ((mine_ref, at_ref[parts]), (other_ref, 1 - at_ref[parts])):
                row = pl.multiple_of((2 * shard + core) * rows, rows)
                w_ref[pl.ds(row, rows), :] = half[shard]

    for m in range(micros):

        @pl.when(pl.program_id(0) == m)
        def _(m=m):
            total = placed[m][...].astype(F32) + vec_ref[0:1, :]
            for j in range(parts):
                piece = pieces[m * parts + j][...]
                cols = piece.shape[1]
                at = pl.multiple_of(at_ref[j] * cols, cols)
                total = total + product(piece, w_ref[pl.ds(at, cols), :])
                heads_ref[:, pl.ds(at, cols)] = piece
            norm, scale = normed(total)
            first = norm * vec_ref[1:2, :] + vec_ref[2:3, :]
            norm_ref[...] = norm
            scale_ref[...] = jnp.broadcast_to(scale, scale_ref.shape)
            first_ref[...] = first + vec_ref[3:4, :]
            low_ref[...] = first.astype(BF)


def attend(at, pieces, placed, w_mine, w_other, vectors):
    micros, parts = len(pieces), len(pieces[0])
    rows, width = placed[0].shape
    flat = [p for group in pieces for p in group]

    def out(cols, dtype):
        return jax.ShapeDtypeStruct((micros * rows, cols), dtype)

    return pl.pallas_call(
        functools.partial(attend_kernel, micros, parts),
        out_shape=(
            out(width, BF),
            out(width, F32),
            out(128, F32),
            out(width, F32),
            out(width, BF),
            jax.ShapeDtypeStruct((width, width), BF),
        ),
        grid_spec=pltpu.PrefetchScalarGridSpec(
            num_scalar_prefetch=1,
            grid=(micros,),
            in_specs=[whole_block(*a.shape) for a in (*flat, *placed, w_mine, w_other, vectors)],
            out_specs=tuple(
                pl.BlockSpec((rows, cols), lambda i, s: (i, 0)) for cols in (width, width, 128, width, width)
            )
            + (whole_block(width, width),),
        ),
        compiler_params=params(60),
        cost_estimate=cost(2 * micros * rows * width * width, 20 * micros * rows * width),
        name="attend",
    )(at, *flat, *placed, w_mine, w_other, vectors)


def second_norm_kernel(pre_ref, cot_ref, vec_ref, out_ref, d_ref, low_ref, sums_ref):
    norm, scale = normed(pre_ref[...])
    cot = cot_ref[...]
    out_ref[...] = (norm * vec_ref[0:1, :] + vec_ref[1:2, :]).astype(BF)
    d_pre = norm_backward(norm, scale, vec_ref[0:1, :], cot)
    d_ref[...] = d_pre
    low_ref[...] = d_pre.astype(BF)
    column_sums(sums_ref, d_pre, cot * norm, cot)


def second_norm(pre, cot, vectors):
    rows, width = pre.shape
    block = pl.BlockSpec((rows // 2, width), lambda i: (i, 0))
    return pl.pallas_call(
        second_norm_kernel,
        out_shape=(
            jax.ShapeDtypeStruct((rows, width), BF),
            jax.ShapeDtypeStruct((rows, width), F32),
            jax.ShapeDtypeStruct((rows, width), BF),
            jax.ShapeDtypeStruct((8, width), F32),
        ),
        grid=(2,),
        in_specs=[block, block, whole_block(*vectors.shape)],
        out_specs=(block, block, block, whole_block(8, width)),
        compiler_params=params(),
        cost_estimate=cost(30 * rows * width, 16 * rows * width),
        name="second_norm",
    )(pre, cot, vectors)


def attend_back_kernel(parts, at_ref, d_first_ref, norm_ref, scale_ref, vec_ref, w_ref, *refs):
    d_ref, low_ref, sums_ref = refs[:3]
    outs, low_all = refs[3:-1], refs[-1]
    d_first, norm = d_first_ref[...], norm_ref[...]
    d_pre = norm_backward(norm, scale_ref[:, 0:1], vec_ref[1:2, :], d_first)
    low = d_pre.astype(BF)
    d_ref[...] = d_pre
    low_ref[...] = low
    column_sums(sums_ref, d_pre, d_first * norm, d_first)
    rows = low.shape[0]
    step = pl.program_id(0)
    low_all[pl.ds(pl.multiple_of(step * rows, rows), rows), :] = low

    @pl.when(step == pl.num_programs(0) - 1)
    def _():
        for j in range(parts):
            cols = outs[j].shape[1]
            at = pl.multiple_of(at_ref[j] * cols, cols)
            outs[j][...] = against(low_all[...], w_ref[pl.ds(at, cols), :]).astype(BF)


def attend_back(at, d_first, norm, scale, vectors, w_out, parts):
    rows, width = d_first.shape
    split = 2
    block = pl.BlockSpec((rows // split, width), lambda i, s: (i, 0))
    piece = (rows, width // parts)
    return pl.pallas_call(
        functools.partial(attend_back_kernel, parts),
        out_shape=(
            jax.ShapeDtypeStruct((rows, width), F32),
            jax.ShapeDtypeStruct((rows, width), BF),
            jax.ShapeDtypeStruct((8, width), F32),
        )
        + (jax.ShapeDtypeStruct(piece, BF),) * parts,
        grid_spec=pltpu.PrefetchScalarGridSpec(
            num_scalar_prefetch=1,
            grid=(split,),
            in_specs=[
                block,
                block,
                pl.BlockSpec((rows // split, 128), lambda i, s: (i, 0)),
                whole_block(*vectors.shape),
                whole_block(*w_out.shape),
            ],
            out_specs=(block, block, whole_block(8, width)) + (whole_block(*piece),) * parts,
            scratch_shapes=[pltpu.VMEM((rows, width), BF)],
        ),
        compiler_params=params(),
        cost_estimate=cost(2 * rows * width * width, 20 * rows * width),
        name="attend_back",
    )(at, d_first, norm, scale, vectors, w_out)


def next_blocks(blocks, buf, sem):
    step = pl.program_id(0)

    def start(index, slot):
        for h in range(2):
            pltpu.make_async_copy(blocks[2 * index + h], buf.at[slot, h], sem.at[slot, h]).start()

    @pl.when(step == 0)
    def _():
        start(0, 0)

    for index in range(1, len(blocks) // 2):

        @pl.when(step + 1 == index)
        def _(index=index):
            start(index, index % 2)

    slot = step % 2
    for h in range(2):
        pltpu.make_async_copy(blocks[0], buf.at[slot, h], sem.at[slot, h]).wait()
    return [buf.at[slot, h] for h in range(2)]


def upper_tail(size, falling):
    t = 1.0 / (1.0 + (0.3275911 * 0.5**0.5) * size)
    series = 0.5 * 1.061405429 * t - 0.5 * 1.453152027
    series = series * t + 0.5 * 1.421413741
    series = series * t - 0.5 * 0.284496736
    series = series * t + 0.5 * 0.254829592
    return series * t * falling


def ff_forward_kernel(ff_half, count, first_ref, init_ref, *refs):
    sum_ref, hidden_ref, slope_ref, buf, sem = refs[-5:]
    cut = ff_half + PAD

    @pl.when(pl.program_id(0) == 0)
    def _():
        sum_ref[...] = init_ref[...]

    total = 0.0
    for h, block in enumerate(next_blocks(refs[:count], buf, sem)):
        bias = block[pl.ds(ff_half, PAD), pl.ds(0, ff_half)][0:1].astype(F32)
        upper = against(first_ref[...], block[pl.ds(0, ff_half), :]) + bias
        falling = jnp.exp(-0.5 * upper * upper)
        tail = upper_tail(jnp.abs(upper), falling)
        big_phi = jnp.where(upper > 0.0, 1.0 - tail, tail)
        hidden = (upper * big_phi).astype(BF)
        lanes = pl.ds(h * ff_half, ff_half)
        hidden_ref[:, lanes] = hidden
        slope_ref[:, lanes] = big_phi + upper * (falling * 0.3989422804014327)
        total = total + product(hidden, block[pl.ds(cut, ff_half), :])
    sum_ref[...] += total


def ff_forward(first_low, init, blocks, ff_half):
    rows, width = first_low.shape
    count = len(blocks)
    column = pl.BlockSpec((rows, 2 * ff_half), lambda i: (0, i))
    return pl.pallas_call(
        functools.partial(ff_forward_kernel, ff_half, count),
        out_shape=(
            jax.ShapeDtypeStruct((rows, width), F32),
            jax.ShapeDtypeStruct((rows, count * ff_half), BF),
            jax.ShapeDtypeStruct((rows, count * ff_half), F32),
        ),
        grid=(count // 2,),
        in_specs=[whole_block(rows, width)] * 2 + [pl.BlockSpec(memory_space=pl.ANY)] * count,
        out_specs=(whole_block(rows, width), column, column),
        scratch_shapes=[
            pltpu.VMEM((2, 2) + blocks[0].shape, BF),
            pltpu.SemaphoreType.DMA((2, 2)),
        ],
        compiler_params=params(),
        cost_estimate=cost(1, 1),
        name="ff_forward",
    )(first_low, init, *blocks)


def ff_backward_kernel(ff_half, count, base, d_fed_ref, init_ref, slope_ref, *refs):
    d_upper_ref, d_first_ref, column_ref, buf, sem = refs[-5:]
    cut = ff_half + PAD

    @pl.when(pl.program_id(0) == 0)
    def _():
        d_first_ref[...] = init_ref[...]
        column_ref[...] = refs[count][...]

    total = 0.0
    for h, block in enumerate(next_blocks(refs[:count], buf, sem)):
        lanes = pl.ds(h * ff_half, ff_half)
        d_hidden = against(d_fed_ref[...], block[pl.ds(cut, ff_half), :])
        d_upper = (d_hidden * slope_ref[:, lanes]).astype(BF)
        d_upper_ref[:, lanes] = d_upper
        row = base + 2 * pl.program_id(0) + h
        column_ref[pl.ds(row, 1), :] = jnp.sum(d_upper.astype(F32), axis=0, keepdims=True)
        total = total + product(d_upper, block[pl.ds(0, ff_half), :])
    d_first_ref[...] += total


def ff_backward(d_fed, init, slope, blocks, columns, base, ff_half):
    rows, width = d_fed.shape
    count = len(blocks)
    column = pl.BlockSpec((rows, 2 * ff_half), lambda i: (0, i))
    return pl.pallas_call(
        functools.partial(ff_backward_kernel, ff_half, count, base),
        out_shape=(
            jax.ShapeDtypeStruct(slope.shape, BF),
            jax.ShapeDtypeStruct((rows, width), F32),
            jax.ShapeDtypeStruct(columns.shape, F32),
        ),
        grid=(count // 2,),
        in_specs=[whole_block(rows, width)] * 2 + [column]
        + [pl.BlockSpec(memory_space=pl.ANY)] * count
        + [whole_block(*columns.shape)],
        out_specs=(column, whole_block(rows, width), whole_block(*columns.shape)),
        scratch_shapes=[
            pltpu.VMEM((2, 2) + blocks[0].shape, BF),
            pltpu.SemaphoreType.DMA((2, 2)),
        ],
        compiler_params=params(),
        cost_estimate=cost(
            4 * rows * width * ff_half * count,
            10 * rows * width + count * ff_half * (4 * width + 6 * rows),
        ),
        name="ff_backward",
    )(d_fed, init, slope, *blocks, columns)


def ff_grad_kernel(ff_half, spans, splits, joined, first_ref, fed_ref, up_ref, hidden_ref, *refs):
    count = len(spans)
    total = splits[-1]
    adds = list(refs[: sum(map(len, spans))])
    results = refs[len(adds) :]
    pieces = len(splits) - 1
    ups = over_rows(up_ref[...], first_ref[...])
    hiddens = over_rows(hidden_ref[...], fed_ref[...])
    for index in range(count):
        mine = [adds.pop(0) for _ in spans[index]]
        at = slice(index * ff_half, (index + 1) * ff_half)
        for low, high, share in ((0, ff_half, ups[at]), (ff_half, total, hiddens[at])):
            for (start, stop), add in zip(spans[index], mine):
                if start <= low and high <= stop:
                    share = share + add[pl.ds(low - start, high - low), :].astype(F32)
            for piece in range(pieces):
                if splits[piece] <= low and high <= splits[piece + 1]:
                    target = results[0 if joined else index * pieces + piece]
                    row = low - splits[piece] + joined * index * total
                    target[pl.ds(row, high - low), :] = share.astype(BF)


def ff_grad(d_upper, hidden, first_low, d_fed, place, adds, ff_half, cuts=(), joined=False, megabytes=24):
    rows, width = first_low.shape
    cols = width
    count = len(adds)
    total = 2 * ff_half
    splits = (0, *cuts, total)
    lanes = pl.BlockSpec((rows, cols), lambda i: (0, i))
    column = pl.BlockSpec((rows, count * ff_half), lambda i: (0, place))
    spans = tuple(tuple((start, start + height) for start, height, _, _ in arrived) for arrived in adds)
    flat = [add for arrived in adds for add in arrived]

    def lane_block(height, at=0):
        return pl.BlockSpec((height, cols), lambda i: (at, i))

    heights = [count * total] if joined else [b - a for a, b in zip(splits, splits[1:])] * count
    return pl.pallas_call(
        functools.partial(ff_grad_kernel, ff_half, spans, splits, int(joined)),
        out_shape=tuple(jax.ShapeDtypeStruct((height, width), BF) for height in heights),
        grid=(1,),
        in_specs=[lanes, lanes, column, column] + [lane_block(height, at) for _, height, _, at in flat],
        out_specs=tuple(lane_block(height) for height in heights),
        compiler_params=params(megabytes),
        cost_estimate=cost(1, 1),
        name="ff_grad",
    )(first_low, d_fed, d_upper, hidden, *[array for _, _, array, _ in flat])


def turn_kernel(in_ref, out_ref):
    out_ref[...] = in_ref[...].T


def turned(values):
    height, width = values.shape
    return pl.pallas_call(
        turn_kernel,
        out_shape=jax.ShapeDtypeStruct((width, height), values.dtype),
        grid=(1,),
        in_specs=[whole_block(height, width)],
        out_specs=whole_block(width, height),
        compiler_params=params(),
        cost_estimate=cost(1, 1),
        name="turned",
    )(values)


def combine_kernel(spans, *refs):
    arrays = list(refs[: sum(map(len, spans))])
    step = pl.program_id(0)
    for result, terms in zip(refs[len(arrays) :], spans):
        total = 0.0
        for low, high in terms:
            term = arrays.pop(0)[...].astype(F32)
            total = total + (term if (low, high) == terms[0] else jnp.where((low <= step) & (step < high), term, 0.0))
        result[...] = total.astype(BF)


def combine(*sums):
    height, width = sums[0][0][1].shape
    split = 2
    rows = height // split
    spans = tuple(tuple((low // rows, (low + array.shape[0]) // rows) for low, array in terms) for terms in sums)

    def row_block(low, high):
        return pl.BlockSpec((rows, width), lambda i: (jnp.clip(i - low, 0, high - low - 1), 0))

    return pl.pallas_call(
        functools.partial(combine_kernel, spans),
        out_shape=tuple(jax.ShapeDtypeStruct((height, width), BF) for _ in sums),
        grid=(split,),
        in_specs=[row_block(*span) for terms in spans for span in terms],
        out_specs=tuple(row_block(0, split) for _ in sums),
        compiler_params=params(),
        cost_estimate=cost(1, 1),
        name="combine",
    )(*[array for terms in sums for _, array in terms])


def diagonal_kernel(d_ref, w_ref, two_ref, one_ref):
    share = against(d_ref[...], w_ref[...]).astype(BF)
    half = two_ref.shape[0]
    two_ref[...] = share[:half]
    one_ref[...] = share[half:]


def diagonal_share(d_joint, w_seq, parts):
    rows, joint_width = d_joint.shape[0] // parts, d_joint.shape[1]
    width = w_seq.shape[0]
    half = (rows // 2, width)
    return pl.pallas_call(
        diagonal_kernel,
        out_shape=(jax.ShapeDtypeStruct(half, BF),) * 2,
        grid=(1,),
        in_specs=[pl.BlockSpec((rows, joint_width), lambda i: (parts - 1, 0)), whole_block(*w_seq.shape)],
        out_specs=(whole_block(*half),) * 2,
        compiler_params=params(),
        cost_estimate=cost(1, 1),
        name="diagonal_share",
    )(d_joint, w_seq)


def side_kernel(one_ref, two_ref, w_ref, to_two_ref, to_one_ref, via_one_ref, via_two_ref):
    half = to_two_ref.shape[0]
    share = against(one_ref[...], w_ref[...])
    via_one_ref[pl.ds(0, half), :] = (share[:half] + to_two_ref[...].astype(F32)).astype(BF)
    via_one_ref[pl.ds(half, half), :] = share[half:].astype(BF)
    share = against(two_ref[...], w_ref[...])
    via_two_ref[pl.ds(0, half), :] = share[:half].astype(BF)
    via_two_ref[pl.ds(half, half), :] = (share[half:] + to_one_ref[...].astype(F32)).astype(BF)


def side_shares(d_joint, w_seq, to_two, to_one, parts):
    rows, joint_width = d_joint.shape[0] // parts, d_joint.shape[1]
    width = w_seq.shape[0]
    return pl.pallas_call(
        side_kernel,
        out_shape=(jax.ShapeDtypeStruct((rows, width), BF),) * 2,
        grid=(1,),
        in_specs=[
            pl.BlockSpec((rows, joint_width), lambda i: (1, 0)),
            pl.BlockSpec((rows, joint_width), lambda i: (2, 0)),
            whole_block(*w_seq.shape),
            whole_block(*to_two.shape),
            whole_block(*to_one.shape),
        ],
        out_specs=(whole_block(rows, width),) * 2,
        compiler_params=params(),
        cost_estimate=cost(1, 1),
        name="side_shares",
    )(d_joint, d_joint, w_seq, to_two, to_one)


def row_grad_kernel(micros, d_pre_ref, w_ref, *refs):
    joints, arrived, out_ref = refs[:micros], refs[micros:-1], refs[-1]
    for m in range(micros):

        @pl.when(pl.program_id(0) == m)
        def _(m=m):
            total = d_pre_ref[...] + against(joints[m][...], w_ref[...])
            for term in arrived[2 * m : 2 * m + 2]:
                total = total + term[...].astype(F32)
            out_ref[...] = total


def row_grad(d_pre, w_seq, d_joints, arrived, parts):
    micros = len(d_joints)
    rows, joint_width = d_joints[0].shape[0] // parts, d_joints[0].shape[1]
    width = w_seq.shape[0]
    block = pl.BlockSpec((rows, width), lambda i: (i, 0))
    flat = [a for pair in arrived for a in pair]
    return pl.pallas_call(
        functools.partial(row_grad_kernel, micros),
        out_shape=jax.ShapeDtypeStruct(d_pre.shape, F32),
        grid=(micros,),
        in_specs=[block, whole_block(*w_seq.shape)]
        + [whole_block(rows, joint_width)] * micros
        + [whole_block(rows, width)] * len(flat),
        out_specs=block,
        compiler_params=params(),
        cost_estimate=cost(1, 1),
        name="row_grad",
    )(d_pre, w_seq, *d_joints, *flat)


def shards(
    embedded,
    token_table,
    masked_pos,
    replace_ids,
    w_query,
    b_query,
    w_key,
    w_value,
    b_value,
    w_out,
    b_out,
    ln1_gain,
    ln1_bias,
    w_up,
    b_up,
    w_down,
    b_down,
    ln2_gain,
    ln2_bias,
    grad_masked,
):
    rank = lax.axis_index("tensor")
    count = lax.axis_size("tensor")
    dp_count = lax.axis_size("dp")
    core = lax.axis_index("dp") % 2
    row_part = lax.axis_index("dp") // 2 % 2
    micro_count, row_count, width = embedded.shape
    local_width = w_query.shape[1]
    ff_local = w_up.shape[1]
    vocab_count = token_table.shape[0]
    parts = LEN // row_count
    groups = count // parts
    part = rank % parts
    group = rank // parts
    part_width = width // parts
    pairs = part_width // PAIR
    half_count = row_count // 2
    half_rows = width // 2
    ff_half = ff_local // 2
    out_half = local_width // 2
    cut = ff_half + PAD
    own_first = core == 0
    micros = range(micro_count)

    def by_core(mine, other, axis=0, first=None):
        return jnp.where(
            own_first if first is None else first,
            jnp.concatenate([mine, other], axis=axis),
            jnp.concatenate([other, mine], axis=axis),
        )

    order = list(range(0, count, 2)) + list(range(count - 1, 0, -2))
    ring_fw = [(order[i], order[(i + 1) % count]) for i in range(count)]
    ring_bw = [(b, a) for a, b in ring_fw]
    far = count // 2
    ring_pos = jnp.where(rank % 2 == 0, rank // 2, count - 1 - rank // 2)
    offsets = [0] + [sign * s for s in range(1, far) for sign in (-1, 1)] + [far]

    def forward(values):
        return lax.ppermute(values, "tensor", ring_fw)

    def backward(values):
        return lax.ppermute(values, "tensor", ring_bw)

    part_order = jnp.stack([part ^ j for j in range(parts)]).astype(jnp.int32)

    slot_pos = lax.dynamic_index_in_dim(masked_pos, group, 1, keepdims=False)
    slot_ids = lax.dynamic_index_in_dim(replace_ids, group, 1, keepdims=False)
    slot_grads = lax.dynamic_index_in_dim(grad_masked, group, 1, keepdims=False)
    vocab_iota = jnp.arange(vocab_count, dtype=jnp.int32)

    def replacement(positions, step):
        matches = positions[:, None] == slot_pos[step][None, :]
        replaced = jnp.any(matches, axis=1)
        row_ids = jnp.sum(jnp.where(matches, slot_ids[step][None, :], 0), axis=1)
        hot = (row_ids[:, None] == vocab_iota[None, :]) & replaced[:, None]
        return matches, replaced, hot

    row_iota = jnp.arange(row_count, dtype=jnp.int32)
    placed, replaced_list, hots, cots, seq_hots = [], [], [], [], []
    for step in micros:
        matches, replaced, hot = replacement(part * row_count + row_iota, step)
        inserted = product(hot.astype(BF), token_table)
        placed.append(jnp.where(replaced[:, None], inserted, embedded[step].astype(F32)).astype(BF))
        replaced_list.append(replaced)
        hots.append(hot.astype(F32))
        cots.append(product(matches.astype(BF), slot_grads[step]))
        seq_pos = jnp.concatenate([(part ^ j) * row_count + row_iota for j in range(parts)])
        seq_hot = replacement(seq_pos, step)[2].astype(BF)
        seq_hots.append(jnp.concatenate([seq_hot, jnp.ones_like(seq_hot[:, :2])], axis=1))

    joint_half = jnp.concatenate(
        [
            lax.dynamic_slice_in_dim(
                jnp.concatenate([w_query, w_key, w_value], axis=1), core * half_rows, half_rows, 0
            ),
            jnp.pad(
                jnp.concatenate([b_query, jnp.zeros_like(b_query), b_value])[None, :],
                ((0, PAD - 1), (0, 0)),
            ),
        ],
        axis=0,
    )
    spread = [
        [(groups * p + i, p + parts * ((i + k) % groups)) for p in range(parts) for i in range(groups)]
        for k in range(groups)
    ]
    piece = jnp.concatenate(
        [
            lax.dynamic_slice_in_dim(w_up.T, core * ff_half, ff_half, 0),
            jnp.pad(
                lax.dynamic_slice_in_dim(b_up, core * ff_half, ff_half, 0)[None, :],
                ((0, PAD - 1), (0, width - ff_half)),
            ),
            lax.dynamic_slice_in_dim(w_down, core * ff_half, ff_half, 0),
        ],
        axis=0,
    )

    w_mine = [lax.ppermute(joint_half, "tensor", spread[k]) for k in range(groups)]
    ones = [swap(placed[0], "tensor", 1)]
    twos = [swap(placed[0], "tensor", 2)]
    ones, twos, w_mine, placed, piece, cots, w_out, hots, seq_hots, replaced_list = fence(
        ones, twos, w_mine, placed, piece, cots, w_out, hots, seq_hots, replaced_list
    )
    w_out_half = lax.all_gather(
        lax.dynamic_slice_in_dim(w_out, core * out_half, out_half, 0), "tensor", axis=0
    )
    w_other = [swap(w, "dp", 1) for w in w_mine]
    w_seq, b_seq = assemble(
        jnp.stack([core] + [(group - i) % groups for i in range(groups)]).astype(jnp.int32),
        w_mine,
        w_other,
        local_width,
    )

    joints, x_mine, x_other, heads, log_sums, own_heads = [], [], [], [], [], []
    near = [piece[:cut], piece[cut:]]
    arrived = []
    at_core = core[None].astype(jnp.int32)
    for step in micros:
        threes = (swap(ones[step][:half_count], "tensor", 2), swap(twos[step][half_count:], "tensor", 1))
        rows = [placed[step], ones[step], twos[step], *threes]
        if step + 1 < micro_count:
            ones.append(swap(placed[step + 1], "tensor", 1))
            twos.append(swap(placed[step + 1], "tensor", 2))
        moved = (forward(near[step]), backward(near[step]))
        joint, mine, other = project(at_core, rows, w_seq, b_seq)
        pieces, whole, sums = attn_forward(joint, parts)
        joints.append(joint)
        log_sums.append(sums)
        own_heads.append(whole)
        x_mine.append(mine)
        x_other.append(other)
        ones, twos, moved, pieces, near = fence(ones, twos, moved, pieces, near)
        arrived.append(moved)
        heads.append([pieces[0]] + [swap(pieces[j], "tensor", j) for j in range(1, parts)])
    fw, bw = (jnp.concatenate([arrived[0][d], arrived[1][d]], axis=0) for d in range(2))
    heads, fw, bw, w_out_half = fence(heads, fw, bw, w_out_half)
    w_out_other = swap(w_out_half, "dp", 1)
    blocks = [piece, swap(piece, "dp", 1), fw, bw, swap(fw, "dp", 1), swap(bw, "dp", 1)]

    vectors_one = jnp.stack([b_out, ln1_gain, ln1_bias, b_down] + [b_out] * 4).astype(F32)
    heads_out, norm_one, scale_one, pre_two, first_low, w_out_all = attend(
        jnp.concatenate([part_order, at_core]), heads, placed, w_out_half, w_out_other, vectors_one
    )

    step_blocks = [blocks[:2], blocks[2:6]]
    hidden_low, slopes = [None] * (far + 1), [None] * (far + 1)
    for s in range(2, far + 1):
        if s < far:
            moved = [forward(fw), backward(bw)]
        else:
            moved = [forward(fw[:cut]), backward(bw[cut:])]
        for t in (0, 1) if s == 2 else (s - 1,):
            pre_two, hidden_low[t], slopes[t] = ff_forward(first_low, pre_two, step_blocks[t], ff_half)
        moved, pre_two = fence(moved, pre_two)
        if s == far:
            moved = [jnp.concatenate(moved, axis=0)]
        else:
            fw, bw = moved
        step_blocks.append(moved + [swap(block, "dp", 1) for block in moved])
    pre_two, hidden_low[far], slopes[far] = ff_forward(first_low, pre_two, step_blocks[far], ff_half)

    vectors_two = jnp.stack([ln2_gain, ln2_bias] + [ln2_bias] * 6).astype(F32)
    layer_out, d_pre_two, d_fed, sums_two = second_norm(pre_two, jnp.concatenate(cots, axis=0), vectors_two)
    total = 2 * ff_half

    def ff_blocks(offsets_, other, adds=None, cuts=(), megabytes=24):
        s = abs(offsets_[0])
        result = ff_grad(
            d_uppers[s], hidden_low[s], first_low, d_fed, other, adds or [[] for _ in offsets_], ff_half, cuts,
            bool(other), megabytes,
        )
        return result[0] if other else result

    def both(s):
        return [-s, s] if s else [0]

    def summed(s, others, megabytes=24):
        return ff_blocks(both(s), 0, [[(0, total, others, i)] for i in range(len(both(s)))], (), megabytes)

    d_uppers = [None] * (far + 1)
    rel_b_up = jnp.zeros((2 * count, ff_half), F32)

    def back(s, d_first):
        nonlocal rel_b_up
        base = 4 * s - 2 if s else 0
        d_uppers[s], d_first, rel_b_up = ff_backward(
            d_fed, d_first, slopes[s], step_blocks[s], rel_b_up, base, ff_half
        )
        return d_first

    d_first = back(far, d_pre_two)
    others = ff_blocks([far], 1)
    others, d_uppers[far], d_first = fence(others, d_uppers[far], d_first)
    others = swap(others, "dp", 1)
    d_first = back(far - 1, d_first)
    others, d_uppers[far], d_first = fence(others, d_uppers[far], d_first)
    parcel = ff_blocks([far], 0, [[(0, total, others, 0)]], (ff_half,))
    next_others = ff_blocks(both(far - 1), 1)
    parcel, next_others, d_uppers[far - 1], d_first = fence(parcel, next_others, d_uppers[far - 1], d_first)
    moved = [forward(parcel[0]), backward(parcel[1])]
    others = swap(next_others, "dp", 1)
    for s in range(far - 2, far // 2 - 1, -1):
        d_first = back(s, d_first)
    others, d_uppers[far - 1], d_first = fence(others, d_uppers[far - 1], d_first)
    share = summed(far - 1, others)
    next_others = ff_blocks(both(far - 2), 1)
    moved, share, next_others, d_first = fence(moved, share, next_others, d_first)
    parcel = combine([(0, share[0]), (ff_half, moved[1])], [(0, share[1]), (0, moved[0])])
    parcel, next_others, d_first = fence(parcel, next_others, d_first)
    moved = [forward(parcel[1]), backward(parcel[0])]
    others = swap(next_others, "dp", 1)
    for s in range(far // 2 - 1, -1, -1):
        d_first = back(s, d_first)
    d_pre_one, d_attended, sums_one, *d_heads = attend_back(
        part_order, d_first, norm_one, scale_one, vectors_one, w_out_all, parts
    )
    others, d_uppers[far - 2], d_heads = fence(others, d_uppers[far - 2], d_heads)
    seq_grads = [d_heads[0]] + [swap(d_heads[j], "tensor", j) for j in range(1, parts)]
    share = summed(far - 2, others)
    next_others = ff_blocks(both(far - 3), 1)

    d_out = over_rows(heads_out, d_attended).astype(BF).reshape(count, 2, out_half, width)
    out_other = lax.dynamic_index_in_dim(d_out, 1 - core, 1, keepdims=False).reshape(-1, width)
    out_mine = lax.dynamic_index_in_dim(d_out, core, 1, keepdims=False).reshape(-1, width)
    moved, share, seq_grads, next_others, out_other = fence(moved, share, seq_grads, next_others, out_other)
    seq_grads = jnp.concatenate(seq_grads, axis=0)

    d_joints = [jnp.zeros((), BF) for _ in micros]
    work = [(m, g) for m in micros for g in range(pairs)]

    def over_dp(values, bit=2):
        while bit < dp_count:
            values = (values.astype(F32) + swap(values, "dp", bit).astype(F32)).astype(BF)
            bit *= 2
        return values

    def diagonal(step):
        to_two, to_one = diagonal_share(d_joints[step], w_seq, parts)
        return (swap(to_two, "tensor", 2), swap(to_one, "tensor", 1))

    def side_parcels(step, arrived):
        return side_shares(d_joints[step], w_seq, *arrived, parts)

    def sides(parcels):
        return (swap(parcels[0], "tensor", 1), swap(parcels[1], "tensor", 2))

    def own_table(d_rows):
        return lax.dot_general(
            jnp.concatenate(hots, axis=0),
            d_rows,
            ROWS_DIMS,
            precision=lax.Precision.HIGHEST,
            preferred_element_type=F32,
        )

    partial, stage = [() for _ in micros], [0 for _ in micros]
    d_w = []
    table = own_table(d_pre_one)
    plan = [work[:pairs], work[pairs:-1], work[-1:]]
    for index in range(max(far - 1, len(plan))):
        s = far - 2 - index
        if s > 0:
            parcel = combine([(0, share[0]), (0, moved[1])], [(0, share[1]), (0, moved[0])])
            joints, d_joints, d_fed, parcel, next_others = fence(joints, d_joints, d_fed, parcel, next_others)
            moved = [forward(parcel[1]), backward(parcel[0])]
            others = swap(next_others, "dp", 1)
        elif s == 0:
            parcel = combine([(0, share[0]), (0, moved[0]), (0, moved[1])])[0]
            ff_up, ff_down = parcel[:ff_half], parcel[ff_half:]
            joints, d_joints, ff_up, ff_down = fence(joints, d_joints, ff_up, ff_down)
            ff_up = over_dp(ff_up)
        if index == 0:
            out_mine = (out_mine.astype(F32) + swap(out_other, "dp", 1).astype(F32)).astype(BF)
            out_mine = out_mine.reshape(count, 2, out_half // 2, width)
            out_other = lax.dynamic_index_in_dim(out_mine, 1 - row_part, 1, keepdims=False).reshape(-1, width)
            out_mine = lax.dynamic_index_in_dim(out_mine, row_part, 1, keepdims=False).reshape(-1, width)
            out_mine = (out_mine.astype(F32) + swap(out_other, "dp", 2).astype(F32)).astype(BF)
        elif index == 1:
            out_sum = lax.psum_scatter(out_mine, "tensor", scatter_dimension=0, tiled=True)
        for m in micros:
            ready = max(i for i, pairs_ in enumerate(plan) if (m, pairs - 1) in pairs_) + 1
            if index == ready:
                partial[m], stage[m] = diagonal(m), 1
            elif index == ready + 1:
                partial[m], stage[m] = sides(side_parcels(m, partial[m])), 2
        if index == len(plan) - 1:
            d_w = [(over_rows(x_other[m], d_joints[m]), over_rows(x_mine[m], d_joints[m])) for m in micros[:-1]]
        next_others = ()
        if s > 1:
            next_others = ff_blocks(both(s - 2), 1)
        for m, g in plan[index] if index < len(plan) else ():
            d_joints[m] = attn_backward(
                joints[m], log_sums[m], seq_grads, own_heads[m], parts, m, micro_count, g, (d_joints[m],) if g else ()
            )
        if s > 0:
            share = summed(s - 1, others)
            moved, share, next_others, d_joints, partial, table, d_w, out_mine = fence(
                moved, share, next_others, d_joints, partial, table, d_w, out_mine
            )
        elif s == 0:
            ff_up, d_joints, partial, table, d_w = fence(ff_up, d_joints, partial, table, d_w)

    last = micro_count - 1
    d_w.append((over_rows(x_other[last], d_joints[last]), None))
    other_half = sum(other for other, _ in d_w).astype(BF)
    other_half, d_joints, partial, ff_up, ff_down = fence(other_half, d_joints, partial, ff_up, ff_down)
    other_half = swap(other_half, "dp", 1)
    for m in micros:
        if stage[m] == 0:
            partial[m] = diagonal(m)
        elif stage[m] == 1:
            partial[m] = sides(side_parcels(m, partial[m]))

    def over_bits(values, axis, low, high):
        while low < high:
            bits = (low, 2 * low, 3 * low) if 2 * low < high else (low,)
            sent = values.astype(BF)
            terms = [sent.astype(F32)] + [swap(sent, axis, bit).astype(F32) for bit in bits]
            while len(terms) > 1:
                terms = [a + b for a, b in zip(terms[::2], terms[1::2])]
            values = terms[0]
            low *= 4
        return values

    row_offset, row_other = [0, 0], [0, 1]
    for s in range(1, far):
        row_offset += [-s % count, s, -s % count, s]
        row_other += [0, 0, 1, 1]
    row_offset, row_other = jnp.array(row_offset + [far, far]), jnp.array(row_other + [0, 1])
    place = jnp.repeat(jnp.array([order.index(i) for i in range(count)]), 2)
    half_of = jnp.tile(jnp.arange(2), count)
    chosen = (((place - ring_pos) % count)[:, None] == row_offset[None, :]) & (
        (half_of != core)[:, None] == (row_other[None, :] == 1)
    )
    all_b_up = jnp.dot(
        chosen.astype(F32), rel_b_up, precision=lax.Precision.HIGHEST, preferred_element_type=F32
    )
    all_b_up = jnp.pad(all_b_up, ((0, 0), (0, width - ff_half)))
    hot_sum = sum(over_rows(seq_hots[m], d_joints[m]) for m in micros)
    d_b_seq = hot_sum[vocab_count]
    rest, thirds = hot_sum, []
    for _ in range(3):
        thirds.append(rest.astype(BF))
        rest = rest - thirds[-1].astype(F32)
    table_rows = hot_sum.shape[0]
    shares = against(jnp.concatenate(thirds, axis=0), w_seq).reshape(3, table_rows, width)
    table = jnp.pad(table, ((0, table_rows - vocab_count), (0, 0))) + ((shares[2] + shares[1]) + shares[0])
    empty = jnp.zeros((width,), F32)
    d_b_query, d_b_value = (
        lax.dynamic_update_slice_in_dim(
            empty,
            jnp.concatenate([d_b_seq[(3 * g + a) * PAIR : (3 * g + a + 1) * PAIR] for g in range(pairs)]),
            part * part_width,
            0,
        )
        for a in (0, 2)
    )
    place_row = lax.broadcasted_iota(jnp.int32, table.shape, 0)
    table = jnp.where(place_row == vocab_count, d_b_query[None], table)
    table = jnp.where(place_row == vocab_count + 1, d_b_value[None], table)
    small = jnp.concatenate([table, sums_one, sums_two, all_b_up], axis=0)

    my_half = sum(mine for _, mine in d_w[: len(d_w)] if mine is not None)
    my_half = my_half + sum(over_rows(x_mine[m], d_joints[m]) for m in micros if d_w[m][1] is None)
    my_half = (my_half + other_half.astype(F32)).astype(BF)
    my_half, small, ff_up, ff_down, partial = fence(my_half, small, ff_up, ff_down, partial)

    if local_width != PAIR:
        columns = [
            jnp.concatenate(
                [my_half[:, (3 * g + a) * PAIR : (3 * g + a + 1) * PAIR] for g in range(pairs)], axis=1
            )
            for a in range(3)
        ]
        my_half = jnp.concatenate(
            [c[:, i * local_width : (i + 1) * local_width] for i in range(groups) for c in columns], axis=1
        )
    joint_sum = sum(
        lax.ppermute(
            lax.dynamic_slice_in_dim(
                my_half, (group - k) % groups * 3 * local_width, 3 * local_width, 1
            ),
            "tensor",
            [(b, a) for a, b in spread[k]],
        ).astype(F32)
        for k in range(groups)
    ).astype(BF)
    small = over_bits(small, "dp", 1, dp_count)
    ff_down = over_dp(ff_down)
    ff_up = turned(ff_up)
    up_other = swap(ff_up, "dp", 1)
    if stage[last] == 0:
        partial[last] = side_parcels(last, partial[last])
    grad_rows = row_grad(d_pre_one, w_seq, d_joints, partial[:last], parts)
    joint_sum, small, ff_up, ff_down, up_other, out_sum, partial[last], grad_rows = fence(
        joint_sum, small, ff_up, ff_down, up_other, out_sum, partial[last], grad_rows
    )

    joint_sum = over_dp(joint_sum)
    out_sum = over_dp(out_sum, 4)
    out_sum = by_core(out_sum, swap(out_sum, "dp", 2), 0, row_part == 0)
    down_other = swap(ff_down, "dp", 1)
    if stage[last] == 0:
        partial[last] = sides(partial[last])
    small = over_bits(small, "tensor", 1, min(4, count))
    grad_w_up = by_core(ff_up, up_other, 1).astype(F32)
    grad_w_down = by_core(ff_down, down_other).astype(F32)
    joint_sum, partial[last], out_sum, grad_w_up, grad_w_down = fence(
        joint_sum, partial[last], out_sum, grad_w_up, grad_w_down
    )
    out_other = swap(out_sum, "dp", 1)
    grad_w_out = by_core(out_sum, out_other).astype(F32)
    joint_other = swap(joint_sum, "dp", 1)
    small = over_bits(small, "tensor", 4, count)
    late = jnp.concatenate([partial[last][0], partial[last][1]], axis=1).astype(F32)
    late = late[:, :width] + late[:, width:]
    late = jnp.concatenate([jnp.zeros((row_count * last, width), F32), late], axis=0)
    grad_rows = jnp.where(jnp.concatenate(replaced_list)[:, None], 0.0, grad_rows + late)
    grad_query, grad_key, grad_value = (
        by_core(joint_sum[:, at : at + local_width], joint_other[:, at : at + local_width]).astype(F32)
        for at in (0, local_width, 2 * local_width)
    )
    grad_b_query, grad_b_value = (
        lax.dynamic_slice_in_dim(small[vocab_count + i], rank * local_width, local_width, 0) for i in range(2)
    )
    sums_at = (table_rows, table_rows + 8)
    grad_b_out, grad_gone, grad_bone, grad_b_down, grad_gtwo, grad_btwo = (
        small[at + i] for at in sums_at for i in range(3)
    )
    grad_b_up = lax.dynamic_slice_in_dim(small, table_rows + 16 + 2 * rank, 2, 0)[:, :ff_half].reshape(-1)

    return (
        layer_out.reshape(micro_count, row_count, width),
        grad_rows.reshape(micro_count, row_count, width),
        small[:vocab_count],
        grad_query,
        grad_b_query,
        grad_key,
        grad_value,
        grad_b_value,
        grad_w_out,
        grad_b_out,
        grad_gone,
        grad_bone,
        grad_w_up,
        grad_b_up,
        grad_w_down,
        grad_b_down,
        grad_gtwo,
        grad_btwo,
    )


def solution(mesh):
    return jax.shard_map(
        shards,
        mesh=mesh,
        in_specs=(
            P(None, ("dp", "tensor"), None),
            P(),
            P(None, "dp", None),
            P(None, "dp", None),
            P(None, "tensor"),
            P("tensor"),
            P(None, "tensor"),
            P(None, "tensor"),
            P("tensor"),
            P("tensor", None),
            P(),
            P(),
            P(),
            P(None, "tensor"),
            P("tensor"),
            P("tensor", None),
            P(),
            P(),
            P(),
            P(None, "dp", None, None),
        ),
        out_specs=(
            P(None, ("dp", "tensor"), None),
            P(None, ("dp", "tensor"), None),
            P(),
            P(None, "tensor"),
            P("tensor"),
            P(None, "tensor"),
            P(None, "tensor"),
            P("tensor"),
            P("tensor", None),
            P(),
            P(),
            P(),
            P(None, "tensor"),
            P("tensor"),
            P("tensor", None),
            P(),
            P(),
            P(),
        ),
        check_vma=False,
    )
```
